32 devices in a mesh: row: 8 (over y, x, core), col: 4 (over z).
Axes of the slice: x: 2, y: 2, z: 4, core: 2. Of those that a mesh axis runs over, the one named last changes fastest.
Arguments:
- images: float32 [32, 197, 768], P(('row', 'col')), may hold values from -6 to 6
- cotangent: float32 [32, 197, 768], P(('row', 'col')), may hold values from -6 to 6
- counts: int32 [8], replicated, may hold values from 1 to 4, as said below
- w_qkv: float32 [2, 768, 2304], P(None, 'row', 'col'), may hold values from -2 to 2
- w_out: float32 [2, 768, 768], P(None, 'col', 'row'), may hold values from -1.5 to 1.5
- w_up: float32 [2, 768, 3072], P(None, 'row', 'col'), may hold values from -0.21875 to 0.21875
- w_down: float32 [2, 3072, 768], P(None, 'col', 'row'), may hold values from -0.109375 to 0.109375
- norm_gains: float32 [2, 2, 768], replicated, may hold values from 0.5 to 1.5
- res_biases: float32 [2, 2, 768], replicated, may hold values from -1.5 to 1.5
- b_up: float32 [2, 3072], replicated, may hold values from -1.5 to 1.5
- m_qkv: float32 [2, 768, 2304], P(None, 'row', 'col'), may hold values from -60 to 60
- m_out: float32 [2, 768, 768], P(None, 'col', 'row'), may hold values from -60 to 60
- m_up: float32 [2, 768, 3072], P(None, 'row', 'col'), may hold values from -60 to 60
- m_down: float32 [2, 3072, 768], P(None, 'col', 'row'), may hold values from -60 to 60
- m_gains: float32 [2, 2, 768], replicated, may hold values from -60 to 60
- m_biases: float32 [2, 2, 768], replicated, may hold values from -60 to 60
- m_bup: float32 [2, 3072], replicated, may hold values from -60 to 60
- v_qkv: float32 [2, 768, 2304], P(None, 'row', 'col'), may hold values from 0.5 to 20
- v_out: float32 [2, 768, 768], P(None, 'col', 'row'), may hold values from 0.5 to 20
- v_up: float32 [2, 768, 3072], P(None, 'row', 'col'), may hold values from 0.5 to 20
- v_down: float32 [2, 3072, 768], P(None, 'col', 'row'), may hold values from 0.5 to 20
- v_gains: float32 [2, 2, 768], replicated, may hold values from 0.5 to 20
- v_biases: float32 [2, 2, 768], replicated, may hold values from 0.5 to 20
- v_bup: float32 [2, 3072], replicated, may hold values from 0.5 to 20
Outputs:
- layer_out: float32 [32, 197, 768], P(('row', 'col'))
- grad_images: float32 [32, 197, 768], P(('row', 'col'))
- grad_qkv: float32 [2, 768, 2304], P(None, 'row', 'col')
- grad_out: float32 [2, 768, 768], P(None, 'col', 'row')
- grad_up: float32 [2, 768, 3072], P(None, 'row', 'col')
- grad_down: float32 [2, 3072, 768], P(None, 'col', 'row')
- grad_gains: float32 [2, 2, 768], replicated
- grad_biases: float32 [2, 2, 768], replicated
- grad_bup: float32 [2, 3072], replicated
- new_qkv: float32 [2, 768, 2304], P(None, 'row', 'col')
- new_out: float32 [2, 768, 768], P(None, 'col', 'row')
- new_up: float32 [2, 768, 3072], P(None, 'row', 'col')
- new_down: float32 [2, 3072, 768], P(None, 'col', 'row')
- fresh_m_qkv: float32 [2, 768, 2304], P(None, 'row', 'col')
- fresh_m_out: float32 [2, 768, 768], P(None, 'col', 'row')
- fresh_m_up: float32 [2, 768, 3072], P(None, 'row', 'col')
- fresh_m_down: float32 [2, 3072, 768], P(None, 'col', 'row')
- fresh_m_gains: float32 [2, 2, 768], replicated
- fresh_m_biases: float32 [2, 2, 768], replicated
- fresh_m_bup: float32 [2, 3072], replicated
- fresh_v_qkv: float32 [2, 768, 2304], P(None, 'row', 'col')
- fresh_v_out: float32 [2, 768, 768], P(None, 'col', 'row')
- fresh_v_up: float32 [2, 768, 3072], P(None, 'row', 'col')
- fresh_v_down: float32 [2, 3072, 768], P(None, 'col', 'row')
- fresh_v_gains: float32 [2, 2, 768], replicated
- fresh_v_biases: float32 [2, 2, 768], replicated
- fresh_v_bup: float32 [2, 3072], replicated
The draws below stay inside these ranges and needn't reach their ends.
Inputs may be any that keep to these rules, and one draw needn't show every extreme that they name: Row group g holds counts[g] real images, in slots g * 4 to g * 4 + counts[g] - 1; its other slots are padding. Some group is full in every draw.
All inputs are finite; a program needn't handle non-finite values.
Results may differ from the reference program's by a relative error of at most 0.023.
Values may be sent and summed in bfloat16 or wider, within the bound.
No kernel may reach another device: no remote copies, remote signals or barrier semaphores. Data moves between devices by JAX's collectives and lax.ppermute only.
A program may use at most 192 MiB of HBM per device.

```python
import math
import jax
import jax.numpy as jnp
from jax import lax

D = 768
HEADS = 12
HD = 64
FF = 3072
SEQ = 197
LAYERS = 2
STEP = 3
GROUPS = 8
SLOTS = 4
IMAGES = 32
N_ROW = 8
N_COL = 4


def draw_counts(key, part):
    drawn = jax.random.randint(key, (GROUPS,), 1, SLOTS + 1, dtype=jnp.int32)
    chosen = jax.random.randint(jax.random.fold_in(key, 7), (), 0, GROUPS, dtype=jnp.int32)
    return jnp.where(jnp.arange(GROUPS, dtype=jnp.int32) == chosen, SLOTS, drawn).astype(jnp.int32)


def draw_w_qkv(key, part):
    normal_part = jnp.clip(jax.random.normal(key, (LAYERS, D, 3 * D), jnp.float32), -4.0, 4.0)
    base = normal_part * D ** (-0.5)
    return jnp.clip(base, -2.0, 2.0)


def level_of(own_key, extent, cuts, low, largest):
    def one(position, parts):
        heights = jax.random.uniform(jax.random.fold_in(jax.random.fold_in(own_key, 6), position), (parts,), jnp.float32, low / len(cuts), largest / len(cuts))
        return jnp.repeat(jnp.exp(heights), extent[position] // parts).reshape((-1,) + (1,) * (len(extent) - position - 1))

    level = one(*cuts[0])
    for cut in cuts[1:]:
        level = level * one(*cut)
    return level


def gaussian(key, extent, width, most, split=(), kind=jnp.bfloat16):
    entries = jax.random.normal(key, extent, jnp.float32) * width
    if len(split) > 0:
        entries = level_of(key, extent, split, -0.22, 0.18) * entries
    return jnp.clip(entries, min=-most, max=most).astype(kind)


def setup_inputs(seed: int = 0) -> dict:
    seeds = jax.random.split(jax.random.key(seed), 25)
    images = gaussian(seeds[0], (IMAGES, SEQ, D), 1.0, 6.0, ((0, 32),), jnp.float32)
    cotangent = gaussian(seeds[1], (IMAGES, SEQ, D), 1.0, 6.0, ((0, 32),), jnp.float32)
    counts = draw_counts(jax.random.fold_in(seeds[24], 71), 0)
    w_qkv = draw_w_qkv(jax.random.fold_in(seeds[24], 71), 0)
    w_out = gaussian(seeds[4], (LAYERS, D, D), (max(4 * D // SEQ, 1)) ** -0.5, 1.5, ((1, 4), (2, 8)), jnp.float32)
    w_up = gaussian(seeds[5], (LAYERS, D, FF), D ** -0.5, 0.21875, ((1, 8), (2, 4)), jnp.float32)
    w_down = gaussian(seeds[6], (LAYERS, FF, D), FF ** -0.5, 0.109375, ((1, 4), (2, 8)), jnp.float32)
    norm_gains = jnp.clip(1.0 + 0.1 * jax.random.normal(seeds[7], (LAYERS, 2, D), jnp.float32), 0.5, 1.5)
    res_biases = gaussian(seeds[8], (LAYERS, 2, D), 0.3, 1.5, (), jnp.float32)
    b_up = gaussian(seeds[9], (LAYERS, FF), 0.3, 1.5, (), jnp.float32)
    m_qkv = gaussian(seeds[10], (LAYERS, D, 3 * D), 10.0, 60.0, ((1, 8), (2, 4)), jnp.float32)
    m_out = gaussian(seeds[11], (LAYERS, D, D), 10.0, 60.0, ((1, 4), (2, 8)), jnp.float32)
    m_up = gaussian(seeds[12], (LAYERS, D, FF), 10.0, 60.0, ((1, 8), (2, 4)), jnp.float32)
    m_down = gaussian(seeds[13], (LAYERS, FF, D), 10.0, 60.0, ((1, 4), (2, 8)), jnp.float32)
    m_gains = gaussian(seeds[14], (LAYERS, 2, D), 10.0, 60.0, (), jnp.float32)
    m_biases = gaussian(seeds[15], (LAYERS, 2, D), 10.0, 60.0, (), jnp.float32)
    m_bup = gaussian(seeds[16], (LAYERS, FF), 10.0, 60.0, (), jnp.float32)
    v_qkv = jnp.clip(jnp.exp(math.log(20.0) - 3.6888795 * jax.random.uniform(seeds[17], (LAYERS, D, 3 * D), jnp.float32) ** level_of(seeds[17], (LAYERS, D, 3 * D), ((1, 8), (2, 4)), -0.2, 0.2)), 0.5, 20.0)
    v_out = jnp.clip(jnp.exp(math.log(20.0) - 3.6888795 * jax.random.uniform(seeds[18], (LAYERS, D, D), jnp.float32) ** level_of(seeds[18], (LAYERS, D, D), ((1, 4), (2, 8)), -0.2, 0.2)), 0.5, 20.0)
    v_up = jnp.clip(jnp.exp(math.log(20.0) - 3.6888795 * jax.random.uniform(seeds[19], (LAYERS, D, FF), jnp.float32) ** level_of(seeds[19], (LAYERS, D, FF), ((1, 8), (2, 4)), -0.2, 0.2)), 0.5, 20.0)
    v_down = jnp.clip(jnp.exp(math.log(20.0) - 3.6888795 * jax.random.uniform(seeds[20], (LAYERS, FF, D), jnp.float32) ** level_of(seeds[20], (LAYERS, FF, D), ((1, 4), (2, 8)), -0.2, 0.2)), 0.5, 20.0)
    v_gains = jnp.clip(jnp.exp(jax.random.uniform(seeds[21], (LAYERS, 2, D), jnp.float32, math.log(0.5), math.log(20.0))), 0.5, 20.0)
    v_biases = jnp.clip(jnp.exp(jax.random.uniform(seeds[22], (LAYERS, 2, D), jnp.float32, math.log(0.5), math.log(20.0))), 0.5, 20.0)
    v_bup = jnp.clip(jnp.exp(jax.random.uniform(seeds[23], (LAYERS, FF), jnp.float32, math.log(0.5), math.log(20.0))), 0.5, 20.0)
    return dict(images=images, cotangent=cotangent, counts=counts, w_qkv=w_qkv, w_out=w_out, w_up=w_up, w_down=w_down, norm_gains=norm_gains, res_biases=res_biases, b_up=b_up, m_qkv=m_qkv, m_out=m_out, m_up=m_up, m_down=m_down, m_gains=m_gains, m_biases=m_biases, m_bup=m_bup, v_qkv=v_qkv, v_out=v_out, v_up=v_up, v_down=v_down, v_gains=v_gains, v_biases=v_biases, v_bup=v_bup)


norm_eps = 1e-06
root_half = 0.7071067811865476
inv_root_two_pi = 0.3989422804014327
beta_one = 0.9
beta_two = 0.999
adam_eps = 1e-08
learn_rate = 0.06
decay_rate = 0.05

def normalize(tokens, gain):
    center = lax.optimization_barrier(jnp.mean(tokens, axis=-1, keepdims=True))
    shifted = tokens - center
    inverse = lax.rsqrt(lax.optimization_barrier(jnp.mean(shifted * shifted, axis=-1, keepdims=True)) + norm_eps)
    scaled = shifted * inverse
    return (scaled, inverse, (scaled * gain).astype(jnp.bfloat16))

def norm_back(upstream, scaled, inverse, gain):
    grad_scaled = upstream * gain
    grad_gain = lax.optimization_barrier(jnp.sum(upstream * scaled, axis=0))
    mean_one = lax.optimization_barrier(jnp.mean(grad_scaled, axis=-1, keepdims=True))
    mean_two = lax.optimization_barrier(jnp.mean(grad_scaled * scaled, axis=-1, keepdims=True))
    return (inverse * (grad_scaled - mean_one - scaled * mean_two), grad_gain)

def gelu_value(pre_act):
    return pre_act * 0.5 * (1.0 + lax.erf(pre_act * root_half))

def gelu_slope(pre_act):
    return 0.5 * (1.0 + lax.erf(pre_act * root_half)) + pre_act * inv_root_two_pi * jnp.exp(-0.5 * pre_act * pre_act)

def split_heads(packed):
    query_part = packed[:, :D].reshape(SEQ, HEADS, HD).astype(jnp.float32)
    key_part = packed[:, D:2 * D].reshape(SEQ, HEADS, HD).astype(jnp.float32)
    value_part = packed[:, 2 * D:].reshape(SEQ, HEADS, HD).astype(jnp.float32)
    return (query_part, key_part, value_part)

def attend(packed):
    query_part, key_part, value_part = split_heads(packed)
    scores = jnp.einsum('qhd,khd->hqk', query_part, key_part) * HD ** (-0.5)
    row_peak = lax.optimization_barrier(jnp.max(scores, axis=-1, keepdims=True))
    row_total = lax.optimization_barrier(jnp.sum(jnp.exp(scores - row_peak), axis=-1, keepdims=True))
    logsum = row_peak + jnp.log(row_total)
    attn_probs = jnp.exp(scores - logsum).astype(jnp.bfloat16)
    attn_mixed = jnp.einsum('hqk,khd->qhd', attn_probs.astype(jnp.float32), value_part)
    return (attn_mixed.reshape(SEQ, D).astype(jnp.bfloat16), logsum)

def attend_back(packed, logsum, grad_mixed):
    query_part, key_part, value_part = split_heads(packed)
    scores = jnp.einsum('qhd,khd->hqk', query_part, key_part) * HD ** (-0.5)
    attn_probs = jnp.exp(scores - logsum)
    probs_low = attn_probs.astype(jnp.bfloat16).astype(jnp.float32)
    grad_heads = grad_mixed.reshape(SEQ, HEADS, HD).astype(jnp.float32)
    grad_values = jnp.einsum('hqk,qhd->khd', probs_low, grad_heads)
    grad_probs = jnp.einsum('qhd,khd->hqk', grad_heads, value_part)
    inner_sum = lax.optimization_barrier(jnp.sum(attn_probs * grad_probs, axis=-1, keepdims=True))
    grad_scores = (attn_probs * (grad_probs - inner_sum) * HD ** (-0.5)).astype(jnp.bfloat16).astype(jnp.float32)
    grad_query = jnp.einsum('hqk,khd->qhd', grad_scores, key_part)
    grad_keys = jnp.einsum('hqk,qhd->khd', grad_scores, query_part)
    joined = jnp.concatenate([grad_query.reshape(SEQ, D), grad_keys.reshape(SEQ, D), grad_values.reshape(SEQ, D)], axis=1)
    return joined.astype(jnp.bfloat16)

def forward_block(stack, weights, gain, bias, up_bias):
    query_w, out_w, up_w, down_w = weights
    images_here = stack.shape[0]
    tokens = stack.reshape(images_here * SEQ, D)
    scaled_one, inverse_one, normed_one = normalize(tokens, gain[0])
    packed = jnp.dot(normed_one, query_w, preferred_element_type=jnp.float32).astype(jnp.bfloat16)
    packed_images = packed.reshape(images_here, SEQ, 3 * D)
    attn_mixed, logsum = jax.vmap(attend)(packed_images)
    attn_mixed = attn_mixed.reshape(images_here * SEQ, D)
    middle = tokens + jnp.dot(attn_mixed, out_w, preferred_element_type=jnp.float32) + bias[0]
    scaled_two, inverse_two, normed_two = normalize(middle, gain[1])
    pre_act = jnp.dot(normed_two, up_w, preferred_element_type=jnp.float32) + up_bias
    active = gelu_value(pre_act).astype(jnp.bfloat16)
    output = middle + jnp.dot(active, down_w, preferred_element_type=jnp.float32) + bias[1]
    saved = (scaled_one, inverse_one, normed_one, packed_images, logsum, attn_mixed, scaled_two, inverse_two, normed_two, pre_act, active)
    return (output.reshape(images_here, SEQ, D), saved)

def backward_block(stack, upstream_stack, weights, gain, bias, up_bias):
    query_w, out_w, up_w, down_w = weights
    images_here = stack.shape[0]
    ignored, saved = forward_block(stack, weights, gain, bias, up_bias)
    scaled_one, inverse_one, normed_one, packed_images, logsum, attn_mixed, scaled_two, inverse_two, normed_two, pre_act, active = saved
    upstream = upstream_stack.reshape(images_here * SEQ, D)
    up_low = upstream.astype(jnp.bfloat16)
    grad_down = jnp.dot(active.T, up_low, preferred_element_type=jnp.float32)
    grad_res_two = lax.optimization_barrier(jnp.sum(upstream, axis=0))
    grad_pre = jnp.dot(up_low, down_w.T, preferred_element_type=jnp.float32) * gelu_slope(pre_act)
    pre_low = grad_pre.astype(jnp.bfloat16)
    grad_bup = lax.optimization_barrier(jnp.sum(grad_pre, axis=0))
    grad_up = jnp.dot(normed_two.T, pre_low, preferred_element_type=jnp.float32)
    grad_normed_two = jnp.dot(pre_low, up_w.T, preferred_element_type=jnp.float32)
    grad_middle, gain_two = norm_back(grad_normed_two, scaled_two, inverse_two, gain[1])
    grad_middle = grad_middle + upstream
    grad_res_one = lax.optimization_barrier(jnp.sum(grad_middle, axis=0))
    middle_low = grad_middle.astype(jnp.bfloat16)
    grad_out = jnp.dot(attn_mixed.T, middle_low, preferred_element_type=jnp.float32)
    grad_mixed = jnp.dot(middle_low, out_w.T, preferred_element_type=jnp.float32).astype(jnp.bfloat16)
    grad_packed = jax.vmap(attend_back)(packed_images, logsum, grad_mixed.reshape(images_here, SEQ, D))
    grad_packed = grad_packed.reshape(images_here * SEQ, 3 * D)
    grad_qkv = jnp.dot(normed_one.T, grad_packed, preferred_element_type=jnp.float32)
    grad_normed_one = jnp.dot(grad_packed, query_w.T, preferred_element_type=jnp.float32)
    grad_below, gain_one = norm_back(grad_normed_one, scaled_one, inverse_one, gain[0])
    grad_tokens = grad_middle + grad_below
    grads = (grad_qkv, grad_out, grad_up, grad_down, jnp.stack([gain_one, gain_two]), jnp.stack([grad_res_one, grad_res_two]), grad_bup)
    return (grad_tokens.reshape(images_here, SEQ, D), grads)

def add_trees(one_tree, two_tree):
    return jax.tree.map(jnp.add, one_tree, two_tree)

def adamw_step(param, gradient, first_moment, second_moment):
    fresh_first = beta_one * first_moment + (1.0 - beta_one) * gradient
    fresh_second = beta_two * second_moment + (1.0 - beta_two) * gradient * gradient
    first_hat = fresh_first / (1.0 - beta_one ** STEP)
    second_hat = fresh_second / (1.0 - beta_two ** STEP)
    updated = param - learn_rate * (first_hat / (jnp.sqrt(second_hat) + adam_eps) + decay_rate * param)
    return (updated, fresh_first, fresh_second)

def reference(images, cotangent, counts, w_qkv, w_out, w_up, w_down, norm_gains, res_biases, b_up, m_qkv, m_out, m_up, m_down, m_gains, m_biases, m_bup, v_qkv, v_out, v_up, v_down, v_gains, v_biases, v_bup):
    slot_ids = jnp.arange(N_ROW * N_COL, dtype=jnp.int32)
    live_mask = (slot_ids % N_COL < counts[slot_ids // N_COL]).astype(jnp.float32)[:, None, None]
    layer_inputs = []
    hidden = images
    for level in range(LAYERS):
        weights = (w_qkv[level].astype(jnp.bfloat16), w_out[level].astype(jnp.bfloat16), w_up[level].astype(jnp.bfloat16), w_down[level].astype(jnp.bfloat16))
        layer_inputs.append(hidden)

        def forward_step(carry, stack):
            output, ignored = forward_block(stack, weights, norm_gains[level], res_biases[level], b_up[level])
            return (carry, output)
        unused, produced = lax.scan(forward_step, jnp.zeros((), jnp.float32), hidden.reshape(N_ROW, N_COL, SEQ, D))
        hidden = produced.reshape(N_ROW * N_COL, SEQ, D)
    layer_out = hidden * live_mask
    upstream = cotangent * live_mask
    collected = []
    for level in reversed(range(LAYERS)):
        weights = (w_qkv[level].astype(jnp.bfloat16), w_out[level].astype(jnp.bfloat16), w_up[level].astype(jnp.bfloat16), w_down[level].astype(jnp.bfloat16))

        def backward_step(totals, pair):
            grad_tokens, grads = backward_block(pair[0], pair[1], weights, norm_gains[level], res_biases[level], b_up[level])
            return (add_trees(totals, grads), grad_tokens)
        zeros = (jnp.zeros((D, 3 * D), jnp.float32), jnp.zeros((D, D), jnp.float32), jnp.zeros((D, FF), jnp.float32), jnp.zeros((FF, D), jnp.float32), jnp.zeros((2, D), jnp.float32), jnp.zeros((2, D), jnp.float32), jnp.zeros((FF,), jnp.float32))
        totals, grad_stack = lax.scan(backward_step, zeros, (layer_inputs[level].reshape(N_ROW, N_COL, SEQ, D), upstream.reshape(N_ROW, N_COL, SEQ, D)))
        upstream = grad_stack.reshape(N_ROW * N_COL, SEQ, D)
        collected.insert(0, totals)
    grad_list = [jnp.stack([entry[index] for entry in collected]) for index in range(7)]
    params = [w_qkv, w_out, w_up, w_down, norm_gains, res_biases, b_up]
    firsts = [m_qkv, m_out, m_up, m_down, m_gains, m_biases, m_bup]
    seconds = [v_qkv, v_out, v_up, v_down, v_gains, v_biases, v_bup]
    results = [adamw_step(params[index], grad_list[index], firsts[index], seconds[index]) for index in range(7)]
    return (layer_out, upstream, grad_list[0], grad_list[1], grad_list[2], grad_list[3], grad_list[4], grad_list[5], grad_list[6], results[0][0], results[1][0], results[2][0], results[3][0], results[0][1], results[1][1], results[2][1], results[3][1], results[4][1], results[5][1], results[6][1], results[0][2], results[1][2], results[2][2], results[3][2], results[4][2], results[5][2], results[6][2])
```

```python
import functools

import jax
import jax.numpy as jnp
from jax import lax
from jax.experimental import pallas as pl
from jax.experimental.pallas import tpu as pltpu
from jax.sharding import PartitionSpec as P

HEADS = 12
LAYERS = 2
STEP = 3
D = 768
FF = 3072
HD = 64
BLOCKS = 4
ROWS = 208
QKV_W = 3 * D // BLOCKS
OUT_W = D // BLOCKS
UP_W = FF // BLOCKS
PIECE = 96

norm_eps = 1e-06
root_half = 0.7071067811865476
inv_root_two_pi = 0.3989422804014327
beta_one = 0.9
beta_two = 0.999
adam_eps = 1e-08
learn_rate = 0.06
decay_rate = 0.05

BF = jnp.bfloat16
F32 = jnp.float32


def dot_nn(a, b):
    return lax.dot_general(a, b, (((1,), (0,)), ((), ())), preferred_element_type=F32)


def dot_nt(a, b):
    return lax.dot_general(a, b, (((1,), (1,)), ((), ())), preferred_element_type=F32)


def dot_tn(a, b):
    return lax.dot_general(a, b, (((0,), (0,)), ((), ())), preferred_element_type=F32)


def scaled_rows(x):
    center = jnp.mean(x, axis=-1, keepdims=True)
    shifted = x - center
    inverse = lax.rsqrt(jnp.mean(shifted * shifted, axis=-1, keepdims=True) + norm_eps)
    return shifted * inverse, inverse


def norm_back(upstream, scaled, inverse, gain):
    grad_scaled = upstream * gain
    mean_one = jnp.mean(grad_scaled, axis=-1, keepdims=True)
    mean_two = jnp.mean(grad_scaled * scaled, axis=-1, keepdims=True)
    grad_gain = jnp.sum(upstream * scaled, axis=0, keepdims=True)
    return inverse * (grad_scaled - mean_one - scaled * mean_two), grad_gain


def block_of(turn, s):
    return lax.rem(turn - s + 2 * BLOCKS, BLOCKS)


def attend_kernel(seq, turn_ref, x_ref, gain_ref, bias_ref, w_ref, qkv_ref, lse_ref, oext_ref, h1_ref, a2_ref, blk):
    turn = turn_ref[0]
    x = x_ref[...]
    scaled, _ = scaled_rows(x)
    a1 = (scaled * gain_ref[0:1, :]).astype(BF)
    for s in range(BLOCKS):
        t = dot_nn(a1, w_ref[s, :, 0:640])
        blk[block_of(turn, s)] = t.astype(BF)
    for b in range(BLOCKS):
        qkv_ref[:, b * QKV_W : (b + 1) * QKV_W] = blk[b, :, 0:QKV_W]
    low_half = lax.broadcasted_iota(jnp.int32, (ROWS, 128), 1) < HD
    key_live = lax.broadcasted_iota(jnp.int32, (ROWS, ROWS), 0) < seq
    scale = HD ** (-0.5)
    oext_ref[:, :, 0:HD] = jnp.zeros((BLOCKS, ROWS, HD), BF)
    for pair in range(HEADS // 2):
        q2 = qkv_ref[:, pair * 128 : (pair + 1) * 128]
        k2 = qkv_ref[:, D + pair * 128 : D + (pair + 1) * 128]
        v2 = qkv_ref[:, 2 * D + pair * 128 : 2 * D + (pair + 1) * 128]
        mixed = []
        for half in range(2):
            live = low_half if half == 0 else jnp.logical_not(low_half)
            qm = jnp.where(live, q2, jnp.zeros_like(q2))
            st = jnp.where(key_live, dot_nt(k2, qm) * scale, -1e30)
            peak = jnp.max(st, axis=0, keepdims=True)
            grown = jnp.exp(st - peak)
            total = jnp.sum(grown, axis=0, keepdims=True)
            head = 2 * pair + half
            lse_ref[head : head + 1, :] = peak + jnp.log(total)
            probs = (grown * (1.0 / total)).astype(BF)
            mixed.append(dot_tn(probs, v2))
        both = jnp.where(low_half, mixed[0], mixed[1]).astype(BF)
        for half in range(2):
            head = 2 * pair + half
            lane = HD + (head % 3) * HD
            oext_ref[head // 3, :, lane : lane + HD] = both[:, half * HD : (half + 1) * HD]
    total = x + bias_ref[0:1, :]
    for s in range(BLOCKS):
        total = total + dot_nt(oext_ref[block_of(turn, s)], w_ref[s, :, 512:768])
    h1_ref[...] = total
    scaled2, _ = scaled_rows(total)
    a2_ref[...] = (scaled2 * gain_ref[1:2, :]).astype(BF)


def feed_kernel(h1_ref, a2_ref, bias_ref, bup_ref, w_ref, z_ref, slope_ref, y_ref):
    s = pl.program_id(0)

    @pl.when(s == 0)
    def _():
        y_ref[...] = h1_ref[...] + bias_ref[1:2, :]

    u = dot_nn(a2_ref[...], w_ref[0, :, 0:UP_W]) + bup_ref[0]
    bell = 0.5 * (1.0 + lax.erf(u * root_half))
    z = (u * bell).astype(BF)
    z_ref[0] = z
    slope_ref[0] = bell + u * inv_root_two_pi * jnp.exp(-0.5 * u * u)
    y_ref[...] += dot_nt(z, w_ref[0, :, UP_W : 2 * UP_W])


def put_grad(near_ref, far_ref, value):
    for m in range(4):
        near_ref[m, 0] = value[m * PIECE : (m + 1) * PIECE]
        far_ref[m, 0] = value[(4 + m) * PIECE : (5 + m) * PIECE]


def feed_back_kernel(
    g_ref, h1_ref, a2_ref, gain_ref, z_ref, slope_ref, w_ref,
    upn_ref, upf_ref, dnn_ref, dnf_ref, bup_ref, dh1_ref, sums_ref, da2, gb_t, a2_t,
):
    s = pl.program_id(0)

    @pl.when(s == 0)
    def _():
        da2[...] = jnp.zeros_like(da2)
        gb_t[...] = g_ref[...].T.astype(BF)
        a2_t[...] = a2_ref[...].T

    gb = g_ref[...].astype(BF)
    put_grad(dnn_ref, dnf_ref, dot_nn(gb_t[...], z_ref[0]).astype(BF))
    du = dot_nn(gb, w_ref[0, :, UP_W : 2 * UP_W]) * slope_ref[0]
    bup_ref[0] = jnp.sum(du, axis=0, keepdims=True)
    dub = du.astype(BF)
    put_grad(upn_ref, upf_ref, dot_nn(a2_t[...], dub).astype(BF))
    da2[...] += dot_nt(dub, w_ref[0, :, 0:UP_W])

    @pl.when(s == BLOCKS - 1)
    def _():
        g = g_ref[...]
        scaled, inverse = scaled_rows(h1_ref[...])
        below, grad_gain = norm_back(da2[...], scaled, inverse, gain_ref[1:2, :])
        dh1 = below + g
        dh1_ref[...] = dh1
        sums_ref[0:1, :] = grad_gain
        sums_ref[1:2, :] = jnp.sum(g, axis=0, keepdims=True)
        sums_ref[2:3, :] = jnp.sum(dh1, axis=0, keepdims=True)


def attend_back_kernel(
    seq, turn_ref, dh1_ref, x_ref, gain_ref, qkv_ref, lse_ref, oext_ref, w_ref,
    near_ref, far_ref, below_ref, sums_ref, dext, dmix, dqkv, dqx,
):
    turn = turn_ref[0]
    dh1 = dh1_ref[...]
    hb = dh1.astype(BF)
    hb_t = dh1.T.astype(BF)
    for s in range(BLOCKS):
        dext[block_of(turn, s)] = dot_nn(hb, w_ref[s, :, 512:768]).astype(BF)
    for b in range(BLOCKS):
        dmix[:, b * OUT_W : (b + 1) * OUT_W] = dext[b, :, HD : HD + OUT_W]
    low_half = lax.broadcasted_iota(jnp.int32, (ROWS, 128), 1) < HD
    key_live = lax.broadcasted_iota(jnp.int32, (ROWS, ROWS), 0) < seq
    scale = HD ** (-0.5)
    for pair in range(HEADS // 2):
        q2 = qkv_ref[:, pair * 128 : (pair + 1) * 128]
        k2 = qkv_ref[:, D + pair * 128 : D + (pair + 1) * 128]
        v2 = qkv_ref[:, 2 * D + pair * 128 : 2 * D + (pair + 1) * 128]
        d2 = dmix[:, pair * 128 : (pair + 1) * 128]
        dq = jnp.zeros((ROWS, 128), F32)
        dk = jnp.zeros((ROWS, 128), F32)
        dv = jnp.zeros((ROWS, 128), F32)
        for half in range(2):
            head = 2 * pair + half
            live = low_half if half == 0 else jnp.logical_not(low_half)
            none = jnp.zeros_like(q2)
            qm = jnp.where(live, q2, none)
            km = jnp.where(live, k2, none)
            dm = jnp.where(live, d2, none)
            st = jnp.where(key_live, dot_nt(k2, qm) * scale, -1e30)
            probs = jnp.exp(st - lse_ref[head : head + 1, :])
            dprobs = dot_nt(v2, dm)
            inner = jnp.sum(probs * dprobs, axis=0, keepdims=True)
            dst = (probs * (dprobs - inner) * scale).astype(BF)
            dv = dv + dot_nn(probs.astype(BF), dm)
            dk = dk + dot_nn(dst, qm)
            dq = dq + dot_tn(dst, km)
        dqkv[:, pair * 128 : (pair + 1) * 128] = dq.astype(BF)
        dqkv[:, D + pair * 128 : D + (pair + 1) * 128] = dk.astype(BF)
        dqkv[:, 2 * D + pair * 128 : 2 * D + (pair + 1) * 128] = dv.astype(BF)
    for b in range(BLOCKS):
        dqx[b, :, 0:QKV_W] = dqkv[:, b * QKV_W : (b + 1) * QKV_W]
        dqx[b, :, QKV_W:640] = jnp.zeros((ROWS, 640 - QKV_W), BF)
    scaled, inverse = scaled_rows(x_ref[...])
    a1_t = (scaled * gain_ref[0:1, :]).T.astype(BF)
    da1 = jnp.zeros((ROWS, D), F32)
    for s in range(BLOCKS):
        own = block_of(turn, s)
        part = dqx[own]
        da1 = da1 + dot_nt(part, w_ref[s, :, 0:640])
        first = dot_nn(a1_t, part)
        second = dot_nn(hb_t, oext_ref[own])
        for m in range(8):
            ref = near_ref if m < 4 else far_ref
            rows = slice(m * PIECE, (m + 1) * PIECE)
            ref[m % 4, s, :, 0:512] = first[rows, 0:512].astype(BF)
            ref[m % 4, s, :, 512:640] = (first[rows, 512:640] + second[rows, 0:128]).astype(BF)
            ref[m % 4, s, :, 640:768] = second[rows, 128:256].astype(BF)
    below, grad_gain = norm_back(da1, scaled, inverse, gain_ref[0:1, :])
    below_ref[...] = below + dh1
    sums_ref[0:1, :] = grad_gain


VM = pl.BlockSpec(memory_space=pltpu.VMEM)
SM = pl.BlockSpec(memory_space=pltpu.SMEM)
LIMIT = 56 * 1024 * 1024


def sds(shape, dtype):
    return jax.ShapeDtypeStruct(shape, dtype)


def attend(seq, turn, x, gains, biases, w):
    return pl.pallas_call(
        functools.partial(attend_kernel, seq),
        out_shape=(
            sds((ROWS, 3 * D), BF), sds((16, ROWS), F32), sds((BLOCKS, ROWS, 256), BF),
            sds((ROWS, D), F32), sds((ROWS, D), BF),
        ),
        in_specs=[SM] + [VM] * 4,
        out_specs=[VM] * 5,
        scratch_shapes=[pltpu.VMEM((BLOCKS, ROWS, 640), BF)],
        compiler_params=pltpu.CompilerParams(vmem_limit_bytes=LIMIT),
        cost_estimate=pl.CostEstimate(flops=10**10, bytes_accessed=8 * 10**6, transcendentals=10**6),
        name="attend",
    )(turn, x, gains, biases, w)


def whole(shape):
    return pl.BlockSpec(shape, lambda s: (0,) * len(shape))


def feed(h1, a2, biases, bup, w):
    return pl.pallas_call(
        feed_kernel,
        grid=(BLOCKS,),
        out_shape=(sds((BLOCKS, ROWS, UP_W), BF), sds((BLOCKS, ROWS, UP_W), F32), sds((ROWS, D), F32)),
        in_specs=[
            whole((ROWS, D)), whole((ROWS, D)), whole((2, D)),
            pl.BlockSpec((1, 1, UP_W), lambda s: (s, 0, 0)),
            pl.BlockSpec((1, D, 2 * UP_W), lambda s: (s, 0, 0)),
        ],
        out_specs=[
            pl.BlockSpec((1, ROWS, UP_W), lambda s: (s, 0, 0)),
            pl.BlockSpec((1, ROWS, UP_W), lambda s: (s, 0, 0)),
            whole((ROWS, D)),
        ],
        compiler_params=pltpu.CompilerParams(vmem_limit_bytes=LIMIT),
        cost_estimate=pl.CostEstimate(flops=10**10, bytes_accessed=14 * 10**6, transcendentals=10**6),
        name="feed",
    )(h1, a2, biases, bup, w)


def feed_back(g, h1, a2, gains, z, slope, w):
    grad = sds((4, BLOCKS, PIECE, UP_W), BF)
    grad_spec = pl.BlockSpec((4, 1, PIECE, UP_W), lambda s: (0, s, 0, 0))
    step_spec = pl.BlockSpec((1, ROWS, UP_W), lambda s: (s, 0, 0))
    return pl.pallas_call(
        feed_back_kernel,
        grid=(BLOCKS,),
        out_shape=(grad, grad, grad, grad, sds((BLOCKS, 1, UP_W), F32), sds((ROWS, D), F32), sds((8, D), F32)),
        in_specs=[
            whole((ROWS, D)), whole((ROWS, D)), whole((ROWS, D)), whole((2, D)), step_spec, step_spec,
            pl.BlockSpec((1, D, 2 * UP_W), lambda s: (s, 0, 0)),
        ],
        out_specs=[
            grad_spec, grad_spec, grad_spec, grad_spec,
            pl.BlockSpec((1, 1, UP_W), lambda s: (s, 0, 0)), whole((ROWS, D)), whole((8, D)),
        ],
        scratch_shapes=[pltpu.VMEM((ROWS, D), F32), pltpu.VMEM((D, ROWS), BF), pltpu.VMEM((D, ROWS), BF)],
        compiler_params=pltpu.CompilerParams(vmem_limit_bytes=LIMIT),
        cost_estimate=pl.CostEstimate(flops=2 * 10**10, bytes_accessed=28 * 10**6, transcendentals=0),
        name="feed_back",
    )(g, h1, a2, gains, z, slope, w)


def attend_back(seq, turn, dh1, x, gains, qkv, lse, oext, w):
    grad = sds((4, BLOCKS, PIECE, D), BF)
    return pl.pallas_call(
        functools.partial(attend_back_kernel, seq),
        out_shape=(grad, grad, sds((ROWS, D), F32), sds((8, D), F32)),
        in_specs=[SM] + [VM] * 7,
        out_specs=[VM] * 4,
        scratch_shapes=[
            pltpu.VMEM((BLOCKS, ROWS, 256), BF), pltpu.VMEM((ROWS, D), BF),
            pltpu.VMEM((ROWS, 3 * D), BF), pltpu.VMEM((BLOCKS, ROWS, 640), BF),
        ],
        compiler_params=pltpu.CompilerParams(vmem_limit_bytes=LIMIT),
        cost_estimate=pl.CostEstimate(flops=2 * 10**10, bytes_accessed=16 * 10**6, transcendentals=10**6),
        name="attend_back",
    )(turn, dh1, x, gains, qkv, lse, oext, w)


def adamw_step(param, gradient, first_moment, second_moment):
    fresh_first = beta_one * first_moment + (1.0 - beta_one) * gradient
    fresh_second = beta_two * second_moment + (1.0 - beta_two) * gradient * gradient
    first_hat = fresh_first / (1.0 - beta_one**STEP)
    second_hat = fresh_second / (1.0 - beta_two**STEP)
    updated = param - learn_rate * (
        first_hat / (jnp.sqrt(second_hat) + adam_eps) + decay_rate * param
    )
    return (updated, fresh_first, fresh_second)


class PlainPlan:
    def __init__(self, mesh):
        self.n_row = mesh.shape["row"]
        self.n_col = mesh.shape["col"]
        self.turn = jnp.zeros((1,), jnp.int32)

    def features(self, x):
        return x

    features_back = features

    def hidden(self, bias):
        return bias

    hidden_back = hidden

    def gather(self, shard, widths):
        full = lax.all_gather(shard, ("col", "row"), axis=0, tiled=True)
        full = full.reshape(self.n_col, D, sum(widths))
        parts = []
        start = 0
        for width in widths:
            part = full[:, :, start : start + width].transpose(1, 0, 2)
            parts.append(part.reshape(D, BLOCKS, -1).transpose(1, 0, 2))
            start += width
        return jnp.concatenate(parts, axis=2)

    def reduce(self, near, far, widths):
        full = jnp.concatenate([near, far], axis=0).transpose(0, 2, 1, 3)
        full = full.reshape(D, BLOCKS, -1)
        parts = []
        start = 0
        for width in widths:
            wide = width * self.n_col // BLOCKS
            part = full[:, :, start : start + wide].reshape(D, self.n_col, width)
            parts.append(part.transpose(1, 0, 2))
            start += wide
        packed = jnp.concatenate(parts, axis=2).reshape(self.n_col * D, sum(widths))
        return lax.psum_scatter(packed, ("col", "row"), scatter_dimension=0, tiled=True).astype(F32)

    def total(self, values):
        return lax.psum(values, ("row", "col"))


def flip_row(x, mask):
    return lax.ppermute(x, "row", [(i, i ^ mask) for i in range(8)])


def turn_col(x, shift):
    return lax.ppermute(x, "col", [(i, (i + shift) % 4) for i in range(4)])


CORE, NEXT_X, NEXT_Y = 1, 2, 4


class RelativePlan:
    def __init__(self, mesh):
        self.row = lax.axis_index("row")
        self.col = lax.axis_index("col")
        self.turn = self.col.reshape(1).astype(jnp.int32)

    def flip(self, x, bit, size):
        swapped = x.reshape(x.shape[:-1] + (-1, 2, size))
        swapped = jnp.concatenate([swapped[..., 1:2, :], swapped[..., 0:1, :]], axis=-2).reshape(x.shape)
        return jnp.where((self.row >> bit) & 1 == 1, swapped, x)

    def features(self, x):
        for bit in range(3):
            x = self.flip(x, bit, PIECE << bit)
        blocks = [x[..., i * PIECE : (i + 1) * PIECE] for i in range(8)]
        return jnp.concatenate([blocks[(p >> 2) | ((p & 3) << 1)] for p in range(8)], axis=-1)

    def features_back(self, x):
        blocks = [x[..., i * PIECE : (i + 1) * PIECE] for i in range(8)]
        x = jnp.concatenate([blocks[((i & 1) << 2) | (i >> 1)] for i in range(8)], axis=-1)
        for bit in range(3):
            x = self.flip(x, bit, PIECE << bit)
        return x

    def order(self):
        return lax.rem(self.col - jnp.arange(BLOCKS) + BLOCKS, BLOCKS)

    def hidden(self, bias):
        return bias[self.order()]

    hidden_back = hidden

    def gather(self, shard, widths):
        own = jnp.stack([shard] + [turn_col(shard, s) for s in range(1, BLOCKS)])
        from_x = flip_row(own, NEXT_X)
        from_y = flip_row(own, NEXT_Y)
        diag_low = flip_row(from_y[0:2], NEXT_X)
        diag_high = flip_row(from_x[2:4], NEXT_Y)
        near = [own, from_x, from_y, jnp.concatenate([diag_low, diag_high], axis=0)]
        far = [flip_row(part, CORE) for part in near]
        return jnp.concatenate(near + far, axis=1)

    def reduce(self, near, far, widths):
        other = flip_row(far, CORE)

        def joined(m, blocks):
            return near[m, blocks].astype(F32) + other[m, blocks].astype(F32)

        low, high, every = slice(0, 2), slice(2, 4), slice(0, 4)
        diag_low = flip_row(joined(3, low).astype(BF), NEXT_X)
        diag_high = flip_row(joined(3, high).astype(BF), NEXT_Y)
        to_x = jnp.concatenate([joined(1, low), joined(1, high) + diag_high.astype(F32)], axis=0)
        to_y = jnp.concatenate([joined(2, low) + diag_low.astype(F32), joined(2, high)], axis=0)
        from_x = flip_row(to_x.astype(BF), NEXT_X)
        from_y = flip_row(to_y.astype(BF), NEXT_Y)
        plane = joined(0, every) + from_x.astype(F32) + from_y.astype(F32)
        out = plane[0]
        for s in range(1, BLOCKS):
            out = out + turn_col(plane[s].astype(BF), -s).astype(F32)
        return out

    def total(self, values):
        for mask in (CORE, NEXT_X, NEXT_Y):
            values = values + flip_row(values, mask)
        for mask in (1, 2):
            values = values + lax.ppermute(values, "col", [(i, i ^ mask) for i in range(4)])
        return values


def per_device(
    mesh,
    images, cotangent, counts, w_qkv, w_out, w_up, w_down, norm_gains, res_biases, b_up,
    m_qkv, m_out, m_up, m_down, m_gains, m_biases, m_bup,
    v_qkv, v_out, v_up, v_down, v_gains, v_biases, v_bup,
):
    seq = images.shape[1]
    relative = mesh.shape["row"] == 8 and mesh.shape["col"] == 4
    plan = RelativePlan(mesh) if relative else PlainPlan(mesh)
    row_index = lax.axis_index("row")
    col_index = lax.axis_index("col")
    group_count = jnp.sum(
        jnp.where(jnp.arange(counts.shape[0], dtype=jnp.int32) == row_index, counts, 0)
    )
    live_mask = (col_index < group_count).astype(F32)
    att_widths = (w_qkv.shape[2], w_out.shape[1])
    ffn_widths = (w_up.shape[2], w_down.shape[1])
    att_full, ffn_full = [], []
    for level in range(LAYERS):
        att_shard = jnp.concatenate([w_qkv[level].astype(BF), w_out[level].T.astype(BF)], axis=1)
        ffn_shard = jnp.concatenate([w_up[level].astype(BF), w_down[level].T.astype(BF)], axis=1)
        att_full.append(plan.gather(att_shard, att_widths))
        ffn_full.append(plan.gather(ffn_shard, ffn_widths))

    pad = ((0, ROWS - seq), (0, 0))
    hidden = jnp.pad(plan.features(images[0]), pad)
    gains = plan.features(norm_gains)
    biases = plan.features(res_biases)
    saved = []
    for level in range(LAYERS):
        bup = plan.hidden(b_up[level].reshape(BLOCKS, UP_W))[:, None]
        qkv, lse, oext, h1, a2 = attend(seq, plan.turn, hidden, gains[level], biases[level], att_full[level])
        z, slope, y = feed(h1, a2, biases[level], bup, ffn_full[level])
        saved.append((hidden, qkv, lse, oext, h1, a2, z, slope))
        hidden = y
    layer_out = (plan.features_back(hidden[:seq]) * live_mask)[None]
    upstream = jnp.pad(plan.features(cotangent[0] * live_mask), pad)
    grads = [None] * LAYERS
    smalls = [None] * LAYERS
    for level in reversed(range(LAYERS)):
        below, qkv, lse, oext, h1, a2, z, slope = saved[level]
        upn, upf, dnn, dnf, bup_sum, dh1, sums_two = feed_back(
            upstream, h1, a2, gains[level], z, slope, ffn_full[level]
        )
        down = plan.reduce(dnn, dnf, ffn_widths[1:])
        up = plan.reduce(upn, upf, ffn_widths[:1])
        atn, atf, upstream, sums_one = attend_back(
            seq, plan.turn, dh1, below, gains[level], qkv, lse, oext, att_full[level]
        )
        att = plan.reduce(atn, atf, att_widths)
        grads[level] = (att[:, : att_widths[0]], att[:, att_widths[0] :].T, up, down.T)
        features = plan.features_back(
            jnp.concatenate([sums_one[0:1], sums_two[0:1], sums_two[2:3], sums_two[1:2]], axis=0)
        )
        bup_row = plan.hidden_back(bup_sum[:, 0]).reshape(4, D)
        smalls[level] = plan.total(jnp.concatenate([features, bup_row], axis=0))
    grad_images = plan.features_back(upstream[:seq])[None]
    grad_list = [jnp.stack([grads[level][index] for level in range(LAYERS)]) for index in range(4)]
    grad_list.append(jnp.stack([small[0:2] for small in smalls]))
    grad_list.append(jnp.stack([small[2:4] for small in smalls]))
    grad_list.append(jnp.stack([small[4:8].reshape(FF) for small in smalls]))
    params = [w_qkv, w_out, w_up, w_down, norm_gains, res_biases, b_up]
    firsts = [m_qkv, m_out, m_up, m_down, m_gains, m_biases, m_bup]
    seconds = [v_qkv, v_out, v_up, v_down, v_gains, v_biases, v_bup]
    results = [
        adamw_step(params[index], grad_list[index], firsts[index], seconds[index])
        for index in range(7)
    ]
    return (
        (layer_out, grad_images)
        + tuple(grad_list)
        + tuple(result[0] for result in results[:4])
        + tuple(result[1] for result in results)
        + tuple(result[2] for result in results)
    )


def solution(mesh):
    tokens = P(("row", "col"), None, None)
    matrices = (P(None, "row", "col"), P(None, "col", "row"), P(None, "row", "col"), P(None, "col", "row"))
    vectors = (P(), P(), P())
    in_specs = (tokens, tokens, P()) + (matrices + vectors) * 3
    out_specs = (tokens, tokens) + matrices + vectors + matrices + (matrices + vectors) * 2
    return jax.shard_map(
        functools.partial(per_device, mesh), mesh=mesh, in_specs=in_specs, out_specs=out_specs, check_vma=False
    )
```

```python
import functools

import jax
import jax.numpy as jnp
from jax import lax
from jax.experimental import pallas as pl
from jax.experimental.pallas import tpu as pltpu
from jax.sharding import PartitionSpec as P

HEADS = 12
LAYERS = 2
STEP = 3
D = 768
FF = 3072
HD = 64
BLOCKS = 4
ROWS = 208
QKV_W = 3 * D // BLOCKS
OUT_W = D // BLOCKS
UP_W = FF // BLOCKS
PIECE = 96

norm_eps = 1e-06
root_half = 0.7071067811865476
inv_root_two_pi = 0.3989422804014327
beta_one = 0.9
beta_two = 0.999
adam_eps = 1e-08
learn_rate = 0.06
decay_rate = 0.05

BF = jnp.bfloat16
F32 = jnp.float32


def dot_nn(a, b):
    return lax.dot_general(a, b, (((1,), (0,)), ((), ())), preferred_element_type=F32)


def dot_nt(a, b):
    return lax.dot_general(a, b, (((1,), (1,)), ((), ())), preferred_element_type=F32)


def dot_tn(a, b):
    return lax.dot_general(a, b, (((0,), (0,)), ((), ())), preferred_element_type=F32)


def scaled_rows(x):
    center = jnp.mean(x, axis=-1, keepdims=True)
    shifted = x - center
    inverse = lax.rsqrt(jnp.mean(shifted * shifted, axis=-1, keepdims=True) + norm_eps)
    return shifted * inverse, inverse


def norm_back(upstream, scaled, inverse, gain):
    grad_scaled = upstream * gain
    mean_one = jnp.mean(grad_scaled, axis=-1, keepdims=True)
    mean_two = jnp.mean(grad_scaled * scaled, axis=-1, keepdims=True)
    grad_gain = jnp.sum(upstream * scaled, axis=0, keepdims=True)
    return inverse * (grad_scaled - mean_one - scaled * mean_two), grad_gain


def block_of(turn, s):
    return jnp.bitwise_xor(turn, s)


FFN_W = 2 * UP_W


def piece_copies(info_ref, refs, column, w, sems):
    copies = []
    for s in range(BLOCKS):
        row = []
        for index, ref in enumerate(refs):
            for part in range(8 if ref.shape[1] == 8 else 4):
                if ref.shape[1] == 8:
                    block = part
                    lanes = slice(0, w.shape[2])
                    source = ref.at[
                        block_of(info_ref[0], s), jnp.bitwise_xor(info_ref[1], part), :,
                        column : column + w.shape[2],
                    ]
                else:
                    block = 2 * part + index % 2
                    lanes = slice(index // 2 * D, (index // 2 + 1) * D)
                    source = ref.at[part, s]
                target = w.at[s, block * PIECE : (block + 1) * PIECE, lanes]
                row.append(pltpu.make_async_copy(source, target, sems.at[s, len(row)]))
        copies.append(row)
    return copies


def start_all(copies):
    for row in copies:
        for copy in row:
            copy.start()


def wait_row(row):
    for copy in row:
        copy.wait()


def flip_features(x, mask):
    place = lax.broadcasted_iota(jnp.int32, x.shape, 1)
    block = jnp.zeros(x.shape, jnp.int32)
    for edge in range(1, D // PIECE):
        block = block + (place >= edge * PIECE).astype(jnp.int32)
    for bit in range(3):
        size = PIECE << bit
        even = ((block >> bit) & 1) == 0
        swapped = jnp.where(even, pltpu.roll(x, D - size, axis=1), pltpu.roll(x, size, axis=1))
        x = jnp.where(jnp.full(x.shape, (mask >> bit) & 1, jnp.int32) == 1, swapped, x)
    return x


def prepare_kernel(
    seq, info_ref, counts_ref, images_ref, cot_ref, gains_ref, biases_ref, bup_ref,
    x_ref, g_ref, gains_out, biases_out, bup_out,
):
    mask = info_ref[1]
    live = (info_ref[2] < counts_ref[info_ref[3]]).astype(F32)
    x_ref[ROWS - 16 : ROWS, :] = jnp.zeros((16, D), F32)
    g_ref[ROWS - 16 : ROWS, :] = jnp.zeros((16, D), F32)
    x_ref[0:seq, :] = flip_features(images_ref[0], mask)
    g_ref[0:seq, :] = flip_features(cot_ref[0], mask) * live
    gains_out[...] = flip_features(gains_ref[...], mask)
    biases_out[...] = flip_features(biases_ref[...], mask)
    for level in range(LAYERS):
        for s in range(BLOCKS):
            bup_out[level, s] = bup_ref[level * BLOCKS + block_of(info_ref[0], s)]


def finish_kernel(seq, extra, info_ref, counts_ref, y_ref, *rest):
    out_ref = rest[extra]
    live = (info_ref[2] < counts_ref[info_ref[3]]).astype(F32)
    out_ref[0] = flip_features(y_ref[...], info_ref[1])[0:seq] * live


def attend_kernel(seq, level, n_pieces, info_ref, x_ref, gain_ref, bias_ref, *rest):
    pieces = rest[:n_pieces]
    qkv_ref, lse_ref, oext_ref, h1_ref, a2_ref, blk, w, sems = rest[n_pieces:]
    copies = piece_copies(info_ref, pieces, 0, w, sems)
    start_all(copies)
    turn = info_ref[0]
    x = x_ref[...]
    scaled, _ = scaled_rows(x)
    a1 = (scaled * gain_ref[2 * level : 2 * level + 1, :]).astype(BF)
    for s in range(BLOCKS):
        wait_row(copies[s])
        t = dot_nn(a1, w[s, :, 0:640])
        blk[block_of(turn, s)] = t.astype(BF)
    for b in range(BLOCKS):
        qkv_ref[:, b * QKV_W : (b + 1) * QKV_W] = blk[b, :, 0:QKV_W]
    low_half = lax.broadcasted_iota(jnp.int32, (ROWS, 128), 1) < HD
    key_live = lax.broadcasted_iota(jnp.int32, (ROWS, ROWS), 0) < seq
    scale = HD ** (-0.5)
    oext_ref[:, :, 0:HD] = jnp.zeros((BLOCKS, ROWS, HD), BF)
    for pair in range(HEADS // 2):
        q2 = qkv_ref[:, pair * 128 : (pair + 1) * 128]
        k2 = qkv_ref[:, D + pair * 128 : D + (pair + 1) * 128]
        v2 = qkv_ref[:, 2 * D + pair * 128 : 2 * D + (pair + 1) * 128]
        mixed = []
        for half in range(2):
            live = low_half if half == 0 else jnp.logical_not(low_half)
            qm = jnp.where(live, q2, jnp.zeros_like(q2))
            st = jnp.where(key_live, dot_nt(k2, qm) * scale, -1e30)
            peak = jnp.max(st, axis=0, keepdims=True)
            grown = jnp.exp(st - peak)
            total = jnp.sum(grown, axis=0, keepdims=True)
            head = 2 * pair + half
            lse_ref[head : head + 1, :] = peak + jnp.log(total)
            probs = (grown * (1.0 / total)).astype(BF)
            mixed.append(dot_tn(probs, v2))
        both = jnp.where(low_half, mixed[0], mixed[1]).astype(BF)
        for half in range(2):
            head = 2 * pair + half
            lane = HD + (head % 3) * HD
            oext_ref[head // 3, :, lane : lane + HD] = both[:, half * HD : (half + 1) * HD]
    total = x + bias_ref[2 * level : 2 * level + 1, :]
    for s in range(BLOCKS):
        total = total + dot_nt(oext_ref[block_of(turn, s)], w[s, :, 512:768])
    h1_ref[...] = total
    scaled2, _ = scaled_rows(total)
    a2_ref[...] = (scaled2 * gain_ref[2 * level + 1 : 2 * level + 2, :]).astype(BF)


def feed_kernel(level, n_pieces, info_ref, h1_ref, a2_ref, bias_ref, bup_ref, *rest):
    pieces = rest[:n_pieces]
    z_ref, slope_ref, y_ref, w, sems = rest[n_pieces:]
    s = pl.program_id(0)
    copies = piece_copies(info_ref, pieces, D, w, sems)

    @pl.when(s == 0)
    def _():
        start_all(copies)
        y_ref[...] = h1_ref[...] + bias_ref[2 * level + 1 : 2 * level + 2, :]

    for step in range(BLOCKS):

        @pl.when(s == step)
        def _():
            wait_row(copies[step])

    u = dot_nn(a2_ref[...], w[s, :, 0:UP_W]) + bup_ref[0, 0]
    bell = 0.5 * (1.0 + lax.erf(u * root_half))
    z = (u * bell).astype(BF)
    z_ref[0] = z
    slope_ref[0] = bell + u * inv_root_two_pi * jnp.exp(-0.5 * u * u)
    y_ref[...] += dot_nt(z, w[s, :, UP_W:FFN_W])


def put_grad(near_ref, far_ref, value, first, width):
    for j in range(8):
        ref = near_ref if j % 2 == 0 else far_ref
        ref[j // 2, 0, :, first : first + width] = value[j * PIECE : (j + 1) * PIECE]


def feed_back_kernel(level, n_pieces, n_after, info_ref, g_ref, h1_ref, a2_ref, gain_ref, z_ref, slope_ref, *rest):
    pieces = rest[:n_pieces]
    near_ref, far_ref, bup_ref, dh1_ref, sums_ref, da2, gb_t, a2_t, w, sems = rest[n_pieces + n_after :]
    s = pl.program_id(0)
    copies = piece_copies(info_ref, pieces, D, w, sems)

    @pl.when(s == 0)
    def _():
        start_all(copies)
        da2[...] = jnp.zeros_like(da2)
        gb_t[...] = g_ref[...].T.astype(BF)
        a2_t[...] = a2_ref[...].T

    for step in range(BLOCKS):

        @pl.when(s == step)
        def _():
            wait_row(copies[step])

    gb = g_ref[...].astype(BF)
    put_grad(near_ref, far_ref, dot_nn(gb_t[...], z_ref[0]).astype(BF), UP_W, UP_W)
    du = dot_nn(gb, w[s, :, UP_W:FFN_W]) * slope_ref[0]
    bup_ref[0] = jnp.sum(du, axis=0, keepdims=True)
    dub = du.astype(BF)
    put_grad(near_ref, far_ref, dot_nn(a2_t[...], dub).astype(BF), 0, UP_W)
    da2[...] += dot_nt(dub, w[s, :, 0:UP_W])

    @pl.when(s == BLOCKS - 1)
    def _():
        g = g_ref[...]
        scaled, inverse = scaled_rows(h1_ref[...])
        below, grad_gain = norm_back(da2[...], scaled, inverse, gain_ref[2 * level + 1 : 2 * level + 2, :])
        dh1 = below + g
        dh1_ref[...] = dh1
        sums_ref[0:1, :] = grad_gain
        sums_ref[1:2, :] = jnp.sum(dh1, axis=0, keepdims=True)
        sums_ref[2:3, :] = jnp.sum(g, axis=0, keepdims=True)


def attend_back_kernel(
    seq, level, n_pieces, n_after,
    info_ref, dh1_ref, x_ref, gain_ref, qkv_ref, lse_ref, oext_ref, sums_in, bup_in, *rest,
):
    pieces = rest[:n_pieces]
    near_ref, far_ref, below_ref, small_ref, dext, dmix, dqkv, dqx, w, sems = rest[n_pieces + n_after :]
    copies = piece_copies(info_ref, pieces, 0, w, sems)
    start_all(copies)
    turn = info_ref[0]
    dh1 = dh1_ref[...]
    hb = dh1.astype(BF)
    hb_t = dh1.T.astype(BF)
    for s in range(BLOCKS):
        wait_row(copies[s])
        dext[block_of(turn, s)] = dot_nn(hb, w[s, :, 512:768]).astype(BF)
    for b in range(BLOCKS):
        dmix[:, b * OUT_W : (b + 1) * OUT_W] = dext[b, :, HD : HD + OUT_W]
    low_half = lax.broadcasted_iota(jnp.int32, (ROWS, 128), 1) < HD
    key_live = lax.broadcasted_iota(jnp.int32, (ROWS, ROWS), 0) < seq
    scale = HD ** (-0.5)
    for pair in range(HEADS // 2):
        q2 = qkv_ref[:, pair * 128 : (pair + 1) * 128]
        k2 = qkv_ref[:, D + pair * 128 : D + (pair + 1) * 128]
        v2 = qkv_ref[:, 2 * D + pair * 128 : 2 * D + (pair + 1) * 128]
        d2 = dmix[:, pair * 128 : (pair + 1) * 128]
        dq = jnp.zeros((ROWS, 128), F32)
        dk = jnp.zeros((ROWS, 128), F32)
        dv = jnp.zeros((ROWS, 128), F32)
        for half in range(2):
            head = 2 * pair + half
            live = low_half if half == 0 else jnp.logical_not(low_half)
            none = jnp.zeros_like(q2)
            qm = jnp.where(live, q2, none)
            km = jnp.where(live, k2, none)
            dm = jnp.where(live, d2, none)
            st = jnp.where(key_live, dot_nt(k2, qm) * scale, -1e30)
            probs = jnp.exp(st - lse_ref[head : head + 1, :])
            dprobs = dot_nt(v2, dm)
            inner = jnp.sum(probs * dprobs, axis=0, keepdims=True)
            dst = (probs * (dprobs - inner) * scale).astype(BF)
            dv = dv + dot_nn(probs.astype(BF), dm)
            dk = dk + dot_nn(dst, qm)
            dq = dq + dot_tn(dst, km)
        dqkv[:, pair * 128 : (pair + 1) * 128] = dq.astype(BF)
        dqkv[:, D + pair * 128 : D + (pair + 1) * 128] = dk.astype(BF)
        dqkv[:, 2 * D + pair * 128 : 2 * D + (pair + 1) * 128] = dv.astype(BF)
    for b in range(BLOCKS):
        dqx[b, :, 0:QKV_W] = dqkv[:, b * QKV_W : (b + 1) * QKV_W]
        dqx[b, :, QKV_W:640] = jnp.zeros((ROWS, 640 - QKV_W), BF)
    gain = gain_ref[2 * level : 2 * level + 1, :]
    scaled, inverse = scaled_rows(x_ref[...])
    a1_t = (scaled * gain).T.astype(BF)
    da1 = jnp.zeros((ROWS, D), F32)
    for s in range(BLOCKS):
        own = block_of(turn, s)
        part = dqx[own]
        da1 = da1 + dot_nt(part, w[s, :, 0:640])
        first = dot_nn(a1_t, part)
        second = dot_nn(hb_t, oext_ref[own])
        for j in range(8):
            ref = near_ref if j % 2 == 0 else far_ref
            rows = slice(j * PIECE, (j + 1) * PIECE)
            ref[j // 2, s, :, 0:512] = first[rows, 0:512].astype(BF)
            ref[j // 2, s, :, 512:640] = (first[rows, 512:640] + second[rows, 0:128]).astype(BF)
            ref[j // 2, s, :, 640:768] = second[rows, 128:256].astype(BF)
    below, grad_gain = norm_back(da1, scaled, inverse, gain)
    below = below + dh1
    if level == 0:
        below_ref[0] = flip_features(below, info_ref[1])[0:seq]
    else:
        below_ref[...] = below
    small_ref[0:1, :] = grad_gain
    small_ref[1:4, :] = sums_in[0:3, :]
    small_ref[4:8, :] = jnp.zeros((4, D), F32)
    small_ref[...] = flip_features(small_ref[...], info_ref[1])
    for s in range(BLOCKS):
        small_ref[pl.ds(4 + block_of(turn, s), 1), :] = bup_in[s]


VM = pl.BlockSpec(memory_space=pltpu.VMEM)
SM = pl.BlockSpec(memory_space=pltpu.SMEM)
HB = pl.BlockSpec(memory_space=pl.ANY)
LIMIT = 60 * 1024 * 1024


def sds(shape, dtype):
    return jax.ShapeDtypeStruct(shape, dtype)


def params():
    return pltpu.CompilerParams(vmem_limit_bytes=LIMIT)


def cost(flops, traffic):
    return pl.CostEstimate(flops=flops, bytes_accessed=traffic, transcendentals=0)


def weight_scratch(width):
    return [pltpu.VMEM((BLOCKS, D, width), BF), pltpu.SemaphoreType.DMA((BLOCKS, 16))]


def prepare(seq, info, counts, images, cotangent, gains, biases, bup):
    return pl.pallas_call(
        functools.partial(prepare_kernel, seq),
        out_shape=(
            sds((ROWS, D), F32), sds((ROWS, D), F32), sds(gains.shape, F32), sds(biases.shape, F32),
            sds((LAYERS, BLOCKS, 1, UP_W), F32),
        ),
        in_specs=[SM, SM] + [VM] * 5,
        out_specs=[VM] * 5,
        compiler_params=params(),
        cost_estimate=cost(10**7, 10**5),
        name="prepare",
    )(info, counts, images, cotangent, gains, biases, bup)


def finish(seq, info, counts, y, after):
    return pl.pallas_call(
        functools.partial(finish_kernel, seq, len(after)),
        out_shape=sds((1, seq, D), F32),
        in_specs=[SM, SM, VM] + [HB] * len(after),
        out_specs=VM,
        compiler_params=params(),
        cost_estimate=cost(10**7, 10**5),
        name="finish",
    )(info, counts, y, *after)


def attend(seq, level, info, x, gains, biases, pieces):
    return pl.pallas_call(
        functools.partial(attend_kernel, seq, level, len(pieces)),
        out_shape=(
            sds((ROWS, 3 * D), BF), sds((16, ROWS), F32), sds((BLOCKS, ROWS, 256), BF),
            sds((ROWS, D), F32), sds((ROWS, D), BF),
        ),
        in_specs=[SM] + [VM] * 3 + [HB] * len(pieces),
        out_specs=[VM] * 5,
        scratch_shapes=[pltpu.VMEM((BLOCKS, ROWS, 640), BF)] + weight_scratch(D),
        compiler_params=params(),
        cost_estimate=cost(10**7, 10**5),
        name="attend",
    )(info, x, gains, biases, *pieces)


def whole(shape):
    return pl.BlockSpec(shape, lambda s: (0,) * len(shape))


def feed(level, info, h1, a2, biases, bup, pieces):
    return pl.pallas_call(
        functools.partial(feed_kernel, level, len(pieces)),
        grid=(BLOCKS,),
        out_shape=(sds((BLOCKS, ROWS, UP_W), BF), sds((BLOCKS, ROWS, UP_W), F32), sds((ROWS, D), F32)),
        in_specs=[
            SM, whole((ROWS, D)), whole((ROWS, D)), whole(biases.shape),
            pl.BlockSpec((1, 1, 1, UP_W), lambda s: (level, s, 0, 0)),
        ]
        + [HB] * len(pieces),
        out_specs=[
            pl.BlockSpec((1, ROWS, UP_W), lambda s: (s, 0, 0)),
            pl.BlockSpec((1, ROWS, UP_W), lambda s: (s, 0, 0)),
            whole((ROWS, D)),
        ],
        scratch_shapes=weight_scratch(FFN_W),
        compiler_params=params(),
        cost_estimate=cost(10**7, 10**5),
        name="feed",
    )(info, h1, a2, biases, bup, *pieces)


def feed_back(level, info, g, h1, a2, gains, z, slope, pieces, after):
    grad = sds((4, BLOCKS, PIECE, FFN_W), BF)
    grad_spec = pl.BlockSpec((4, 1, PIECE, FFN_W), lambda s: (0, s, 0, 0))
    step_spec = pl.BlockSpec((1, ROWS, UP_W), lambda s: (s, 0, 0))
    return pl.pallas_call(
        functools.partial(feed_back_kernel, level, len(pieces), len(after)),
        grid=(BLOCKS,),
        out_shape=(grad, grad, sds((BLOCKS, 1, UP_W), F32), sds((ROWS, D), F32), sds((8, D), F32)),
        in_specs=[SM, whole((ROWS, D)), whole((ROWS, D)), whole((ROWS, D)), whole(gains.shape), step_spec, step_spec]
        + [HB] * (len(pieces) + len(after)),
        out_specs=[
            grad_spec, grad_spec,
            pl.BlockSpec((1, 1, UP_W), lambda s: (s, 0, 0)), whole((ROWS, D)), whole((8, D)),
        ],
        scratch_shapes=[pltpu.VMEM((ROWS, D), F32), pltpu.VMEM((D, ROWS), BF), pltpu.VMEM((D, ROWS), BF)]
        + weight_scratch(FFN_W),
        compiler_params=params(),
        cost_estimate=cost(10**7, 10**5),
        name="feed_back",
    )(info, g, h1, a2, gains, z, slope, *pieces, *after)


def attend_back(seq, level, info, dh1, x, gains, qkv, lse, oext, sums, bup, pieces, after):
    grad = sds((4, BLOCKS, PIECE, D), BF)
    below = sds((1, seq, D), F32) if level == 0 else sds((ROWS, D), F32)
    return pl.pallas_call(
        functools.partial(attend_back_kernel, seq, level, len(pieces), len(after)),
        out_shape=(grad, grad, below, sds((8, D), F32)),
        in_specs=[SM] + [VM] * 8 + [HB] * (len(pieces) + len(after)),
        out_specs=[VM] * 4,
        scratch_shapes=[
            pltpu.VMEM((BLOCKS, ROWS, 256), BF), pltpu.VMEM((ROWS, D), BF),
            pltpu.VMEM((ROWS, 3 * D), BF), pltpu.VMEM((BLOCKS, ROWS, 640), BF),
        ]
        + weight_scratch(D),
        compiler_params=params(),
        cost_estimate=cost(10**7, 10**5),
        name="attend_back",
    )(info, dh1, x, gains, qkv, lse, oext, sums, bup, *pieces, *after)


def adamw_step(param, gradient, first_moment, second_moment):
    fresh_first = beta_one * first_moment + (1.0 - beta_one) * gradient
    fresh_second = beta_two * second_moment + (1.0 - beta_two) * gradient * gradient
    first_hat = fresh_first / (1.0 - beta_one**STEP)
    second_hat = fresh_second / (1.0 - beta_two**STEP)
    updated = param - learn_rate * (
        first_hat / (jnp.sqrt(second_hat) + adam_eps) + decay_rate * param
    )
    return (updated, fresh_first, fresh_second)


def after(value, *earlier):
    return lax.optimization_barrier((value,) + earlier)[0]


class PlainPlan:
    def __init__(self, mesh):
        self.n_row = mesh.shape["row"]
        self.n_col = mesh.shape["col"]
        self.turn = jnp.int32(0)
        self.mask = jnp.int32(0)

    def gather(self, shard, widths):
        full = lax.all_gather(shard, ("col", "row"), axis=0, tiled=True)
        full = full.reshape(self.n_col, D, sum(widths))
        parts = []
        start = 0
        for width in widths:
            part = full[:, :, start : start + width].transpose(1, 0, 2)
            parts.append(part.reshape(D, BLOCKS, -1).transpose(1, 0, 2))
            start += width
        return jnp.concatenate(parts, axis=2).reshape(BLOCKS, 8, PIECE, -1)

    def reduce(self, near, far, widths, *earlier):
        full = jnp.stack([near, far], axis=1).transpose(0, 1, 3, 2, 4)
        full = full.reshape(D, BLOCKS, -1)
        parts = []
        start = 0
        for width in widths:
            wide = width * self.n_col // BLOCKS
            part = full[:, :, start : start + wide].reshape(D, self.n_col, width)
            parts.append(part.transpose(1, 0, 2))
            start += wide
        packed = jnp.concatenate(parts, axis=2).reshape(self.n_col * D, sum(widths))
        done = lax.psum_scatter(packed, ("col", "row"), scatter_dimension=0, tiled=True).astype(F32)
        for _ in range(2):
            yield done
        yield done, done
        yield done
        yield done

    def total(self, values, stages):
        return lax.psum(values, ("row", "col"))


def flip_row(x, mask):
    return lax.ppermute(x, "row", [(i, i ^ mask) for i in range(8)])


def flip_col(x, mask):
    return lax.ppermute(x, "col", [(i, i ^ mask) for i in range(4)])


CORE, NEXT_X, NEXT_Y = 1, 2, 4


class RelativeFetch:
    def __init__(self, shard):
        self.shard = shard

    def turn_one(self, *hold):
        shard = after(self.shard, *hold)
        self.pair = jnp.stack([shard, flip_col(shard, 1)])
        return self.pair[1]

    def turn_two(self, *hold):
        self.others = flip_col(after(self.pair, *hold), 2)
        return self.others

    def plane(self, *hold):
        self.own = after(jnp.concatenate([self.pair, self.others], axis=0), *hold)
        self.from_x = flip_row(self.own, NEXT_X)
        self.from_y = flip_row(self.own, NEXT_Y)
        return self.from_x

    def rest(self, *hold):
        from_x, from_y = after(self.from_x, self.from_y, *hold), after(self.from_y, self.from_x, *hold)
        diag_low = flip_row(from_y[0:2], NEXT_X)
        diag_high = flip_row(from_x[2:4], NEXT_Y)
        near = jnp.concatenate([self.own, from_x, from_y, diag_low, diag_high], axis=0)
        near = near.reshape((4, BLOCKS) + self.shard.shape)
        return [near, flip_row(near, CORE)]


class RelativePlan:
    def __init__(self, mesh):
        self.turn = lax.axis_index("col").astype(jnp.int32)
        self.mask = lax.axis_index("row").astype(jnp.int32)

    def gather(self, shard, widths):
        full = lax.all_gather(shard, ("col", "row"), axis=0, tiled=True)
        return full.reshape(BLOCKS, 8, PIECE, -1)

    def reduce(self, near, far, widths, *earlier):
        far = after(far, *earlier)
        other = flip_row(far, CORE)
        hold = yield other

        def joined(m, blocks):
            return near[m, blocks].astype(F32) + other[m, blocks].astype(F32)

        low, high, every = slice(0, 2), slice(2, 4), slice(0, 4)
        diag_low = flip_row(after(joined(3, low).astype(BF), *hold), NEXT_X)
        diag_high = flip_row(after(joined(3, high).astype(BF), *hold), NEXT_Y)
        hold = yield diag_low, diag_high
        to_x = jnp.concatenate([joined(1, low), joined(1, high) + diag_high.astype(F32)], axis=0)
        to_y = jnp.concatenate([joined(2, low) + diag_low.astype(F32), joined(2, high)], axis=0)
        from_x = flip_row(after(to_x.astype(BF), *hold), NEXT_X)
        from_y = flip_row(after(to_y.astype(BF), *hold), NEXT_Y)
        hold = yield from_x, from_y
        plane = joined(0, every) + from_x.astype(F32) + from_y.astype(F32)
        others = flip_col(after(plane[2:4].astype(BF), *hold), 2)
        hold = yield others
        pair = plane[0:2] + after(others, *hold).astype(F32)
        yield pair[0] + flip_col(pair[1].astype(BF), 1).astype(F32)

    def total(self, values, stages):
        hops = [(flip_row, CORE), (flip_row, NEXT_X), (flip_row, NEXT_Y), (flip_col, 1), (flip_col, 2)]
        for (flip, mask), stage in zip(hops, stages):
            values = values + after(flip(values, mask), *stage)
        return values


def per_device(
    mesh,
    images, cotangent, counts, w_qkv, w_out, w_up, w_down, norm_gains, res_biases, b_up,
    m_qkv, m_out, m_up, m_down, m_gains, m_biases, m_bup,
    v_qkv, v_out, v_up, v_down, v_gains, v_biases, v_bup,
):
    seq = images.shape[1]
    relative = mesh.shape["row"] == 8 and mesh.shape["col"] == 4
    plan = RelativePlan(mesh) if relative else PlainPlan(mesh)
    info = jnp.stack([plan.turn, plan.mask, lax.axis_index("col"), lax.axis_index("row")]).astype(jnp.int32)
    att_widths = (w_qkv.shape[2], w_out.shape[1])
    ffn_widths = (w_up.shape[2], w_down.shape[1])
    shards = []
    for level in range(LAYERS):
        shards.append([
            jnp.concatenate([w_qkv[level].astype(BF), w_out[level].T.astype(BF)], axis=1),
            w_up[level].astype(BF),
            w_down[level].T.astype(BF),
        ])

    hidden, upstream, gains, biases, bup = prepare(
        seq, info, counts, images, cotangent,
        norm_gains.reshape(2 * LAYERS, D), res_biases.reshape(2 * LAYERS, D),
        b_up.reshape(LAYERS * BLOCKS, 1, UP_W),
    )
    saved, att_full, ffn_full = [], [], []

    def forward_attend(level, hidden, pieces):
        att_full.append(pieces)
        return attend(seq, level, info, hidden, gains, biases, pieces)

    def forward_feed(level, hidden, state, pieces):
        qkv, lse, oext, h1, a2 = state
        ffn_full.append(pieces)
        z, slope, y = feed(level, info, h1, a2, biases, bup, pieces)
        saved.append((hidden, qkv, lse, oext, h1, a2, z, slope))
        return y

    def gathered(level):
        return [plan.gather(jnp.concatenate(shards[level], axis=1), att_widths + ffn_widths)]

    later = gathered(1)
    if relative:
        fetches = [RelativeFetch(shard) for shard in shards[0]]
        one = fetches[0].turn_one()
        two = fetches[0].turn_two()
        plane, arrived = (), []
        for index, fetch in enumerate(fetches):
            plane = (fetch.plane(*plane),)
            if index + 1 < len(fetches):
                one = fetches[index + 1].turn_one(one)
                two = fetches[index + 1].turn_two(two)
            arrived.append(fetch.rest(two))
        sooner = arrived[0], arrived[1] + arrived[2]
    else:
        sooner = (gathered(0),) * 2
    state = forward_attend(0, hidden, sooner[0])
    middle = forward_feed(0, hidden, state, sooner[1])
    state = forward_attend(1, middle, later)
    hidden = forward_feed(1, middle, state, later)
    smalls = [None] * LAYERS

    def backward_feed(level, upstream, landed):
        below, qkv, lse, oext, h1, a2, z, slope = saved[level]
        return feed_back(level, info, upstream, h1, a2, gains, z, slope, ffn_full[level], landed)

    def backward_attend(level, dh1, sums, bup_sum, landed):
        below, qkv, lse, oext, h1, a2, z, slope = saved[level]
        return attend_back(
            seq, level, info, dh1, below, gains, qkv, lse, oext, sums, bup_sum, att_full[level], landed
        )

    near, far, bup_sum, dh1, sums = backward_feed(1, upstream, [])
    ffn_one = plan.reduce(near, far, ffn_widths)
    core_ffn_one = next(ffn_one)
    near, far, upstream, smalls[1] = backward_attend(1, dh1, sums, bup_sum, [])
    one_near, one_far = near, far
    near, far, bup_sum, dh1, sums = backward_feed(0, upstream, [core_ffn_one])
    diag_ffn_one = ffn_one.send(())
    zero_near, zero_far = near, far
    near, far, upstream, smalls[0] = backward_attend(0, dh1, sums, bup_sum, [*diag_ffn_one])
    plane_ffn_one = ffn_one.send(())
    att_one = plan.reduce(one_near, one_far, att_widths, smalls[0])
    core_att_one = next(att_one)
    ffn_zero = plan.reduce(zero_near, zero_far, ffn_widths, smalls[0], core_att_one)
    core_ffn_zero = next(ffn_zero)
    att_zero = plan.reduce(near, far, att_widths, core_ffn_zero)
    core_att_zero = next(att_zero)
    diag_att_one = att_one.send(diag_ffn_one)
    plane_att_one = att_one.send(())
    diag_ffn_zero = ffn_zero.send(plane_ffn_one)
    plane_ffn_zero = ffn_zero.send(())
    diag_att_zero = att_zero.send(plane_att_one)
    plane_att_zero = att_zero.send(())
    turn_ffn_one, turn_att_one = ffn_one.send((smalls[0],)), att_one.send(())
    turn_ffn_zero, turn_att_zero = ffn_zero.send(()), att_zero.send(())
    done = {}
    done["ffn", 1], done["att", 1] = ffn_one.send(diag_ffn_zero), att_one.send(plane_ffn_zero)
    done["ffn", 0], done["att", 0] = ffn_zero.send(plane_att_zero), att_zero.send(())
    layer_out = finish(seq, info, counts, hidden, [upstream])
    grads = []
    for level in range(LAYERS):
        ffn, att = done["ffn", level], done["att", level]
        grads.append((
            att[:, : att_widths[0]], att[:, att_widths[0] :].T, ffn[:, : ffn_widths[0]], ffn[:, ffn_widths[0] :].T
        ))
    stages = [plane_ffn_one, diag_att_one, plane_att_one, diag_ffn_zero, plane_ffn_zero]
    small = plan.total(jnp.concatenate(smalls, axis=0), stages).reshape(LAYERS, 8, D)
    grad_list = [jnp.stack([grads[level][index] for level in range(LAYERS)]) for index in range(4)]
    grad_list += [small[:, 0:2], small[:, 2:4], small[:, 4:8].reshape(LAYERS, FF)]
    params_in = [w_qkv, w_out, w_up, w_down, norm_gains, res_biases, b_up]
    firsts = [m_qkv, m_out, m_up, m_down, m_gains, m_biases, m_bup]
    seconds = [v_qkv, v_out, v_up, v_down, v_gains, v_biases, v_bup]
    results = [
        adamw_step(params_in[index], grad_list[index], firsts[index], seconds[index])
        for index in range(7)
    ]
    return (
        (layer_out, upstream)
        + tuple(grad_list)
        + tuple(result[0] for result in results[:4])
        + tuple(result[1] for result in results)
        + tuple(result[2] for result in results)
    )


def solution(mesh):
    tokens = P(("row", "col"), None, None)
    matrices = (P(None, "row", "col"), P(None, "col", "row"), P(None, "row", "col"), P(None, "col", "row"))
    vectors = (P(), P(), P())
    in_specs = (tokens, tokens, P()) + (matrices + vectors) * 3
    out_specs = (tokens, tokens) + matrices + vectors + matrices + (matrices + vectors) * 2
    return jax.shard_map(
        functools.partial(per_device, mesh), mesh=mesh, in_specs=in_specs, out_specs=out_specs, check_vma=False
    )
```

```python
import functools

import jax
import jax.numpy as jnp
from jax import lax
from jax.experimental import pallas as pl
from jax.experimental.pallas import tpu as pltpu
from jax.sharding import PartitionSpec as P

HEADS = 12
LAYERS = 2
STEP = 3
D = 768
FF = 3072
HD = 64
BLOCKS = 4
ROWS = 208
QKV_W = 3 * D // BLOCKS
OUT_W = D // BLOCKS
UP_W = FF // BLOCKS
PIECE = 96

norm_eps = 1e-06
root_half = 0.7071067811865476
inv_root_two_pi = 0.3989422804014327
beta_one = 0.9
beta_two = 0.999
adam_eps = 1e-08
learn_rate = 0.06
decay_rate = 0.05

BF = jnp.bfloat16
F32 = jnp.float32


def dot_nn(a, b):
    return lax.dot_general(a, b, (((1,), (0,)), ((), ())), preferred_element_type=F32)


def dot_nt(a, b):
    return lax.dot_general(a, b, (((1,), (1,)), ((), ())), preferred_element_type=F32)


def dot_tn(a, b):
    return lax.dot_general(a, b, (((0,), (0,)), ((), ())), preferred_element_type=F32)


def scaled_rows(x):
    center = jnp.mean(x, axis=-1, keepdims=True)
    shifted = x - center
    inverse = lax.rsqrt(jnp.mean(shifted * shifted, axis=-1, keepdims=True) + norm_eps)
    return shifted * inverse, inverse


def norm_back(upstream, scaled, inverse, gain):
    grad_scaled = upstream * gain
    mean_one = jnp.mean(grad_scaled, axis=-1, keepdims=True)
    mean_two = jnp.mean(grad_scaled * scaled, axis=-1, keepdims=True)
    grad_gain = jnp.sum(upstream * scaled, axis=0, keepdims=True)
    return inverse * (grad_scaled - mean_one - scaled * mean_two), grad_gain


def block_of(turn, s):
    return jnp.bitwise_xor(turn, s)


FFN_W = 2 * UP_W


def piece_copies(info_ref, refs, column, w, sems):
    copies = []
    for s in range(BLOCKS):
        row = []
        for index, ref in enumerate(refs):
            for part in range(8 if ref.shape[1] == 8 else 4):
                if ref.shape[1] == 8:
                    block = part
                    lanes = slice(0, w.shape[2])
                    source = ref.at[
                        block_of(info_ref[0], s), jnp.bitwise_xor(info_ref[1], part), :,
                        column : column + w.shape[2],
                    ]
                else:
                    block = 2 * part + index % 2
                    lanes = slice(index // 2 * D, (index // 2 + 1) * D)
                    source = ref.at[part, s]
                target = w.at[s, block * PIECE : (block + 1) * PIECE, lanes]
                row.append(pltpu.make_async_copy(source, target, sems.at[s, len(row)]))
        copies.append(row)
    return copies


def start_all(copies):
    for row in copies:
        for copy in row:
            copy.start()


def wait_row(row):
    for copy in row:
        copy.wait()


def flip_features(x, mask):
    place = lax.broadcasted_iota(jnp.int32, x.shape, 1)
    block = jnp.zeros(x.shape, jnp.int32)
    for edge in range(1, D // PIECE):
        block = block + (place >= edge * PIECE).astype(jnp.int32)
    for bit in range(3):
        size = PIECE << bit
        even = ((block >> bit) & 1) == 0
        swapped = jnp.where(even, pltpu.roll(x, D - size, axis=1), pltpu.roll(x, size, axis=1))
        x = jnp.where(jnp.full(x.shape, (mask >> bit) & 1, jnp.int32) == 1, swapped, x)
    return x


def prepare_kernel(
    seq, info_ref, counts_ref, images_ref, cot_ref, gains_ref, biases_ref, bup_ref,
    x_ref, g_ref, gains_out, biases_out, bup_out,
):
    mask = info_ref[1]
    live = (info_ref[2] < counts_ref[info_ref[3]]).astype(F32)
    x_ref[ROWS - 16 : ROWS, :] = jnp.zeros((16, D), F32)
    g_ref[ROWS - 16 : ROWS, :] = jnp.zeros((16, D), F32)
    x_ref[0:seq, :] = flip_features(images_ref[0], mask)
    g_ref[0:seq, :] = flip_features(cot_ref[0], mask) * live
    gains_out[...] = flip_features(gains_ref[...], mask)
    biases_out[...] = flip_features(biases_ref[...], mask)
    for level in range(LAYERS):
        for s in range(BLOCKS):
            bup_out[level, s] = bup_ref[level * BLOCKS + block_of(info_ref[0], s)]


def finish_kernel(seq, extra, info_ref, counts_ref, y_ref, *rest):
    out_ref = rest[extra]
    live = (info_ref[2] < counts_ref[info_ref[3]]).astype(F32)
    out_ref[0] = flip_features(y_ref[...], info_ref[1])[0:seq] * live


def attend_kernel(seq, level, n_pieces, info_ref, x_ref, gain_ref, bias_ref, *rest):
    pieces = rest[:n_pieces]
    qkv_ref, lse_ref, oext_ref, h1_ref, a2_ref, blk, w, sems = rest[n_pieces:]
    copies = piece_copies(info_ref, pieces, 0, w, sems)
    start_all(copies)
    turn = info_ref[0]
    x = x_ref[...]
    scaled, _ = scaled_rows(x)
    a1 = (scaled * gain_ref[2 * level : 2 * level + 1, :]).astype(BF)
    for s in range(BLOCKS):
        wait_row(copies[s])
        t = dot_nn(a1, w[s, :, 0:640])
        blk[block_of(turn, s)] = t.astype(BF)
    for b in range(BLOCKS):
        qkv_ref[:, b * QKV_W : (b + 1) * QKV_W] = blk[b, :, 0:QKV_W]
    low_half = lax.broadcasted_iota(jnp.int32, (ROWS, 128), 1) < HD
    key_live = lax.broadcasted_iota(jnp.int32, (ROWS, ROWS), 0) < seq
    scale = HD ** (-0.5)
    oext_ref[:, :, 0:HD] = jnp.zeros((BLOCKS, ROWS, HD), BF)
    for pair in range(HEADS // 2):
        q2 = qkv_ref[:, pair * 128 : (pair + 1) * 128]
        k2 = qkv_ref[:, D + pair * 128 : D + (pair + 1) * 128]
        v2 = qkv_ref[:, 2 * D + pair * 128 : 2 * D + (pair + 1) * 128]
        mixed = []
        for half in range(2):
            live = low_half if half == 0 else jnp.logical_not(low_half)
            qm = jnp.where(live, q2, jnp.zeros_like(q2))
            st = jnp.where(key_live, dot_nt(k2, qm) * scale, -1e30)
            peak = jnp.max(st, axis=0, keepdims=True)
            grown = jnp.exp(st - peak)
            total = jnp.sum(grown, axis=0, keepdims=True)
            head = 2 * pair + half
            lse_ref[head : head + 1, :] = peak + jnp.log(total)
            probs = (grown * (1.0 / total)).astype(BF)
            mixed.append(dot_tn(probs, v2))
        both = jnp.where(low_half, mixed[0], mixed[1]).astype(BF)
        for half in range(2):
            head = 2 * pair + half
            lane = HD + (head % 3) * HD
            oext_ref[head // 3, :, lane : lane + HD] = both[:, half * HD : (half + 1) * HD]
    total = x + bias_ref[2 * level : 2 * level + 1, :]
    for s in range(BLOCKS):
        total = total + dot_nt(oext_ref[block_of(turn, s)], w[s, :, 512:768])
    h1_ref[...] = total
    scaled2, _ = scaled_rows(total)
    a2_ref[...] = (scaled2 * gain_ref[2 * level + 1 : 2 * level + 2, :]).astype(BF)


def feed_kernel(level, n_pieces, info_ref, h1_ref, a2_ref, bias_ref, bup_ref, *rest):
    pieces = rest[:n_pieces]
    z_ref, slope_ref, y_ref, w, sems = rest[n_pieces:]
    s = pl.program_id(0)
    copies = piece_copies(info_ref, pieces, D, w, sems)

    @pl.when(s == 0)
    def _():
        start_all(copies)
        y_ref[...] = h1_ref[...] + bias_ref[2 * level + 1 : 2 * level + 2, :]

    for step in range(BLOCKS):

        @pl.when(s == step)
        def _():
            wait_row(copies[step])

    u = dot_nn(a2_ref[...], w[s, :, 0:UP_W]) + bup_ref[0, 0]
    bell = 0.5 * (1.0 + lax.erf(u * root_half))
    z = (u * bell).astype(BF)
    z_ref[0] = z
    slope_ref[0] = bell + u * inv_root_two_pi * jnp.exp(-0.5 * u * u)
    y_ref[...] += dot_nt(z, w[s, :, UP_W:FFN_W])


def put_grad(near_ref, far_ref, value, first, width):
    for j in range(8):
        ref = near_ref if j % 2 == 0 else far_ref
        ref[j // 2, 0, :, first : first + width] = value[j * PIECE : (j + 1) * PIECE]


def feed_back_kernel(level, n_pieces, n_after, info_ref, g_ref, h1_ref, a2_ref, gain_ref, z_ref, slope_ref, *rest):
    pieces = rest[:n_pieces]
    near_ref, far_ref, bup_ref, dh1_ref, sums_ref, da2, gb_t, a2_t, w, sems = rest[n_pieces + n_after :]
    s = pl.program_id(0)
    copies = piece_copies(info_ref, pieces, D, w, sems)

    @pl.when(s == 0)
    def _():
        start_all(copies)
        da2[...] = jnp.zeros_like(da2)
        gb_t[...] = g_ref[...].T.astype(BF)
        a2_t[...] = a2_ref[...].T

    for step in range(BLOCKS):

        @pl.when(s == step)
        def _():
            wait_row(copies[step])

    gb = g_ref[...].astype(BF)
    put_grad(near_ref, far_ref, dot_nn(gb_t[...], z_ref[0]).astype(BF), UP_W, UP_W)
    du = dot_nn(gb, w[s, :, UP_W:FFN_W]) * slope_ref[0]
    bup_ref[0] = jnp.sum(du, axis=0, keepdims=True)
    dub = du.astype(BF)
    put_grad(near_ref, far_ref, dot_nn(a2_t[...], dub).astype(BF), 0, UP_W)
    da2[...] += dot_nt(dub, w[s, :, 0:UP_W])

    @pl.when(s == BLOCKS - 1)
    def _():
        g = g_ref[...]
        scaled, inverse = scaled_rows(h1_ref[...])
        below, grad_gain = norm_back(da2[...], scaled, inverse, gain_ref[2 * level + 1 : 2 * level + 2, :])
        dh1 = below + g
        dh1_ref[...] = dh1
        sums_ref[0:1, :] = grad_gain
        sums_ref[1:2, :] = jnp.sum(dh1, axis=0, keepdims=True)
        sums_ref[2:3, :] = jnp.sum(g, axis=0, keepdims=True)


def attend_back_kernel(
    seq, level, whole_order, n_pieces, n_after,
    info_ref, dh1_ref, x_ref, gain_ref, qkv_ref, lse_ref, oext_ref, sums_in, bup_in, *rest,
):
    pieces = rest[:n_pieces]
    *outs, below_ref, small_ref = rest[n_pieces + n_after : -6]
    dext, dmix, dqkv, dqx, w, sems = rest[-6:]
    copies = piece_copies(info_ref, pieces, 0, w, sems)
    start_all(copies)
    turn = info_ref[0]
    dh1 = dh1_ref[...]
    hb = dh1.astype(BF)
    hb_t = dh1.T.astype(BF)
    for s in range(BLOCKS):
        wait_row(copies[s])
        dext[block_of(turn, s)] = dot_nn(hb, w[s, :, 512:768]).astype(BF)
    for b in range(BLOCKS):
        dmix[:, b * OUT_W : (b + 1) * OUT_W] = dext[b, :, HD : HD + OUT_W]
    low_half = lax.broadcasted_iota(jnp.int32, (ROWS, 128), 1) < HD
    key_live = lax.broadcasted_iota(jnp.int32, (ROWS, ROWS), 0) < seq
    scale = HD ** (-0.5)
    for pair in range(HEADS // 2):
        q2 = qkv_ref[:, pair * 128 : (pair + 1) * 128]
        k2 = qkv_ref[:, D + pair * 128 : D + (pair + 1) * 128]
        v2 = qkv_ref[:, 2 * D + pair * 128 : 2 * D + (pair + 1) * 128]
        d2 = dmix[:, pair * 128 : (pair + 1) * 128]
        dq = jnp.zeros((ROWS, 128), F32)
        dk = jnp.zeros((ROWS, 128), F32)
        dv = jnp.zeros((ROWS, 128), F32)
        for half in range(2):
            head = 2 * pair + half
            live = low_half if half == 0 else jnp.logical_not(low_half)
            none = jnp.zeros_like(q2)
            qm = jnp.where(live, q2, none)
            km = jnp.where(live, k2, none)
            dm = jnp.where(live, d2, none)
            st = jnp.where(key_live, dot_nt(k2, qm) * scale, -1e30)
            probs = jnp.exp(st - lse_ref[head : head + 1, :])
            dprobs = dot_nt(v2, dm)
            inner = jnp.sum(probs * dprobs, axis=0, keepdims=True)
            dst = (probs * (dprobs - inner) * scale).astype(BF)
            dv = dv + dot_nn(probs.astype(BF), dm)
            dk = dk + dot_nn(dst, qm)
            dq = dq + dot_tn(dst, km)
        dqkv[:, pair * 128 : (pair + 1) * 128] = dq.astype(BF)
        dqkv[:, D + pair * 128 : D + (pair + 1) * 128] = dk.astype(BF)
        dqkv[:, 2 * D + pair * 128 : 2 * D + (pair + 1) * 128] = dv.astype(BF)
    for b in range(BLOCKS):
        dqx[b, :, 0:QKV_W] = dqkv[:, b * QKV_W : (b + 1) * QKV_W]
        dqx[b, :, QKV_W:640] = jnp.zeros((ROWS, 640 - QKV_W), BF)
    gain = gain_ref[2 * level : 2 * level + 1, :]
    scaled, inverse = scaled_rows(x_ref[...])
    a1_t = (scaled * gain).T.astype(BF)
    da1 = jnp.zeros((ROWS, D), F32)
    for s in range(BLOCKS):
        own = block_of(turn, s)
        part = dqx[own]
        da1 = da1 + dot_nt(part, w[s, :, 0:640])
        first = dot_nn(a1_t, part)
        second = dot_nn(hb_t, oext_ref[own])
        for j in range(8):
            rows = slice(j * PIECE, (j + 1) * PIECE)
            if whole_order:
                ref = outs[0].at[own, jnp.bitwise_xor(info_ref[1], j)]
            else:
                ref = outs[j % 2].at[j // 2, s]
            ref[:, 0:512] = first[rows, 0:512].astype(BF)
            ref[:, 512:640] = (first[rows, 512:640] + second[rows, 0:128]).astype(BF)
            ref[:, 640:768] = second[rows, 128:256].astype(BF)
    below, grad_gain = norm_back(da1, scaled, inverse, gain)
    below = below + dh1
    if level == 0:
        below_ref[0] = flip_features(below, info_ref[1])[0:seq]
    else:
        below_ref[...] = below
    small_ref[0:1, :] = grad_gain
    small_ref[1:4, :] = sums_in[0:3, :]
    small_ref[4:8, :] = jnp.zeros((4, D), F32)
    small_ref[...] = flip_features(small_ref[...], info_ref[1])
    for s in range(BLOCKS):
        small_ref[pl.ds(4 + block_of(turn, s), 1), :] = bup_in[s]


VM = pl.BlockSpec(memory_space=pltpu.VMEM)
SM = pl.BlockSpec(memory_space=pltpu.SMEM)
HB = pl.BlockSpec(memory_space=pl.ANY)
LIMIT = 60 * 1024 * 1024


def sds(shape, dtype):
    return jax.ShapeDtypeStruct(shape, dtype)


def params():
    return pltpu.CompilerParams(vmem_limit_bytes=LIMIT)


def cost(flops, traffic):
    return pl.CostEstimate(flops=flops, bytes_accessed=traffic, transcendentals=0)


def weight_scratch(width):
    return [pltpu.VMEM((BLOCKS, D, width), BF), pltpu.SemaphoreType.DMA((BLOCKS, 16))]


def prepare(seq, info, counts, images, cotangent, gains, biases, bup):
    return pl.pallas_call(
        functools.partial(prepare_kernel, seq),
        out_shape=(
            sds((ROWS, D), F32), sds((ROWS, D), F32), sds(gains.shape, F32), sds(biases.shape, F32),
            sds((LAYERS, BLOCKS, 1, UP_W), F32),
        ),
        in_specs=[SM, SM] + [VM] * 5,
        out_specs=[VM] * 5,
        compiler_params=params(),
        cost_estimate=cost(10**7, 10**5),
        name="prepare",
    )(info, counts, images, cotangent, gains, biases, bup)


def finish(seq, info, counts, y, after):
    return pl.pallas_call(
        functools.partial(finish_kernel, seq, len(after)),
        out_shape=sds((1, seq, D), F32),
        in_specs=[SM, SM, VM] + [HB] * len(after),
        out_specs=VM,
        compiler_params=params(),
        cost_estimate=cost(10**7, 10**5),
        name="finish",
    )(info, counts, y, *after)


def attend(seq, level, info, x, gains, biases, pieces):
    return pl.pallas_call(
        functools.partial(attend_kernel, seq, level, len(pieces)),
        out_shape=(
            sds((ROWS, 3 * D), BF), sds((16, ROWS), F32), sds((BLOCKS, ROWS, 256), BF),
            sds((ROWS, D), F32), sds((ROWS, D), BF),
        ),
        in_specs=[SM] + [VM] * 3 + [HB] * len(pieces),
        out_specs=[VM] * 5,
        scratch_shapes=[pltpu.VMEM((BLOCKS, ROWS, 640), BF)] + weight_scratch(D),
        compiler_params=params(),
        cost_estimate=cost(10**7, 10**5),
        name="attend",
    )(info, x, gains, biases, *pieces)


def whole(shape):
    return pl.BlockSpec(shape, lambda s: (0,) * len(shape))


def feed(level, info, h1, a2, biases, bup, pieces):
    return pl.pallas_call(
        functools.partial(feed_kernel, level, len(pieces)),
        grid=(BLOCKS,),
        out_shape=(sds((BLOCKS, ROWS, UP_W), BF), sds((BLOCKS, ROWS, UP_W), F32), sds((ROWS, D), F32)),
        in_specs=[
            SM, whole((ROWS, D)), whole((ROWS, D)), whole(biases.shape),
            pl.BlockSpec((1, 1, 1, UP_W), lambda s: (level, s, 0, 0)),
        ]
        + [HB] * len(pieces),
        out_specs=[
            pl.BlockSpec((1, ROWS, UP_W), lambda s: (s, 0, 0)),
            pl.BlockSpec((1, ROWS, UP_W), lambda s: (s, 0, 0)),
            whole((ROWS, D)),
        ],
        scratch_shapes=weight_scratch(FFN_W),
        compiler_params=params(),
        cost_estimate=cost(10**7, 10**5),
        name="feed",
    )(info, h1, a2, biases, bup, *pieces)


def feed_back(level, info, g, h1, a2, gains, z, slope, pieces, after):
    grad = sds((4, BLOCKS, PIECE, FFN_W), BF)
    grad_spec = pl.BlockSpec((4, 1, PIECE, FFN_W), lambda s: (0, s, 0, 0))
    step_spec = pl.BlockSpec((1, ROWS, UP_W), lambda s: (s, 0, 0))
    return pl.pallas_call(
        functools.partial(feed_back_kernel, level, len(pieces), len(after)),
        grid=(BLOCKS,),
        out_shape=(grad, grad, sds((BLOCKS, 1, UP_W), F32), sds((ROWS, D), F32), sds((8, D), F32)),
        in_specs=[SM, whole((ROWS, D)), whole((ROWS, D)), whole((ROWS, D)), whole(gains.shape), step_spec, step_spec]
        + [HB] * (len(pieces) + len(after)),
        out_specs=[
            grad_spec, grad_spec,
            pl.BlockSpec((1, 1, UP_W), lambda s: (s, 0, 0)), whole((ROWS, D)), whole((8, D)),
        ],
        scratch_shapes=[pltpu.VMEM((ROWS, D), F32), pltpu.VMEM((D, ROWS), BF), pltpu.VMEM((D, ROWS), BF)]
        + weight_scratch(FFN_W),
        compiler_params=params(),
        cost_estimate=cost(10**7, 10**5),
        name="feed_back",
    )(info, g, h1, a2, gains, z, slope, *pieces, *after)


def attend_back(seq, level, whole_order, info, dh1, x, gains, qkv, lse, oext, sums, bup, pieces, after):
    grads = [sds((BLOCKS, 8, PIECE, D), BF)] if whole_order else [sds((4, BLOCKS, PIECE, D), BF)] * 2
    below = sds((1, seq, D), F32) if level == 0 else sds((ROWS, D), F32)
    return pl.pallas_call(
        functools.partial(attend_back_kernel, seq, level, whole_order, len(pieces), len(after)),
        out_shape=(*grads, below, sds((8, D), F32)),
        in_specs=[SM] + [VM] * 8 + [HB] * (len(pieces) + len(after)),
        out_specs=[VM] * (len(grads) + 2),
        scratch_shapes=[
            pltpu.VMEM((BLOCKS, ROWS, 256), BF), pltpu.VMEM((ROWS, D), BF),
            pltpu.VMEM((ROWS, 3 * D), BF), pltpu.VMEM((BLOCKS, ROWS, 640), BF),
        ]
        + weight_scratch(D),
        compiler_params=params(),
        cost_estimate=cost(10**7, 10**5),
        name="attend_back",
    )(info, dh1, x, gains, qkv, lse, oext, sums, bup, *pieces, *after)


def adamw_step(param, gradient, first_moment, second_moment):
    fresh_first = beta_one * first_moment + (1.0 - beta_one) * gradient
    fresh_second = beta_two * second_moment + (1.0 - beta_two) * gradient * gradient
    first_hat = fresh_first / (1.0 - beta_one**STEP)
    second_hat = fresh_second / (1.0 - beta_two**STEP)
    updated = param - learn_rate * (
        first_hat / (jnp.sqrt(second_hat) + adam_eps) + decay_rate * param
    )
    return (updated, fresh_first, fresh_second)


def after(value, *earlier):
    return lax.optimization_barrier((value,) + earlier)[0]


class PlainPlan:
    def __init__(self, mesh):
        self.n_row = mesh.shape["row"]
        self.n_col = mesh.shape["col"]
        self.turn = jnp.int32(0)
        self.mask = jnp.int32(0)

    def gather(self, shard, widths):
        full = lax.all_gather(shard, ("col", "row"), axis=0, tiled=True)
        full = full.reshape(self.n_col, D, sum(widths))
        parts = []
        start = 0
        for width in widths:
            part = full[:, :, start : start + width].transpose(1, 0, 2)
            parts.append(part.reshape(D, BLOCKS, -1).transpose(1, 0, 2))
            start += width
        return jnp.concatenate(parts, axis=2).reshape(BLOCKS, 8, PIECE, -1)

    def reduce(self, near, far, widths, *earlier):
        done = self.scatter(jnp.stack([near, far], axis=1).transpose(2, 0, 1, 3, 4), widths)
        for _ in range(2):
            yield done
        yield done, done
        yield done
        yield done

    def scatter(self, full, widths):
        full = full.reshape(BLOCKS, D, -1).transpose(1, 0, 2)
        parts = []
        start = 0
        for width in widths:
            wide = width * self.n_col // BLOCKS
            part = full[:, :, start : start + wide].reshape(D, self.n_col, width)
            parts.append(part.transpose(1, 0, 2))
            start += wide
        packed = jnp.concatenate(parts, axis=2).reshape(self.n_col * D, sum(widths))
        return lax.psum_scatter(packed, ("col", "row"), scatter_dimension=0, tiled=True).astype(F32)

    def total(self, values, stages):
        return lax.psum(values, ("row", "col"))


def flip_row(x, mask):
    return lax.ppermute(x, "row", [(i, i ^ mask) for i in range(8)])


def flip_col(x, mask):
    return lax.ppermute(x, "col", [(i, i ^ mask) for i in range(4)])


CORE, NEXT_X, NEXT_Y = 1, 2, 4


class RelativeFetch:
    def __init__(self, shard):
        self.shard = shard

    def turn_one(self, *hold):
        shard = after(self.shard, *hold)
        self.pair = jnp.stack([shard, flip_col(shard, 1)])
        return self.pair[1]

    def turn_two(self, *hold):
        self.others = flip_col(after(self.pair, *hold), 2)
        return self.others

    def plane(self, *hold):
        self.own = after(jnp.concatenate([self.pair, self.others], axis=0), *hold)
        self.from_x = flip_row(self.own, NEXT_X)
        self.from_y = flip_row(self.own, NEXT_Y)
        return self.from_x

    def rest(self, *hold):
        from_x, from_y = after(self.from_x, self.from_y, *hold), after(self.from_y, self.from_x, *hold)
        diag_low = flip_row(from_y[0:2], NEXT_X)
        diag_high = flip_row(from_x[2:4], NEXT_Y)
        near = jnp.concatenate([self.own, from_x, from_y, diag_low, diag_high], axis=0)
        near = near.reshape((4, BLOCKS) + self.shard.shape)
        return [near, flip_row(near, CORE)]


class RelativePlan:
    def __init__(self, mesh):
        self.turn = lax.axis_index("col").astype(jnp.int32)
        self.mask = lax.axis_index("row").astype(jnp.int32)

    def gather(self, shard, widths):
        full = lax.all_gather(shard, ("col", "row"), axis=0, tiled=True)
        return full.reshape(BLOCKS, 8, PIECE, -1)

    def scatter(self, full, widths):
        full = full.reshape(BLOCKS * D, -1)
        return lax.psum_scatter(full, ("col", "row"), scatter_dimension=0, tiled=True).astype(F32)

    def reduce(self, near, far, widths, *earlier):
        far = after(far, *earlier)
        other = flip_row(far, CORE)
        hold = yield other
        other = after(other, *hold)

        def joined(m, blocks):
            return near[m, blocks].astype(F32) + other[m, blocks].astype(F32)

        low, high, every = slice(0, 2), slice(2, 4), slice(0, 4)
        diag_low = flip_row(after(joined(3, low).astype(BF), *hold), NEXT_X)
        diag_high = flip_row(after(joined(3, high).astype(BF), *hold), NEXT_Y)
        hold = yield diag_low, diag_high
        to_x = jnp.concatenate([joined(1, low), joined(1, high) + diag_high.astype(F32)], axis=0)
        to_y = jnp.concatenate([joined(2, low) + diag_low.astype(F32), joined(2, high)], axis=0)
        from_x = flip_row(after(to_x.astype(BF), *hold), NEXT_X)
        from_y = flip_row(after(to_y.astype(BF), *hold), NEXT_Y)
        hold = yield from_x, from_y
        from_x, from_y = after(from_x, from_y, *hold), after(from_y, from_x, *hold)
        plane = joined(0, every) + from_x.astype(F32) + from_y.astype(F32)
        others = flip_col(plane[2:4].astype(BF), 2)
        hold = yield others
        pair = plane[0:2] + after(others, *hold).astype(F32)
        yield pair[0] + flip_col(pair[1].astype(BF), 1).astype(F32)

    def total(self, values, stages):
        hops = [(flip_row, CORE), (flip_row, NEXT_X), (flip_row, NEXT_Y), (flip_col, 1), (flip_col, 2)]
        for (flip, mask), stage in zip(hops, stages):
            values = values + after(flip(values, mask), *stage)
        return values


def per_device(
    mesh,
    images, cotangent, counts, w_qkv, w_out, w_up, w_down, norm_gains, res_biases, b_up,
    m_qkv, m_out, m_up, m_down, m_gains, m_biases, m_bup,
    v_qkv, v_out, v_up, v_down, v_gains, v_biases, v_bup,
):
    seq = images.shape[1]
    relative = mesh.shape["row"] == 8 and mesh.shape["col"] == 4
    plan = RelativePlan(mesh) if relative else PlainPlan(mesh)
    info = jnp.stack([plan.turn, plan.mask, lax.axis_index("col"), lax.axis_index("row")]).astype(jnp.int32)
    att_widths = (w_qkv.shape[2], w_out.shape[1])
    ffn_widths = (w_up.shape[2], w_down.shape[1])
    shards = []
    for level in range(LAYERS):
        shards.append([
            jnp.concatenate([w_qkv[level].astype(BF), w_out[level].T.astype(BF)], axis=1),
            w_up[level].astype(BF),
            w_down[level].T.astype(BF),
        ])

    hidden, upstream, gains, biases, bup = prepare(
        seq, info, counts, images, cotangent,
        norm_gains.reshape(2 * LAYERS, D), res_biases.reshape(2 * LAYERS, D),
        b_up.reshape(LAYERS * BLOCKS, 1, UP_W),
    )
    saved, att_full, ffn_full = [], [], []

    def forward_attend(level, hidden, pieces):
        att_full.append(pieces)
        return attend(seq, level, info, hidden, gains, biases, pieces)

    def forward_feed(level, hidden, state, pieces):
        qkv, lse, oext, h1, a2 = state
        ffn_full.append(pieces)
        z, slope, y = feed(level, info, h1, a2, biases, bup, pieces)
        saved.append((hidden, qkv, lse, oext, h1, a2, z, slope))
        return y

    def gathered(level):
        return [plan.gather(jnp.concatenate(shards[level], axis=1), att_widths + ffn_widths)]

    later = gathered(1)
    if relative:
        fetches = [RelativeFetch(shard) for shard in shards[0]]
        one = fetches[0].turn_one()
        two = fetches[0].turn_two()
        plane, ran, arrived = (), (), []
        for index, fetch in enumerate(fetches):
            plane = (fetch.plane(*plane),)
            if index + 1 < len(fetches):
                one = fetches[index + 1].turn_one(one)
                two = fetches[index + 1].turn_two(two)
            if index == 2:
                state = forward_attend(0, hidden, arrived[0])
                ran = (state[1],)
            arrived.append(fetch.rest(two, *ran))
            ran = (gains,)
        sooner = arrived[1] + arrived[2]
    else:
        sooner = gathered(0)
        state = forward_attend(0, hidden, sooner)
    middle = forward_feed(0, hidden, state, sooner)
    state = forward_attend(1, middle, later)
    hidden = forward_feed(1, middle, state, later)
    smalls = [None] * LAYERS

    def backward_feed(level, upstream, landed):
        below, qkv, lse, oext, h1, a2, z, slope = saved[level]
        return feed_back(level, info, upstream, h1, a2, gains, z, slope, ffn_full[level], landed)

    def backward_attend(level, dh1, sums, bup_sum, landed):
        below, qkv, lse, oext, h1, a2, z, slope = saved[level]
        return attend_back(
            seq, level, level == 1, info, dh1, below, gains, qkv, lse, oext, sums, bup_sum, att_full[level], landed
        )

    done = {}
    near, far, bup_sum, dh1, sums = backward_feed(1, upstream, [])
    ffn_one = plan.reduce(near, far, ffn_widths)
    core_one = next(ffn_one)
    whole_one, upstream, smalls[1] = backward_attend(1, dh1, sums, bup_sum, [])
    done["att", 1] = plan.scatter(whole_one, att_widths)
    diag_one = ffn_one.send(())
    near, far, bup_sum, dh1, sums = backward_feed(0, upstream, [*diag_one])
    plane_one = ffn_one.send(())
    ffn_zero = plan.reduce(near, far, ffn_widths)
    core_zero = next(ffn_zero)
    near, far, upstream, smalls[0] = backward_attend(0, dh1, sums, bup_sum, [])
    att_zero = plan.reduce(near, far, att_widths, core_zero)
    core_last = next(att_zero)
    diag_zero = ffn_zero.send((smalls[0],))
    plane_zero = ffn_zero.send(())
    diag_last = att_zero.send(diag_zero)
    plane_last = att_zero.send(())
    turn_one, turn_zero, turn_last = ffn_one.send((smalls[0],)), ffn_zero.send(diag_last), att_zero.send(())
    done["ffn", 1], done["ffn", 0], done["att", 0] = ffn_one.send(diag_zero), ffn_zero.send(plane_last), att_zero.send(())
    layer_out = finish(seq, info, counts, hidden, [upstream])
    grads = []
    for level in range(LAYERS):
        ffn, att = done["ffn", level], done["att", level]
        grads.append((
            att[:, : att_widths[0]], att[:, att_widths[0] :].T, ffn[:, : ffn_widths[0]], ffn[:, ffn_widths[0] :].T
        ))
    stages = [diag_zero, diag_zero, plane_zero, plane_zero, diag_last]
    small = plan.total(jnp.concatenate(smalls, axis=0), stages).reshape(LAYERS, 8, D)
    grad_list = [jnp.stack([grads[level][index] for level in range(LAYERS)]) for index in range(4)]
    grad_list += [small[:, 0:2], small[:, 2:4], small[:, 4:8].reshape(LAYERS, FF)]
    params_in = [w_qkv, w_out, w_up, w_down, norm_gains, res_biases, b_up]
    firsts = [m_qkv, m_out, m_up, m_down, m_gains, m_biases, m_bup]
    seconds = [v_qkv, v_out, v_up, v_down, v_gains, v_biases, v_bup]
    results = [
        adamw_step(params_in[index], grad_list[index], firsts[index], seconds[index])
        for index in range(7)
    ]
    return (
        (layer_out, upstream)
        + tuple(grad_list)
        + tuple(result[0] for result in results[:4])
        + tuple(result[1] for result in results)
        + tuple(result[2] for result in results)
    )


def solution(mesh):
    tokens = P(("row", "col"), None, None)
    matrices = (P(None, "row", "col"), P(None, "col", "row"), P(None, "row", "col"), P(None, "col", "row"))
    vectors = (P(), P(), P())
    in_specs = (tokens, tokens, P()) + (matrices + vectors) * 3
    out_specs = (tokens, tokens) + matrices + vectors + matrices + (matrices + vectors) * 2
    return jax.shard_map(
        functools.partial(per_device, mesh), mesh=mesh, in_specs=in_specs, out_specs=out_specs, check_vma=False
    )
```

```python
import functools

import jax
import jax.numpy as jnp
from jax import lax
from jax.experimental import pallas as pl
from jax.experimental.pallas import tpu as pltpu
from jax.sharding import PartitionSpec as P

HEADS = 12
LAYERS = 2
STEP = 3
D = 768
FF = 3072
HD = 64
BLOCKS = 4
ROWS = 208
QKV_W = 3 * D // BLOCKS
OUT_W = D // BLOCKS
UP_W = FF // BLOCKS
PIECE = 96

norm_eps = 1e-06
root_half = 0.7071067811865476
inv_root_two_pi = 0.3989422804014327
beta_one = 0.9
beta_two = 0.999
adam_eps = 1e-08
learn_rate = 0.06
decay_rate = 0.05

BF = jnp.bfloat16
F32 = jnp.float32


def dot_nn(a, b):
    return lax.dot_general(a, b, (((1,), (0,)), ((), ())), preferred_element_type=F32)


def dot_nt(a, b):
    return lax.dot_general(a, b, (((1,), (1,)), ((), ())), preferred_element_type=F32)


def dot_tn(a, b):
    return lax.dot_general(a, b, (((0,), (0,)), ((), ())), preferred_element_type=F32)


def scaled_rows(x):
    center = jnp.mean(x, axis=-1, keepdims=True)
    shifted = x - center
    inverse = lax.rsqrt(jnp.mean(shifted * shifted, axis=-1, keepdims=True) + norm_eps)
    return shifted * inverse, inverse


def norm_back(upstream, scaled, inverse, gain):
    grad_scaled = upstream * gain
    mean_one = jnp.mean(grad_scaled, axis=-1, keepdims=True)
    mean_two = jnp.mean(grad_scaled * scaled, axis=-1, keepdims=True)
    grad_gain = jnp.sum(upstream * scaled, axis=0, keepdims=True)
    return inverse * (grad_scaled - mean_one - scaled * mean_two), grad_gain


def block_of(turn, s):
    return jnp.bitwise_xor(turn, s)


FFN_W = 2 * UP_W


def piece_copies(info_ref, refs, column, w, sems):
    copies = []
    for s in range(BLOCKS):
        row = []
        for index, ref in enumerate(refs):
            for part in range(8 if ref.shape[1] == 8 else 4):
                if ref.shape[1] == 8:
                    block = part
                    lanes = slice(0, w.shape[2])
                    source = ref.at[
                        block_of(info_ref[0], s), jnp.bitwise_xor(info_ref[1], part), :,
                        column : column + w.shape[2],
                    ]
                else:
                    block = 2 * part + index % 2
                    lanes = slice(index // 2 * D, (index // 2 + 1) * D)
                    source = ref.at[part, s]
                target = w.at[s, block * PIECE : (block + 1) * PIECE, lanes]
                row.append(pltpu.make_async_copy(source, target, sems.at[s, len(row)]))
        copies.append(row)
    return copies


def start_all(copies):
    for row in copies:
        for copy in row:
            copy.start()


def wait_row(row):
    for copy in row:
        copy.wait()


def flip_features(x, mask):
    place = lax.broadcasted_iota(jnp.int32, x.shape, 1)
    block = jnp.zeros(x.shape, jnp.int32)
    for edge in range(1, D // PIECE):
        block = block + (place >= edge * PIECE).astype(jnp.int32)
    for bit in range(3):
        size = PIECE << bit
        even = ((block >> bit) & 1) == 0
        swapped = jnp.where(even, pltpu.roll(x, D - size, axis=1), pltpu.roll(x, size, axis=1))
        x = jnp.where(jnp.full(x.shape, (mask >> bit) & 1, jnp.int32) == 1, swapped, x)
    return x


def prepare_kernel(
    seq, info_ref, counts_ref, images_ref, cot_ref, gains_ref, biases_ref, bup_ref,
    x_ref, g_ref, gains_out, biases_out, bup_out,
):
    mask = info_ref[1]
    live = (info_ref[2] < counts_ref[info_ref[3]]).astype(F32)
    x_ref[ROWS - 16 : ROWS, :] = jnp.zeros((16, D), F32)
    g_ref[ROWS - 16 : ROWS, :] = jnp.zeros((16, D), F32)
    x_ref[0:seq, :] = flip_features(images_ref[0], mask)
    g_ref[0:seq, :] = flip_features(cot_ref[0], mask) * live
    gains_out[...] = flip_features(gains_ref[...], mask)
    biases_out[...] = flip_features(biases_ref[...], mask)
    for level in range(LAYERS):
        for s in range(BLOCKS):
            bup_out[level, s] = bup_ref[level * BLOCKS + block_of(info_ref[0], s)]


def finish_kernel(seq, extra, info_ref, counts_ref, y_ref, *rest):
    out_ref = rest[extra]
    live = (info_ref[2] < counts_ref[info_ref[3]]).astype(F32)
    out_ref[0] = flip_features(y_ref[...], info_ref[1])[0:seq] * live


def attend_kernel(seq, level, n_pieces, info_ref, x_ref, gain_ref, bias_ref, *rest):
    pieces = rest[:n_pieces]
    qkv_ref, lse_ref, oext_ref, h1_ref, a2_ref, blk, w, sems = rest[n_pieces:]
    copies = piece_copies(info_ref, pieces, 0, w, sems)
    start_all(copies)
    turn = info_ref[0]
    x = x_ref[...]
    scaled, _ = scaled_rows(x)
    a1 = (scaled * gain_ref[2 * level : 2 * level + 1, :]).astype(BF)
    for s in range(BLOCKS):
        wait_row(copies[s])
        t = dot_nn(a1, w[s, :, 0:640])
        blk[block_of(turn, s)] = t.astype(BF)
    for b in range(BLOCKS):
        qkv_ref[:, b * QKV_W : (b + 1) * QKV_W] = blk[b, :, 0:QKV_W]
    low_half = lax.broadcasted_iota(jnp.int32, (ROWS, 128), 1) < HD
    key_live = lax.broadcasted_iota(jnp.int32, (ROWS, ROWS), 0) < seq
    scale = HD ** (-0.5)
    oext_ref[:, :, 0:HD] = jnp.zeros((BLOCKS, ROWS, HD), BF)
    for pair in range(HEADS // 2):
        q2 = qkv_ref[:, pair * 128 : (pair + 1) * 128]
        k2 = qkv_ref[:, D + pair * 128 : D + (pair + 1) * 128]
        v2 = qkv_ref[:, 2 * D + pair * 128 : 2 * D + (pair + 1) * 128]
        mixed = []
        for half in range(2):
            live = low_half if half == 0 else jnp.logical_not(low_half)
            qm = jnp.where(live, q2, jnp.zeros_like(q2))
            st = jnp.where(key_live, dot_nt(k2, qm) * scale, -1e30)
            peak = jnp.max(st, axis=0, keepdims=True)
            grown = jnp.exp(st - peak)
            total = jnp.sum(grown, axis=0, keepdims=True)
            head = 2 * pair + half
            lse_ref[head : head + 1, :] = peak + jnp.log(total)
            probs = (grown * (1.0 / total)).astype(BF)
            mixed.append(dot_tn(probs, v2))
        both = jnp.where(low_half, mixed[0], mixed[1]).astype(BF)
        for half in range(2):
            head = 2 * pair + half
            lane = HD + (head % 3) * HD
            oext_ref[head // 3, :, lane : lane + HD] = both[:, half * HD : (half + 1) * HD]
    total = x + bias_ref[2 * level : 2 * level + 1, :]
    for s in range(BLOCKS):
        total = total + dot_nt(oext_ref[block_of(turn, s)], w[s, :, 512:768])
    h1_ref[...] = total
    scaled2, _ = scaled_rows(total)
    a2_ref[...] = (scaled2 * gain_ref[2 * level + 1 : 2 * level + 2, :]).astype(BF)


def feed_kernel(level, n_pieces, info_ref, h1_ref, a2_ref, bias_ref, bup_ref, *rest):
    pieces = rest[:n_pieces]
    z_ref, slope_ref, y_ref, w, sems = rest[n_pieces:]
    s = pl.program_id(0)
    copies = piece_copies(info_ref, pieces, D, w, sems)

    @pl.when(s == 0)
    def _():
        start_all(copies)
        y_ref[...] = h1_ref[...] + bias_ref[2 * level + 1 : 2 * level + 2, :]

    for step in range(BLOCKS):

        @pl.when(s == step)
        def _():
            wait_row(copies[step])

    u = dot_nn(a2_ref[...], w[s, :, 0:UP_W]) + bup_ref[0, 0]
    bell = 0.5 * (1.0 + lax.erf(u * root_half))
    z = (u * bell).astype(BF)
    z_ref[0] = z
    slope_ref[0] = bell + u * inv_root_two_pi * jnp.exp(-0.5 * u * u)
    y_ref[...] += dot_nt(z, w[s, :, UP_W:FFN_W])


def put_grad(near_ref, far_ref, value, first, width):
    for j in range(8):
        ref = near_ref if j % 2 == 0 else far_ref
        ref[j // 2, 0, :, first : first + width] = value[j * PIECE : (j + 1) * PIECE]


def feed_back_kernel(level, n_pieces, n_after, info_ref, g_ref, h1_ref, a2_ref, gain_ref, z_ref, slope_ref, *rest):
    pieces = rest[:n_pieces]
    near_ref, far_ref, bup_ref, dh1_ref, sums_ref, da2, gb_t, a2_t, w, sems = rest[n_pieces + n_after :]
    s = pl.program_id(0)
    copies = piece_copies(info_ref, pieces, D, w, sems)

    @pl.when(s == 0)
    def _():
        start_all(copies)
        da2[...] = jnp.zeros_like(da2)
        gb_t[...] = g_ref[...].T.astype(BF)
        a2_t[...] = a2_ref[...].T

    for step in range(BLOCKS):

        @pl.when(s == step)
        def _():
            wait_row(copies[step])

    gb = g_ref[...].astype(BF)
    put_grad(near_ref, far_ref, dot_nn(gb_t[...], z_ref[0]).astype(BF), UP_W, UP_W)
    du = dot_nn(gb, w[s, :, UP_W:FFN_W]) * slope_ref[0]
    bup_ref[0] = jnp.sum(du, axis=0, keepdims=True)
    dub = du.astype(BF)
    put_grad(near_ref, far_ref, dot_nn(a2_t[...], dub).astype(BF), 0, UP_W)
    da2[...] += dot_nt(dub, w[s, :, 0:UP_W])

    @pl.when(s == BLOCKS - 1)
    def _():
        g = g_ref[...]
        scaled, inverse = scaled_rows(h1_ref[...])
        below, grad_gain = norm_back(da2[...], scaled, inverse, gain_ref[2 * level + 1 : 2 * level + 2, :])
        dh1 = below + g
        dh1_ref[...] = dh1
        sums_ref[0:1, :] = grad_gain
        sums_ref[1:2, :] = jnp.sum(dh1, axis=0, keepdims=True)
        sums_ref[2:3, :] = jnp.sum(g, axis=0, keepdims=True)


def attend_back_kernel(
    seq, level, whole_order, n_pieces, n_after,
    info_ref, dh1_ref, x_ref, gain_ref, qkv_ref, lse_ref, oext_ref, sums_in, bup_in, *rest,
):
    pieces = rest[:n_pieces]
    *outs, below_ref, small_ref = rest[n_pieces + n_after : -6]
    dext, dmix, dqkv, dqx, w, sems = rest[-6:]
    copies = piece_copies(info_ref, pieces, 0, w, sems)
    start_all(copies)
    turn = info_ref[0]
    dh1 = dh1_ref[...]
    hb = dh1.astype(BF)
    hb_t = dh1.T.astype(BF)
    for s in range(BLOCKS):
        wait_row(copies[s])
        dext[block_of(turn, s)] = dot_nn(hb, w[s, :, 512:768]).astype(BF)
    for b in range(BLOCKS):
        dmix[:, b * OUT_W : (b + 1) * OUT_W] = dext[b, :, HD : HD + OUT_W]
    low_half = lax.broadcasted_iota(jnp.int32, (ROWS, 128), 1) < HD
    key_live = lax.broadcasted_iota(jnp.int32, (ROWS, ROWS), 0) < seq
    scale = HD ** (-0.5)
    for pair in range(HEADS // 2):
        q2 = qkv_ref[:, pair * 128 : (pair + 1) * 128]
        k2 = qkv_ref[:, D + pair * 128 : D + (pair + 1) * 128]
        v2 = qkv_ref[:, 2 * D + pair * 128 : 2 * D + (pair + 1) * 128]
        d2 = dmix[:, pair * 128 : (pair + 1) * 128]
        dq = jnp.zeros((ROWS, 128), F32)
        dk = jnp.zeros((ROWS, 128), F32)
        dv = jnp.zeros((ROWS, 128), F32)
        for half in range(2):
            head = 2 * pair + half
            live = low_half if half == 0 else jnp.logical_not(low_half)
            none = jnp.zeros_like(q2)
            qm = jnp.where(live, q2, none)
            km = jnp.where(live, k2, none)
            dm = jnp.where(live, d2, none)
            st = jnp.where(key_live, dot_nt(k2, qm) * scale, -1e30)
            probs = jnp.exp(st - lse_ref[head : head + 1, :])
            dprobs = dot_nt(v2, dm)
            inner = jnp.sum(probs * dprobs, axis=0, keepdims=True)
            dst = (probs * (dprobs - inner) * scale).astype(BF)
            dv = dv + dot_nn(probs.astype(BF), dm)
            dk = dk + dot_nn(dst, qm)
            dq = dq + dot_tn(dst, km)
        dqkv[:, pair * 128 : (pair + 1) * 128] = dq.astype(BF)
        dqkv[:, D + pair * 128 : D + (pair + 1) * 128] = dk.astype(BF)
        dqkv[:, 2 * D + pair * 128 : 2 * D + (pair + 1) * 128] = dv.astype(BF)
    for b in range(BLOCKS):
        dqx[b, :, 0:QKV_W] = dqkv[:, b * QKV_W : (b + 1) * QKV_W]
        dqx[b, :, QKV_W:640] = jnp.zeros((ROWS, 640 - QKV_W), BF)
    gain = gain_ref[2 * level : 2 * level + 1, :]
    scaled, inverse = scaled_rows(x_ref[...])
    a1_t = (scaled * gain).T.astype(BF)
    da1 = jnp.zeros((ROWS, D), F32)
    for s in range(BLOCKS):
        own = block_of(turn, s)
        part = dqx[own]
        da1 = da1 + dot_nt(part, w[s, :, 0:640])
        first = dot_nn(a1_t, part)
        second = dot_nn(hb_t, oext_ref[own])
        for j in range(8):
            rows = slice(j * PIECE, (j + 1) * PIECE)
            if whole_order:
                ref = outs[0].at[own, jnp.bitwise_xor(info_ref[1], j)]
            else:
                ref = outs[j % 2].at[j // 2, s]
            ref[:, 0:512] = first[rows, 0:512].astype(BF)
            ref[:, 512:640] = (first[rows, 512:640] + second[rows, 0:128]).astype(BF)
            ref[:, 640:768] = second[rows, 128:256].astype(BF)
    below, grad_gain = norm_back(da1, scaled, inverse, gain)
    below = below + dh1
    if level == 0:
        below_ref[0] = flip_features(below, info_ref[1])[0:seq]
    else:
        below_ref[...] = below
    small_ref[0:1, :] = grad_gain
    small_ref[1:4, :] = sums_in[0:3, :]
    small_ref[4:8, :] = jnp.zeros((4, D), F32)
    small_ref[...] = flip_features(small_ref[...], info_ref[1])
    for s in range(BLOCKS):
        small_ref[pl.ds(4 + block_of(turn, s), 1), :] = bup_in[s]


VM = pl.BlockSpec(memory_space=pltpu.VMEM)
SM = pl.BlockSpec(memory_space=pltpu.SMEM)
HB = pl.BlockSpec(memory_space=pl.ANY)
LIMIT = 60 * 1024 * 1024


def sds(shape, dtype):
    return jax.ShapeDtypeStruct(shape, dtype)


def params():
    return pltpu.CompilerParams(vmem_limit_bytes=LIMIT)


def cost(flops, traffic):
    return pl.CostEstimate(flops=flops, bytes_accessed=traffic, transcendentals=0)


def weight_scratch(width):
    return [pltpu.VMEM((BLOCKS, D, width), BF), pltpu.SemaphoreType.DMA((BLOCKS, 16))]


def prepare(seq, info, counts, images, cotangent, gains, biases, bup):
    return pl.pallas_call(
        functools.partial(prepare_kernel, seq),
        out_shape=(
            sds((ROWS, D), F32), sds((ROWS, D), F32), sds(gains.shape, F32), sds(biases.shape, F32),
            sds((LAYERS, BLOCKS, 1, UP_W), F32),
        ),
        in_specs=[SM, SM] + [VM] * 5,
        out_specs=[VM] * 5,
        compiler_params=params(),
        cost_estimate=cost(10**7, 10**5),
        name="prepare",
    )(info, counts, images, cotangent, gains, biases, bup)


def finish(seq, info, counts, y, after):
    return pl.pallas_call(
        functools.partial(finish_kernel, seq, len(after)),
        out_shape=sds((1, seq, D), F32),
        in_specs=[SM, SM, VM] + [HB] * len(after),
        out_specs=VM,
        compiler_params=params(),
        cost_estimate=cost(10**7, 10**5),
        name="finish",
    )(info, counts, y, *after)


def attend(seq, level, info, x, gains, biases, pieces):
    return pl.pallas_call(
        functools.partial(attend_kernel, seq, level, len(pieces)),
        out_shape=(
            sds((ROWS, 3 * D), BF), sds((16, ROWS), F32), sds((BLOCKS, ROWS, 256), BF),
            sds((ROWS, D), F32), sds((ROWS, D), BF),
        ),
        in_specs=[SM] + [VM] * 3 + [HB] * len(pieces),
        out_specs=[VM] * 5,
        scratch_shapes=[pltpu.VMEM((BLOCKS, ROWS, 640), BF)] + weight_scratch(D),
        compiler_params=params(),
        cost_estimate=cost(10**7, 10**5),
        name="attend",
    )(info, x, gains, biases, *pieces)


def whole(shape):
    return pl.BlockSpec(shape, lambda s: (0,) * len(shape))


def feed(level, info, h1, a2, biases, bup, pieces):
    return pl.pallas_call(
        functools.partial(feed_kernel, level, len(pieces)),
        grid=(BLOCKS,),
        out_shape=(sds((BLOCKS, ROWS, UP_W), BF), sds((BLOCKS, ROWS, UP_W), F32), sds((ROWS, D), F32)),
        in_specs=[
            SM, whole((ROWS, D)), whole((ROWS, D)), whole(biases.shape),
            pl.BlockSpec((1, 1, 1, UP_W), lambda s: (level, s, 0, 0)),
        ]
        + [HB] * len(pieces),
        out_specs=[
            pl.BlockSpec((1, ROWS, UP_W), lambda s: (s, 0, 0)),
            pl.BlockSpec((1, ROWS, UP_W), lambda s: (s, 0, 0)),
            whole((ROWS, D)),
        ],
        scratch_shapes=weight_scratch(FFN_W),
        compiler_params=params(),
        cost_estimate=cost(10**7, 10**5),
        name="feed",
    )(info, h1, a2, biases, bup, *pieces)


def feed_back(level, info, g, h1, a2, gains, z, slope, pieces, after):
    grad = sds((4, BLOCKS, PIECE, FFN_W), BF)
    grad_spec = pl.BlockSpec((4, 1, PIECE, FFN_W), lambda s: (0, s, 0, 0))
    step_spec = pl.BlockSpec((1, ROWS, UP_W), lambda s: (s, 0, 0))
    return pl.pallas_call(
        functools.partial(feed_back_kernel, level, len(pieces), len(after)),
        grid=(BLOCKS,),
        out_shape=(grad, grad, sds((BLOCKS, 1, UP_W), F32), sds((ROWS, D), F32), sds((8, D), F32)),
        in_specs=[SM, whole((ROWS, D)), whole((ROWS, D)), whole((ROWS, D)), whole(gains.shape), step_spec, step_spec]
        + [HB] * (len(pieces) + len(after)),
        out_specs=[
            grad_spec, grad_spec,
            pl.BlockSpec((1, 1, UP_W), lambda s: (s, 0, 0)), whole((ROWS, D)), whole((8, D)),
        ],
        scratch_shapes=[pltpu.VMEM((ROWS, D), F32), pltpu.VMEM((D, ROWS), BF), pltpu.VMEM((D, ROWS), BF)]
        + weight_scratch(FFN_W),
        compiler_params=params(),
        cost_estimate=cost(10**7, 10**5),
        name="feed_back",
    )(info, g, h1, a2, gains, z, slope, *pieces, *after)


def attend_back(seq, level, whole_order, info, dh1, x, gains, qkv, lse, oext, sums, bup, pieces, after):
    grads = [sds((BLOCKS, 8, PIECE, D), BF)] if whole_order else [sds((4, BLOCKS, PIECE, D), BF)] * 2
    below = sds((1, seq, D), F32) if level == 0 else sds((ROWS, D), F32)
    return pl.pallas_call(
        functools.partial(attend_back_kernel, seq, level, whole_order, len(pieces), len(after)),
        out_shape=(*grads, below, sds((8, D), F32)),
        in_specs=[SM] + [VM] * 8 + [HB] * (len(pieces) + len(after)),
        out_specs=[VM] * (len(grads) + 2),
        scratch_shapes=[
            pltpu.VMEM((BLOCKS, ROWS, 256), BF), pltpu.VMEM((ROWS, D), BF),
            pltpu.VMEM((ROWS, 3 * D), BF), pltpu.VMEM((BLOCKS, ROWS, 640), BF),
        ]
        + weight_scratch(D),
        compiler_params=params(),
        cost_estimate=cost(10**7, 10**5),
        name="attend_back",
    )(info, dh1, x, gains, qkv, lse, oext, sums, bup, *pieces, *after)


def adamw_step(param, gradient, first_moment, second_moment):
    fresh_first = beta_one * first_moment + (1.0 - beta_one) * gradient
    fresh_second = beta_two * second_moment + (1.0 - beta_two) * gradient * gradient
    first_hat = fresh_first / (1.0 - beta_one**STEP)
    second_hat = fresh_second / (1.0 - beta_two**STEP)
    updated = param - learn_rate * (
        first_hat / (jnp.sqrt(second_hat) + adam_eps) + decay_rate * param
    )
    return (updated, fresh_first, fresh_second)


def after(value, *earlier):
    return lax.optimization_barrier((value,) + earlier)[0]


class PlainPlan:
    def __init__(self, mesh):
        self.n_row = mesh.shape["row"]
        self.n_col = mesh.shape["col"]
        self.turn = jnp.int32(0)
        self.mask = jnp.int32(0)

    def gather(self, shard, widths):
        full = lax.all_gather(shard, ("col", "row"), axis=0, tiled=True)
        full = full.reshape(self.n_col, D, sum(widths))
        parts = []
        start = 0
        for width in widths:
            part = full[:, :, start : start + width].transpose(1, 0, 2)
            parts.append(part.reshape(D, BLOCKS, -1).transpose(1, 0, 2))
            start += width
        return jnp.concatenate(parts, axis=2).reshape(BLOCKS, 8, PIECE, -1)

    def reduce(self, near, far, widths, *earlier):
        done = self.scatter(jnp.stack([near, far], axis=1).transpose(2, 0, 1, 3, 4), widths)
        for _ in range(2):
            yield done
        yield done, done
        yield done
        yield done

    def scatter(self, full, widths):
        full = full.reshape(BLOCKS, D, -1).transpose(1, 0, 2)
        parts = []
        start = 0
        for width in widths:
            wide = width * self.n_col // BLOCKS
            part = full[:, :, start : start + wide].reshape(D, self.n_col, width)
            parts.append(part.transpose(1, 0, 2))
            start += wide
        packed = jnp.concatenate(parts, axis=2).reshape(self.n_col * D, sum(widths))
        return lax.psum_scatter(packed, ("col", "row"), scatter_dimension=0, tiled=True)

    def total(self, values, stages):
        return lax.psum(values, ("row", "col"))


def flip_row(x, mask):
    return lax.ppermute(x, "row", [(i, i ^ mask) for i in range(8)])


def flip_col(x, mask):
    return lax.ppermute(x, "col", [(i, i ^ mask) for i in range(4)])


CORE, NEXT_X, NEXT_Y = 1, 2, 4


def update_kernel(*refs):
    grads, inputs, outputs = refs[:LAYERS], refs[LAYERS : LAYERS + 6], refs[LAYERS + 6 :]
    cut = inputs[0].shape[2]
    for level in range(LAYERS):
        both = grads[level][...].astype(F32)
        for index in range(2):
            param, first, second = inputs[3 * index : 3 * index + 3]
            grad_out, param_out, first_out, second_out = outputs[4 * index : 4 * index + 4]
            gradient = both[:, cut:].T if index else both[:, :cut]
            grad_out[level] = gradient
            fresh = adamw_step(param[level], gradient, first[level], second[level])
            param_out[level], first_out[level], second_out[level] = fresh


def update_matrices(grads, first, second):
    return pl.pallas_call(
        update_kernel,
        out_shape=[sds(group[0].shape, F32) for group in (first, second) for _ in range(4)],
        in_specs=[VM] * (LAYERS + 6),
        out_specs=[VM] * 8,
        compiler_params=params(),
        cost_estimate=cost(10**7, 10**5),
        name="update",
    )(*grads, *first, *second)


class RelativeFetch:
    def __init__(self, shard):
        self.shard = shard

    def turn_one(self, *hold):
        shard = after(self.shard, *hold)
        self.pair = jnp.stack([shard, flip_col(shard, 1)])
        return self.pair[1]

    def turn_two(self, *hold):
        self.others = flip_col(after(self.pair, *hold), 2)
        return self.others

    def plane(self, *hold):
        self.own = after(jnp.concatenate([self.pair, self.others], axis=0), *hold)
        self.from_x = flip_row(self.own, NEXT_X)
        self.from_y = flip_row(self.own, NEXT_Y)
        return self.from_x

    def rest(self, *hold):
        from_x, from_y = after(self.from_x, self.from_y, *hold), after(self.from_y, self.from_x, *hold)
        diag_low = flip_row(from_y[0:2], NEXT_X)
        diag_high = flip_row(from_x[2:4], NEXT_Y)
        near = jnp.concatenate([self.own, from_x, from_y, diag_low, diag_high], axis=0)
        near = near.reshape((4, BLOCKS) + self.shard.shape)
        return [near, flip_row(near, CORE)]


class RelativePlan:
    def __init__(self, mesh):
        self.turn = lax.axis_index("col").astype(jnp.int32)
        self.mask = lax.axis_index("row").astype(jnp.int32)

    def gather(self, shard, widths):
        full = lax.all_gather(shard, ("col", "row"), axis=0, tiled=True)
        return full.reshape(BLOCKS, 8, PIECE, -1)

    def scatter(self, full, widths):
        full = full.reshape(BLOCKS * D, -1)
        return lax.psum_scatter(full, ("col", "row"), scatter_dimension=0, tiled=True)

    def reduce(self, near, far, widths, *earlier):
        far = after(far, *earlier)
        other = flip_row(far, CORE)
        hold = yield other
        other = after(other, *hold)

        def joined(m, blocks):
            return near[m, blocks].astype(F32) + other[m, blocks].astype(F32)

        low, high, every = slice(0, 2), slice(2, 4), slice(0, 4)
        diag_low = flip_row(after(joined(3, low).astype(BF), *hold), NEXT_X)
        diag_high = flip_row(after(joined(3, high).astype(BF), *hold), NEXT_Y)
        hold = yield diag_low, diag_high
        to_x = jnp.concatenate([joined(1, low), joined(1, high) + diag_high.astype(F32)], axis=0)
        to_y = jnp.concatenate([joined(2, low) + diag_low.astype(F32), joined(2, high)], axis=0)
        from_x = flip_row(after(to_x.astype(BF), *hold), NEXT_X)
        from_y = flip_row(after(to_y.astype(BF), *hold), NEXT_Y)
        hold = yield from_x, from_y
        from_x, from_y = after(from_x, from_y, *hold), after(from_y, from_x, *hold)
        plane = joined(0, every) + from_x.astype(F32) + from_y.astype(F32)
        others = flip_col(plane[2:4].astype(BF), 2)
        hold = yield others
        pair = plane[0:2] + after(others, *hold).astype(F32)
        yield pair[0] + flip_col(pair[1].astype(BF), 1).astype(F32)

    def total(self, values, stages):
        hops = [(flip_col, 1), (flip_col, 2), (flip_row, CORE), (flip_row, NEXT_X), (flip_row, NEXT_Y)]
        for (flip, mask), stage in zip(hops, stages):
            values = values + after(flip(values, mask), *stage)
        return values


def per_device(
    mesh,
    images, cotangent, counts, w_qkv, w_out, w_up, w_down, norm_gains, res_biases, b_up,
    m_qkv, m_out, m_up, m_down, m_gains, m_biases, m_bup,
    v_qkv, v_out, v_up, v_down, v_gains, v_biases, v_bup,
):
    seq = images.shape[1]
    relative = mesh.shape["row"] == 8 and mesh.shape["col"] == 4
    plan = RelativePlan(mesh) if relative else PlainPlan(mesh)
    info = jnp.stack([plan.turn, plan.mask, lax.axis_index("col"), lax.axis_index("row")]).astype(jnp.int32)
    att_widths = (w_qkv.shape[2], w_out.shape[1])
    ffn_widths = (w_up.shape[2], w_down.shape[1])
    shards = []
    for level in range(LAYERS):
        shards.append([
            jnp.concatenate([w_qkv[level].astype(BF), w_out[level].T.astype(BF)], axis=1),
            w_up[level].astype(BF),
            w_down[level].T.astype(BF),
        ])

    hidden, upstream, gains, biases, bup = prepare(
        seq, info, counts, images, cotangent,
        norm_gains.reshape(2 * LAYERS, D), res_biases.reshape(2 * LAYERS, D),
        b_up.reshape(LAYERS * BLOCKS, 1, UP_W),
    )
    saved, att_full, ffn_full = [], [], []

    def forward_attend(level, hidden, pieces):
        att_full.append(pieces)
        return attend(seq, level, info, hidden, gains, biases, pieces)

    def forward_feed(level, hidden, state, pieces):
        qkv, lse, oext, h1, a2 = state
        ffn_full.append(pieces)
        z, slope, y = feed(level, info, h1, a2, biases, bup, pieces)
        saved.append((hidden, qkv, lse, oext, h1, a2, z, slope))
        return y

    def gathered(level):
        return [plan.gather(jnp.concatenate(shards[level], axis=1), att_widths + ffn_widths)]

    later = gathered(1)
    if relative:
        fetches = [RelativeFetch(shard) for shard in shards[0]]
        one = fetches[0].turn_one()
        two = fetches[0].turn_two()
        plane, ran, arrived = (), (gains,), []
        for index, fetch in enumerate(fetches):
            plane = (fetch.plane(*plane),)
            if index + 1 < len(fetches):
                one = fetches[index + 1].turn_one(one)
                two = fetches[index + 1].turn_two(two)
            arrived.append(fetch.rest(two, *ran))
            ran = ()
        sooner = arrived[0], arrived[1] + arrived[2]
    else:
        sooner = (gathered(0),) * 2
    state = forward_attend(0, hidden, sooner[0])
    middle = forward_feed(0, hidden, state, sooner[1])
    state = forward_attend(1, middle, later)
    hidden = forward_feed(1, middle, state, later)
    smalls = [None] * LAYERS

    def backward_feed(level, upstream, landed):
        below, qkv, lse, oext, h1, a2, z, slope = saved[level]
        return feed_back(level, info, upstream, h1, a2, gains, z, slope, ffn_full[level], landed)

    def backward_attend(level, dh1, sums, bup_sum, landed):
        below, qkv, lse, oext, h1, a2, z, slope = saved[level]
        return attend_back(
            seq, level, level == 1, info, dh1, below, gains, qkv, lse, oext, sums, bup_sum, att_full[level], landed
        )

    done = {}
    near, far, bup_sum, dh1, sums = backward_feed(1, upstream, [])
    ffn_one = plan.reduce(near, far, ffn_widths)
    core_one = next(ffn_one)
    whole_one, upstream, smalls[1] = backward_attend(1, dh1, sums, bup_sum, [])
    done["att", 1] = plan.scatter(whole_one, att_widths)
    diag_one = ffn_one.send(())
    near, far, bup_sum, dh1, sums = backward_feed(0, upstream, [*diag_one])
    plane_one = ffn_one.send(())
    ffn_zero = plan.reduce(near, far, ffn_widths)
    core_zero = next(ffn_zero)
    near, far, upstream, smalls[0] = backward_attend(0, dh1, sums, bup_sum, [])
    att_zero = plan.reduce(near, far, att_widths, core_zero)
    core_last = next(att_zero)
    diag_zero = ffn_zero.send((smalls[0],))
    plane_zero = ffn_zero.send(())
    diag_last = att_zero.send(diag_zero)
    plane_last = att_zero.send(())
    turn_one, turn_zero, turn_last = ffn_one.send((smalls[0],)), ffn_zero.send(diag_last), att_zero.send(())
    done["ffn", 1], done["ffn", 0], done["att", 0] = ffn_one.send(diag_zero), ffn_zero.send(plane_last), att_zero.send(())
    layer_out = finish(seq, info, counts, hidden, [upstream])
    stages = [(), (), (), plane_one, plane_last]
    small = plan.total(jnp.concatenate(smalls, axis=0), stages).reshape(LAYERS, 8, D)
    ffn, att = [[done[name, level] for level in range(LAYERS)] for name in ("ffn", "att")]
    tops = update_matrices(att, (w_qkv, m_qkv, v_qkv), (w_out, m_out, v_out))
    feeds = update_matrices(ffn, (w_up, m_up, v_up), (w_down, m_down, v_down))
    matrices = [tops[0:4], tops[4:8], feeds[0:4], feeds[4:8]]
    vector_grads = [small[:, 0:2], small[:, 2:4], small[:, 4:8].reshape(LAYERS, FF)]
    params_in = [norm_gains, res_biases, b_up]
    firsts = [m_gains, m_biases, m_bup]
    seconds = [v_gains, v_biases, v_bup]
    vectors = [
        adamw_step(params_in[index], vector_grads[index], firsts[index], seconds[index])
        for index in range(3)
    ]
    return (
        (layer_out, upstream)
        + tuple(matrix[0] for matrix in matrices)
        + tuple(vector_grads)
        + tuple(matrix[1] for matrix in matrices)
        + tuple(matrix[2] for matrix in matrices)
        + tuple(vector[1] for vector in vectors)
        + tuple(matrix[3] for matrix in matrices)
        + tuple(vector[2] for vector in vectors)
    )


def solution(mesh):
    tokens = P(("row", "col"), None, None)
    matrices = (P(None, "row", "col"), P(None, "col", "row"), P(None, "row", "col"), P(None, "col", "row"))
    vectors = (P(), P(), P())
    in_specs = (tokens, tokens, P()) + (matrices + vectors) * 3
    out_specs = (tokens, tokens) + matrices + vectors + matrices + (matrices + vectors) * 2
    return jax.shard_map(
        functools.partial(per_device, mesh), mesh=mesh, in_specs=in_specs, out_specs=out_specs, check_vma=False
    )
```

```python
import functools

import jax
import jax.numpy as jnp
from jax import lax
from jax.experimental import pallas as pl
from jax.experimental.pallas import tpu as pltpu
from jax.sharding import PartitionSpec as P

HEADS = 12
LAYERS = 2
STEP = 3
D = 768
FF = 3072
HD = 64
BLOCKS = 4
ROWS = 208
QKV_W = 3 * D // BLOCKS
OUT_W = D // BLOCKS
UP_W = FF // BLOCKS
PIECE = 96

norm_eps = 1e-06
root_half = 0.7071067811865476
inv_root_two_pi = 0.3989422804014327
beta_one = 0.9
beta_two = 0.999
adam_eps = 1e-08
learn_rate = 0.06
decay_rate = 0.05

BF = jnp.bfloat16
F32 = jnp.float32


def dot_nn(a, b):
    return lax.dot_general(a, b, (((1,), (0,)), ((), ())), preferred_element_type=F32)


def dot_nt(a, b):
    return lax.dot_general(a, b, (((1,), (1,)), ((), ())), preferred_element_type=F32)


def dot_tn(a, b):
    return lax.dot_general(a, b, (((0,), (0,)), ((), ())), preferred_element_type=F32)


def scaled_rows(x):
    center = jnp.mean(x, axis=-1, keepdims=True)
    shifted = x - center
    inverse = lax.rsqrt(jnp.mean(shifted * shifted, axis=-1, keepdims=True) + norm_eps)
    return shifted * inverse, inverse


def norm_back(upstream, scaled, inverse, gain):
    grad_scaled = upstream * gain
    mean_one = jnp.mean(grad_scaled, axis=-1, keepdims=True)
    mean_two = jnp.mean(grad_scaled * scaled, axis=-1, keepdims=True)
    grad_gain = jnp.sum(upstream * scaled, axis=0, keepdims=True)
    return inverse * (grad_scaled - mean_one - scaled * mean_two), grad_gain


def block_of(turn, s):
    return jnp.bitwise_xor(turn, s)


FFN_W = 2 * UP_W


def piece_copies(info_ref, refs, column, w, sems):
    copies = []
    for s in range(BLOCKS):
        row = []
        for index, ref in enumerate(refs):
            for part in range(8 if ref.shape[1] == 8 else 4):
                if ref.shape[1] == 8:
                    block = part
                    lanes = slice(0, w.shape[2])
                    source = ref.at[
                        block_of(info_ref[0], s), jnp.bitwise_xor(info_ref[1], part), :,
                        column : column + w.shape[2],
                    ]
                else:
                    block = 2 * part + index % 2
                    lanes = slice(index // 2 * D, (index // 2 + 1) * D)
                    source = ref.at[part, s]
                target = w.at[s, block * PIECE : (block + 1) * PIECE, lanes]
                row.append(pltpu.make_async_copy(source, target, sems.at[s, len(row)]))
        copies.append(row)
    return copies


def start_all(copies):
    for row in copies:
        for copy in row:
            copy.start()


def wait_row(row):
    for copy in row:
        copy.wait()


def flip_features(x, mask):
    place = lax.broadcasted_iota(jnp.int32, x.shape, 1)
    block = jnp.zeros(x.shape, jnp.int32)
    for edge in range(1, D // PIECE):
        block = block + (place >= edge * PIECE).astype(jnp.int32)
    for bit in range(3):
        size = PIECE << bit
        even = ((block >> bit) & 1) == 0
        swapped = jnp.where(even, pltpu.roll(x, D - size, axis=1), pltpu.roll(x, size, axis=1))
        x = jnp.where(jnp.full(x.shape, (mask >> bit) & 1, jnp.int32) == 1, swapped, x)
    return x


def prepare_kernel(
    seq, info_ref, counts_ref, images_ref, cot_ref, gains_ref, biases_ref, bup_ref,
    x_ref, g_ref, gains_out, biases_out, bup_out,
):
    mask = info_ref[1]
    live = (info_ref[2] < counts_ref[info_ref[3]]).astype(F32)
    x_ref[ROWS - 16 : ROWS, :] = jnp.zeros((16, D), F32)
    g_ref[ROWS - 16 : ROWS, :] = jnp.zeros((16, D), F32)
    x_ref[0:seq, :] = flip_features(images_ref[0], mask)
    g_ref[0:seq, :] = flip_features(cot_ref[0], mask) * live
    gains_out[...] = flip_features(gains_ref[...], mask)
    biases_out[...] = flip_features(biases_ref[...], mask)
    for level in range(LAYERS):
        for s in range(BLOCKS):
            bup_out[level, s] = bup_ref[level * BLOCKS + block_of(info_ref[0], s)]


def finish_kernel(seq, extra, info_ref, counts_ref, y_ref, *rest):
    out_ref = rest[extra]
    live = (info_ref[2] < counts_ref[info_ref[3]]).astype(F32)
    out_ref[0] = flip_features(y_ref[...], info_ref[1])[0:seq] * live


def attend_kernel(seq, level, n_pieces, info_ref, x_ref, gain_ref, bias_ref, *rest):
    pieces = rest[:n_pieces]
    qkv_ref, lse_ref, oext_ref, h1_ref, a2_ref, blk, w, sems = rest[n_pieces:]
    copies = piece_copies(info_ref, pieces, 0, w, sems)
    start_all(copies)
    turn = info_ref[0]
    x = x_ref[...]
    scaled, _ = scaled_rows(x)
    a1 = (scaled * gain_ref[2 * level : 2 * level + 1, :]).astype(BF)
    for s in range(BLOCKS):
        wait_row(copies[s])
        t = dot_nn(a1, w[s, :, 0:640])
        blk[block_of(turn, s)] = t.astype(BF)
    for b in range(BLOCKS):
        qkv_ref[:, b * QKV_W : (b + 1) * QKV_W] = blk[b, :, 0:QKV_W]
    low_half = lax.broadcasted_iota(jnp.int32, (ROWS, 128), 1) < HD
    key_live = lax.broadcasted_iota(jnp.int32, (ROWS, ROWS), 0) < seq
    scale = HD ** (-0.5)
    oext_ref[:, :, 0:HD] = jnp.zeros((BLOCKS, ROWS, HD), BF)
    for pair in range(HEADS // 2):
        q2 = qkv_ref[:, pair * 128 : (pair + 1) * 128]
        k2 = qkv_ref[:, D + pair * 128 : D + (pair + 1) * 128]
        v2 = qkv_ref[:, 2 * D + pair * 128 : 2 * D + (pair + 1) * 128]
        mixed = []
        for half in range(2):
            live = low_half if half == 0 else jnp.logical_not(low_half)
            qm = jnp.where(live, q2, jnp.zeros_like(q2))
            st = jnp.where(key_live, dot_nt(k2, qm) * scale, -1e30)
            peak = jnp.max(st, axis=0, keepdims=True)
            grown = jnp.exp(st - peak)
            total = jnp.sum(grown, axis=0, keepdims=True)
            head = 2 * pair + half
            lse_ref[head : head + 1, :] = peak + jnp.log(total)
            probs = (grown * (1.0 / total)).astype(BF)
            mixed.append(dot_tn(probs, v2))
        both = jnp.where(low_half, mixed[0], mixed[1]).astype(BF)
        for half in range(2):
            head = 2 * pair + half
            lane = HD + (head % 3) * HD
            oext_ref[head // 3, :, lane : lane + HD] = both[:, half * HD : (half + 1) * HD]
    total = x + bias_ref[2 * level : 2 * level + 1, :]
    for s in range(BLOCKS):
        total = total + dot_nt(oext_ref[block_of(turn, s)], w[s, :, 512:768])
    h1_ref[...] = total
    scaled2, _ = scaled_rows(total)
    a2_ref[...] = (scaled2 * gain_ref[2 * level + 1 : 2 * level + 2, :]).astype(BF)


def feed_kernel(level, n_pieces, info_ref, h1_ref, a2_ref, bias_ref, bup_ref, *rest):
    pieces = rest[:n_pieces]
    z_ref, slope_ref, y_ref, w, sems = rest[n_pieces:]
    s = pl.program_id(0)
    copies = piece_copies(info_ref, pieces, D, w, sems)

    @pl.when(s == 0)
    def _():
        start_all(copies)
        y_ref[...] = h1_ref[...] + bias_ref[2 * level + 1 : 2 * level + 2, :]

    for step in range(BLOCKS):

        @pl.when(s == step)
        def _():
            wait_row(copies[step])

    u = dot_nn(a2_ref[...], w[s, :, 0:UP_W]) + bup_ref[0, 0]
    bell = 0.5 * (1.0 + lax.erf(u * root_half))
    z = (u * bell).astype(BF)
    z_ref[0] = z
    slope_ref[0] = bell + u * inv_root_two_pi * jnp.exp(-0.5 * u * u)
    y_ref[...] += dot_nt(z, w[s, :, UP_W:FFN_W])


def put_grad(near_ref, far_ref, value, first, width):
    for j in range(8):
        ref = near_ref if j % 2 == 0 else far_ref
        ref[j // 2, 0, :, first : first + width] = value[j * PIECE : (j + 1) * PIECE]


def feed_back_kernel(level, n_pieces, n_after, info_ref, g_ref, h1_ref, a2_ref, gain_ref, z_ref, slope_ref, *rest):
    pieces = rest[:n_pieces]
    near_ref, far_ref, bup_ref, dh1_ref, sums_ref, da2, gb_t, a2_t, w, sems = rest[n_pieces + n_after :]
    s = pl.program_id(0)
    copies = piece_copies(info_ref, pieces, D, w, sems)

    @pl.when(s == 0)
    def _():
        start_all(copies)
        da2[...] = jnp.zeros_like(da2)
        gb_t[...] = g_ref[...].T.astype(BF)
        a2_t[...] = a2_ref[...].T

    for step in range(BLOCKS):

        @pl.when(s == step)
        def _():
            wait_row(copies[step])

    gb = g_ref[...].astype(BF)
    put_grad(near_ref, far_ref, dot_nn(gb_t[...], z_ref[0]).astype(BF), UP_W, UP_W)
    du = dot_nn(gb, w[s, :, UP_W:FFN_W]) * slope_ref[0]
    bup_ref[0] = jnp.sum(du, axis=0, keepdims=True)
    dub = du.astype(BF)
    put_grad(near_ref, far_ref, dot_nn(a2_t[...], dub).astype(BF), 0, UP_W)
    da2[...] += dot_nt(dub, w[s, :, 0:UP_W])

    @pl.when(s == BLOCKS - 1)
    def _():
        g = g_ref[...]
        scaled, inverse = scaled_rows(h1_ref[...])
        below, grad_gain = norm_back(da2[...], scaled, inverse, gain_ref[2 * level + 1 : 2 * level + 2, :])
        dh1 = below + g
        dh1_ref[...] = dh1
        sums_ref[0:1, :] = grad_gain
        sums_ref[1:2, :] = jnp.sum(dh1, axis=0, keepdims=True)
        sums_ref[2:3, :] = jnp.sum(g, axis=0, keepdims=True)


def attend_back_kernel(
    seq, level, whole_order, n_pieces, n_after,
    info_ref, dh1_ref, x_ref, gain_ref, qkv_ref, lse_ref, oext_ref, sums_in, bup_in, *rest,
):
    pieces = rest[:n_pieces]
    *outs, below_ref, small_ref = rest[n_pieces + n_after : -6]
    dext, dmix, dqkv, dqx, w, sems = rest[-6:]
    copies = piece_copies(info_ref, pieces, 0, w, sems)
    start_all(copies)
    turn = info_ref[0]
    dh1 = dh1_ref[...]
    hb = dh1.astype(BF)
    hb_t = dh1.T.astype(BF)
    for s in range(BLOCKS):
        wait_row(copies[s])
        dext[block_of(turn, s)] = dot_nn(hb, w[s, :, 512:768]).astype(BF)
    for b in range(BLOCKS):
        dmix[:, b * OUT_W : (b + 1) * OUT_W] = dext[b, :, HD : HD + OUT_W]
    low_half = lax.broadcasted_iota(jnp.int32, (ROWS, 128), 1) < HD
    key_live = lax.broadcasted_iota(jnp.int32, (ROWS, ROWS), 0) < seq
    scale = HD ** (-0.5)
    for pair in range(HEADS // 2):
        q2 = qkv_ref[:, pair * 128 : (pair + 1) * 128]
        k2 = qkv_ref[:, D + pair * 128 : D + (pair + 1) * 128]
        v2 = qkv_ref[:, 2 * D + pair * 128 : 2 * D + (pair + 1) * 128]
        d2 = dmix[:, pair * 128 : (pair + 1) * 128]
        dq = jnp.zeros((ROWS, 128), F32)
        dk = jnp.zeros((ROWS, 128), F32)
        dv = jnp.zeros((ROWS, 128), F32)
        for half in range(2):
            head = 2 * pair + half
            live = low_half if half == 0 else jnp.logical_not(low_half)
            none = jnp.zeros_like(q2)
            qm = jnp.where(live, q2, none)
            km = jnp.where(live, k2, none)
            dm = jnp.where(live, d2, none)
            st = jnp.where(key_live, dot_nt(k2, qm) * scale, -1e30)
            probs = jnp.exp(st - lse_ref[head : head + 1, :])
            dprobs = dot_nt(v2, dm)
            inner = jnp.sum(probs * dprobs, axis=0, keepdims=True)
            dst = (probs * (dprobs - inner) * scale).astype(BF)
            dv = dv + dot_nn(probs.astype(BF), dm)
            dk = dk + dot_nn(dst, qm)
            dq = dq + dot_tn(dst, km)
        dqkv[:, pair * 128 : (pair + 1) * 128] = dq.astype(BF)
        dqkv[:, D + pair * 128 : D + (pair + 1) * 128] = dk.astype(BF)
        dqkv[:, 2 * D + pair * 128 : 2 * D + (pair + 1) * 128] = dv.astype(BF)
    for b in range(BLOCKS):
        dqx[b, :, 0:QKV_W] = dqkv[:, b * QKV_W : (b + 1) * QKV_W]
        dqx[b, :, QKV_W:640] = jnp.zeros((ROWS, 640 - QKV_W), BF)
    gain = gain_ref[2 * level : 2 * level + 1, :]
    scaled, inverse = scaled_rows(x_ref[...])
    a1_t = (scaled * gain).T.astype(BF)
    da1 = jnp.zeros((ROWS, D), F32)
    for s in range(BLOCKS):
        own = block_of(turn, s)
        part = dqx[own]
        da1 = da1 + dot_nt(part, w[s, :, 0:640])
        first = dot_nn(a1_t, part)
        second = dot_nn(hb_t, oext_ref[own])
        for j in range(8):
            rows = slice(j * PIECE, (j + 1) * PIECE)
            if whole_order:
                ref = outs[0].at[own, jnp.bitwise_xor(info_ref[1], j)]
            else:
                ref = outs[j % 2].at[j // 2, s]
            ref[:, 0:512] = first[rows, 0:512].astype(BF)
            ref[:, 512:640] = (first[rows, 512:640] + second[rows, 0:128]).astype(BF)
            ref[:, 640:768] = second[rows, 128:256].astype(BF)
    below, grad_gain = norm_back(da1, scaled, inverse, gain)
    below = below + dh1
    if level == 0:
        below_ref[0] = flip_features(below, info_ref[1])[0:seq]
    else:
        below_ref[...] = below
    small_ref[0:1, :] = grad_gain
    small_ref[1:4, :] = sums_in[0:3, :]
    small_ref[4:8, :] = jnp.zeros((4, D), F32)
    small_ref[...] = flip_features(small_ref[...], info_ref[1])
    for s in range(BLOCKS):
        small_ref[pl.ds(4 + block_of(turn, s), 1), :] = bup_in[s]


VM = pl.BlockSpec(memory_space=pltpu.VMEM)
SM = pl.BlockSpec(memory_space=pltpu.SMEM)
HB = pl.BlockSpec(memory_space=pl.ANY)
LIMIT = 60 * 1024 * 1024


def sds(shape, dtype):
    return jax.ShapeDtypeStruct(shape, dtype)


def params():
    return pltpu.CompilerParams(vmem_limit_bytes=LIMIT)


def cost(flops, traffic):
    return pl.CostEstimate(flops=flops, bytes_accessed=traffic, transcendentals=0)


def weight_scratch(width):
    return [pltpu.VMEM((BLOCKS, D, width), BF), pltpu.SemaphoreType.DMA((BLOCKS, 16))]


def prepare(seq, info, counts, images, cotangent, gains, biases, bup):
    return pl.pallas_call(
        functools.partial(prepare_kernel, seq),
        out_shape=(
            sds((ROWS, D), F32), sds((ROWS, D), F32), sds(gains.shape, F32), sds(biases.shape, F32),
            sds((LAYERS, BLOCKS, 1, UP_W), F32),
        ),
        in_specs=[SM, SM] + [VM] * 5,
        out_specs=[VM] * 5,
        compiler_params=params(),
        cost_estimate=cost(10**7, 10**5),
        name="prepare",
    )(info, counts, images, cotangent, gains, biases, bup)


def finish(seq, info, counts, y, after):
    return pl.pallas_call(
        functools.partial(finish_kernel, seq, len(after)),
        out_shape=sds((1, seq, D), F32),
        in_specs=[SM, SM, VM] + [HB] * len(after),
        out_specs=VM,
        compiler_params=params(),
        cost_estimate=cost(10**7, 10**5),
        name="finish",
    )(info, counts, y, *after)


def attend(seq, level, info, x, gains, biases, pieces):
    return pl.pallas_call(
        functools.partial(attend_kernel, seq, level, len(pieces)),
        out_shape=(
            sds((ROWS, 3 * D), BF), sds((16, ROWS), F32), sds((BLOCKS, ROWS, 256), BF),
            sds((ROWS, D), F32), sds((ROWS, D), BF),
        ),
        in_specs=[SM] + [VM] * 3 + [HB] * len(pieces),
        out_specs=[VM] * 5,
        scratch_shapes=[pltpu.VMEM((BLOCKS, ROWS, 640), BF)] + weight_scratch(D),
        compiler_params=params(),
        cost_estimate=cost(10**7, 10**5),
        name="attend",
    )(info, x, gains, biases, *pieces)


def whole(shape):
    return pl.BlockSpec(shape, lambda s: (0,) * len(shape))


def feed(level, info, h1, a2, biases, bup, pieces):
    return pl.pallas_call(
        functools.partial(feed_kernel, level, len(pieces)),
        grid=(BLOCKS,),
        out_shape=(sds((BLOCKS, ROWS, UP_W), BF), sds((BLOCKS, ROWS, UP_W), F32), sds((ROWS, D), F32)),
        in_specs=[
            SM, whole((ROWS, D)), whole((ROWS, D)), whole(biases.shape),
            pl.BlockSpec((1, 1, 1, UP_W), lambda s: (level, s, 0, 0)),
        ]
        + [HB] * len(pieces),
        out_specs=[
            pl.BlockSpec((1, ROWS, UP_W), lambda s: (s, 0, 0)),
            pl.BlockSpec((1, ROWS, UP_W), lambda s: (s, 0, 0)),
            whole((ROWS, D)),
        ],
        scratch_shapes=weight_scratch(FFN_W),
        compiler_params=params(),
        cost_estimate=cost(10**7, 10**5),
        name="feed",
    )(info, h1, a2, biases, bup, *pieces)


def feed_back(level, info, g, h1, a2, gains, z, slope, pieces, after):
    grad = sds((4, BLOCKS, PIECE, FFN_W), BF)
    grad_spec = pl.BlockSpec((4, 1, PIECE, FFN_W), lambda s: (0, s, 0, 0))
    step_spec = pl.BlockSpec((1, ROWS, UP_W), lambda s: (s, 0, 0))
    return pl.pallas_call(
        functools.partial(feed_back_kernel, level, len(pieces), len(after)),
        grid=(BLOCKS,),
        out_shape=(grad, grad, sds((BLOCKS, 1, UP_W), F32), sds((ROWS, D), F32), sds((8, D), F32)),
        in_specs=[SM, whole((ROWS, D)), whole((ROWS, D)), whole((ROWS, D)), whole(gains.shape), step_spec, step_spec]
        + [HB] * (len(pieces) + len(after)),
        out_specs=[
            grad_spec, grad_spec,
            pl.BlockSpec((1, 1, UP_W), lambda s: (s, 0, 0)), whole((ROWS, D)), whole((8, D)),
        ],
        scratch_shapes=[pltpu.VMEM((ROWS, D), F32), pltpu.VMEM((D, ROWS), BF), pltpu.VMEM((D, ROWS), BF)]
        + weight_scratch(FFN_W),
        compiler_params=params(),
        cost_estimate=cost(10**7, 10**5),
        name="feed_back",
    )(info, g, h1, a2, gains, z, slope, *pieces, *after)


def attend_back(seq, level, whole_order, info, dh1, x, gains, qkv, lse, oext, sums, bup, pieces, after):
    grads = [sds((BLOCKS, 8, PIECE, D), BF)] if whole_order else [sds((4, BLOCKS, PIECE, D), BF)] * 2
    below = sds((1, seq, D), F32) if level == 0 else sds((ROWS, D), F32)
    return pl.pallas_call(
        functools.partial(attend_back_kernel, seq, level, whole_order, len(pieces), len(after)),
        out_shape=(*grads, below, sds((8, D), F32)),
        in_specs=[SM] + [VM] * 8 + [HB] * (len(pieces) + len(after)),
        out_specs=[VM] * (len(grads) + 2),
        scratch_shapes=[
            pltpu.VMEM((BLOCKS, ROWS, 256), BF), pltpu.VMEM((ROWS, D), BF),
            pltpu.VMEM((ROWS, 3 * D), BF), pltpu.VMEM((BLOCKS, ROWS, 640), BF),
        ]
        + weight_scratch(D),
        compiler_params=params(),
        cost_estimate=cost(10**7, 10**5),
        name="attend_back",
    )(info, dh1, x, gains, qkv, lse, oext, sums, bup, *pieces, *after)


def adamw_step(param, gradient, first_moment, second_moment):
    fresh_first = beta_one * first_moment + (1.0 - beta_one) * gradient
    fresh_second = beta_two * second_moment + (1.0 - beta_two) * gradient * gradient
    first_hat = fresh_first / (1.0 - beta_one**STEP)
    second_hat = fresh_second / (1.0 - beta_two**STEP)
    updated = param - learn_rate * (
        first_hat / (jnp.sqrt(second_hat) + adam_eps) + decay_rate * param
    )
    return (updated, fresh_first, fresh_second)


def after(value, *earlier):
    return lax.optimization_barrier((value,) + earlier)[0]


class PlainPlan:
    def __init__(self, mesh):
        self.n_row = mesh.shape["row"]
        self.n_col = mesh.shape["col"]
        self.turn = jnp.int32(0)
        self.mask = jnp.int32(0)

    def gather(self, shard, widths):
        full = lax.all_gather(shard, ("col", "row"), axis=0, tiled=True)
        full = full.reshape(self.n_col, D, sum(widths))
        parts = []
        start = 0
        for width in widths:
            part = full[:, :, start : start + width].transpose(1, 0, 2)
            parts.append(part.reshape(D, BLOCKS, -1).transpose(1, 0, 2))
            start += width
        return jnp.concatenate(parts, axis=2).reshape(BLOCKS, 8, PIECE, -1)

    def reduce(self, near, far, widths, *earlier):
        done = self.scatter(jnp.stack([near, far], axis=1).transpose(2, 0, 1, 3, 4), widths)
        for _ in range(2):
            yield done
        yield done, done
        yield done
        yield done

    def scatter(self, full, widths):
        full = full.reshape(BLOCKS, D, -1).transpose(1, 0, 2)
        parts = []
        start = 0
        for width in widths:
            wide = width * self.n_col // BLOCKS
            part = full[:, :, start : start + wide].reshape(D, self.n_col, width)
            parts.append(part.transpose(1, 0, 2))
            start += wide
        packed = jnp.concatenate(parts, axis=2).reshape(self.n_col * D, sum(widths))
        return lax.psum_scatter(packed, ("col", "row"), scatter_dimension=0, tiled=True)

    def total(self, values, stages):
        return lax.psum(values, ("row", "col"))


def flip_row(x, mask):
    return lax.ppermute(x, "row", [(i, i ^ mask) for i in range(8)])


def flip_col(x, mask):
    return lax.ppermute(x, "col", [(i, i ^ mask) for i in range(4)])


CORE, NEXT_X, NEXT_Y = 1, 2, 4


def update_kernel(turn, *refs):
    grads, inputs, outputs = refs[:LAYERS], refs[LAYERS : LAYERS + 6], refs[LAYERS + 6 :]
    cut = inputs[0].shape[2]
    for level in range(LAYERS):
        both = grads[level][...].astype(F32)
        for index in range(2):
            param, first, second = inputs[3 * index : 3 * index + 3]
            grad_out, param_out, first_out, second_out = outputs[4 * index : 4 * index + 4]
            gradient = both[:, cut:] if index else both[:, :cut]
            if index and turn:
                gradient = gradient.T
            grad_out[level] = gradient
            fresh = adamw_step(param[level], gradient, first[level], second[level])
            param_out[level], first_out[level], second_out[level] = fresh


def update_matrices(turn, grads, first, second):
    return pl.pallas_call(
        functools.partial(update_kernel, turn),
        out_shape=[sds(group[0].shape, F32) for group in (first, second) for _ in range(4)],
        in_specs=[VM] * (LAYERS + 6),
        out_specs=[VM] * 8,
        compiler_params=params(),
        cost_estimate=cost(10**7, 10**5),
        name="update",
    )(*grads, *first, *second)


class RelativeFetch:
    def __init__(self, shard):
        self.shard = shard

    def turn_one(self, *hold):
        shard = after(self.shard, *hold)
        self.pair = jnp.stack([shard, flip_col(shard, 1)])
        return self.pair[1]

    def turn_two(self, *hold):
        self.others = flip_col(after(self.pair, *hold), 2)
        return self.others

    def plane(self, *hold):
        self.own = after(jnp.concatenate([self.pair, self.others], axis=0), *hold)
        self.from_x = flip_row(self.own, NEXT_X)
        self.from_y = flip_row(self.own, NEXT_Y)
        return self.from_x

    def rest(self, *hold):
        from_x, from_y = after(self.from_x, self.from_y, *hold), after(self.from_y, self.from_x, *hold)
        diag_low = flip_row(from_y[0:2], NEXT_X)
        diag_high = flip_row(from_x[2:4], NEXT_Y)
        near = jnp.concatenate([self.own, from_x, from_y, diag_low, diag_high], axis=0)
        near = near.reshape((4, BLOCKS) + self.shard.shape)
        return [near, flip_row(near, CORE)]


class RelativePlan:
    def __init__(self, mesh):
        self.turn = lax.axis_index("col").astype(jnp.int32)
        self.mask = lax.axis_index("row").astype(jnp.int32)

    def gather(self, shard, widths):
        full = lax.all_gather(shard, ("col", "row"), axis=0, tiled=True)
        return full.reshape(BLOCKS, 8, PIECE, -1)

    def scatter(self, full, widths):
        full = full.reshape(BLOCKS * D, -1)
        return lax.psum_scatter(full, ("col", "row"), scatter_dimension=0, tiled=True)

    def reduce(self, near, far, widths, *earlier):
        far = after(far, *earlier)
        other = flip_row(far, CORE)
        hold = yield other
        other = after(other, *hold)

        def joined(m, blocks):
            return near[m, blocks].astype(F32) + other[m, blocks].astype(F32)

        low, high, every = slice(0, 2), slice(2, 4), slice(0, 4)
        diag_low = flip_row(after(joined(3, low).astype(BF), *hold), NEXT_X)
        diag_high = flip_row(after(joined(3, high).astype(BF), *hold), NEXT_Y)
        hold = yield diag_low, diag_high
        to_x = jnp.concatenate([joined(1, low), joined(1, high) + diag_high.astype(F32)], axis=0)
        to_y = jnp.concatenate([joined(2, low) + diag_low.astype(F32), joined(2, high)], axis=0)
        from_x = flip_row(after(to_x.astype(BF), *hold), NEXT_X)
        from_y = flip_row(after(to_y.astype(BF), *hold), NEXT_Y)
        hold = yield from_x, from_y
        from_x, from_y = after(from_x, from_y, *hold), after(from_y, from_x, *hold)
        plane = joined(0, every) + from_x.astype(F32) + from_y.astype(F32)
        others = flip_col(plane[2:4].astype(BF), 2)
        hold, last = yield others
        pair = plane[0:2] + after(others, *hold).astype(F32)
        yield pair[0] + flip_col(after(pair[1].astype(BF), *last), 1).astype(F32)

    def total(self, values, stages):
        hops = [(flip_col, 1), (flip_col, 2), (flip_row, CORE), (flip_row, NEXT_X), (flip_row, NEXT_Y)]
        for (flip, mask), stage in zip(hops, stages):
            values = values + after(flip(values, mask), *stage)
        return values


def per_device(
    mesh,
    images, cotangent, counts, w_qkv, w_out, w_up, w_down, norm_gains, res_biases, b_up,
    m_qkv, m_out, m_up, m_down, m_gains, m_biases, m_bup,
    v_qkv, v_out, v_up, v_down, v_gains, v_biases, v_bup,
):
    seq = images.shape[1]
    relative = mesh.shape["row"] == 8 and mesh.shape["col"] == 4
    plan = RelativePlan(mesh) if relative else PlainPlan(mesh)
    info = jnp.stack([plan.turn, plan.mask, lax.axis_index("col"), lax.axis_index("row")]).astype(jnp.int32)
    att_widths = (w_qkv.shape[2], w_out.shape[1])
    ffn_widths = (w_up.shape[2], w_down.shape[1])
    shards = []
    for level in range(LAYERS):
        shards.append([
            jnp.concatenate([w_qkv[level].astype(BF), w_out[level].T.astype(BF)], axis=1),
            w_up[level].astype(BF),
            w_down[level].T.astype(BF),
        ])

    hidden, upstream, gains, biases, bup = prepare(
        seq, info, counts, images, cotangent,
        norm_gains.reshape(2 * LAYERS, D), res_biases.reshape(2 * LAYERS, D),
        b_up.reshape(LAYERS * BLOCKS, 1, UP_W),
    )
    saved, att_full, ffn_full = [], [], []

    def forward_attend(level, hidden, pieces):
        att_full.append(pieces)
        return attend(seq, level, info, hidden, gains, biases, pieces)

    def forward_feed(level, hidden, state, pieces):
        qkv, lse, oext, h1, a2 = state
        ffn_full.append(pieces)
        z, slope, y = feed(level, info, h1, a2, biases, bup, pieces)
        saved.append((hidden, qkv, lse, oext, h1, a2, z, slope))
        return y

    def gathered(level):
        return [plan.gather(jnp.concatenate(shards[level], axis=1), att_widths + ffn_widths)]

    later = gathered(1)
    if relative:
        fetches = [RelativeFetch(shard) for shard in shards[0]]
        one = fetches[0].turn_one()
        two = fetches[0].turn_two()
        plane, ran, arrived = (), (gains,), []
        for index, fetch in enumerate(fetches):
            plane = (fetch.plane(*plane),)
            if index + 1 < len(fetches):
                one = fetches[index + 1].turn_one(one)
                two = fetches[index + 1].turn_two(two)
            arrived.append(fetch.rest(two, *ran))
            ran = ()
        sooner = arrived[0], arrived[1] + arrived[2]
    else:
        sooner = (gathered(0),) * 2
    state = forward_attend(0, hidden, sooner[0])
    middle = forward_feed(0, hidden, state, sooner[1])
    state = forward_attend(1, middle, later)
    hidden = forward_feed(1, middle, state, later)
    smalls = [None] * LAYERS

    def backward_feed(level, upstream, landed):
        below, qkv, lse, oext, h1, a2, z, slope = saved[level]
        return feed_back(level, info, upstream, h1, a2, gains, z, slope, ffn_full[level], landed)

    def backward_attend(level, dh1, sums, bup_sum, landed):
        below, qkv, lse, oext, h1, a2, z, slope = saved[level]
        return attend_back(
            seq, level, level == 1, info, dh1, below, gains, qkv, lse, oext, sums, bup_sum, att_full[level], landed
        )

    done = {}
    near, far, bup_sum, dh1, sums = backward_feed(1, upstream, [])
    ffn_one = plan.reduce(near, far, ffn_widths)
    core_one = next(ffn_one)
    whole_one, upstream, smalls[1] = backward_attend(1, dh1, sums, bup_sum, [])
    done["att", 1] = plan.scatter(whole_one, att_widths)
    diag_one = ffn_one.send(())
    near, far, bup_sum, dh1, sums = backward_feed(0, upstream, [*diag_one])
    plane_one = ffn_one.send(())
    ffn_zero = plan.reduce(near, far, ffn_widths)
    core_zero = next(ffn_zero)
    near, far, upstream, smalls[0] = backward_attend(0, dh1, sums, bup_sum, [])
    att_zero = plan.reduce(near, far, att_widths, core_zero)
    core_last = next(att_zero)
    diag_zero = ffn_zero.send((smalls[0],))
    plane_zero = ffn_zero.send(())
    diag_last = att_zero.send(diag_zero)
    plane_last = att_zero.send(())
    turn_one, turn_zero, turn_last = ffn_one.send((smalls[0],)), ffn_zero.send(diag_last), att_zero.send((done["att", 1],))
    done["ffn", 1], done["ffn", 0], done["att", 0] = (
        ffn_one.send((diag_zero, ())),
        ffn_zero.send((plane_last, ())),
        att_zero.send(((), ())),
    )
    layer_out = finish(seq, info, counts, hidden, [upstream])
    stages = [(), (), (), plane_one, plane_last]
    small = plan.total(jnp.concatenate(smalls, axis=0), stages).reshape(LAYERS, 8, D)
    ffn, att = [[done[name, level] for level in range(LAYERS)] for name in ("ffn", "att")]

    def turned(arrays):
        return [array.transpose(0, 2, 1) for array in arrays]

    tops = update_matrices(True, att, (w_qkv, m_qkv, v_qkv), (w_out, m_out, v_out))
    feeds = update_matrices(False, ffn, (w_up, m_up, v_up), turned((w_down, m_down, v_down)))
    matrices = [tops[0:4], tops[4:8], feeds[0:4], turned(feeds[4:8])]
    vector_grads = [small[:, 0:2], small[:, 2:4], small[:, 4:8].reshape(LAYERS, FF)]
    params_in = [norm_gains, res_biases, b_up]
    firsts = [m_gains, m_biases, m_bup]
    seconds = [v_gains, v_biases, v_bup]
    vectors = [
        adamw_step(params_in[index], vector_grads[index], firsts[index], seconds[index])
        for index in range(3)
    ]
    return (
        (layer_out, upstream)
        + tuple(matrix[0] for matrix in matrices)
        + tuple(vector_grads)
        + tuple(matrix[1] for matrix in matrices)
        + tuple(matrix[2] for matrix in matrices)
        + tuple(vector[1] for vector in vectors)
        + tuple(matrix[3] for matrix in matrices)
        + tuple(vector[2] for vector in vectors)
    )


def solution(mesh):
    tokens = P(("row", "col"), None, None)
    matrices = (P(None, "row", "col"), P(None, "col", "row"), P(None, "row", "col"), P(None, "col", "row"))
    vectors = (P(), P(), P())
    in_specs = (tokens, tokens, P()) + (matrices + vectors) * 3
    out_specs = (tokens, tokens) + matrices + vectors + matrices + (matrices + vectors) * 2
    return jax.shard_map(
        functools.partial(per_device, mesh), mesh=mesh, in_specs=in_specs, out_specs=out_specs, check_vma=False
    )
```

```python
import functools

import jax
import jax.numpy as jnp
from jax import lax
from jax.experimental import pallas as pl
from jax.experimental.pallas import tpu as pltpu
from jax.sharding import PartitionSpec as P

HEADS = 12
LAYERS = 2
STEP = 3
D = 768
FF = 3072
HD = 64
BLOCKS = 4
ROWS = 208
QKV_W = 3 * D // BLOCKS
OUT_W = D // BLOCKS
UP_W = FF // BLOCKS
PIECE = 96

norm_eps = 1e-06
root_half = 0.7071067811865476
inv_root_two_pi = 0.3989422804014327
beta_one = 0.9
beta_two = 0.999
adam_eps = 1e-08
learn_rate = 0.06
decay_rate = 0.05

BF = jnp.bfloat16
F32 = jnp.float32


def dot_nn(a, b):
    return lax.dot_general(a, b, (((1,), (0,)), ((), ())), preferred_element_type=F32)


def dot_nt(a, b):
    return lax.dot_general(a, b, (((1,), (1,)), ((), ())), preferred_element_type=F32)


def dot_tn(a, b):
    return lax.dot_general(a, b, (((0,), (0,)), ((), ())), preferred_element_type=F32)


def scaled_rows(x):
    center = jnp.mean(x, axis=-1, keepdims=True)
    shifted = x - center
    inverse = lax.rsqrt(jnp.mean(shifted * shifted, axis=-1, keepdims=True) + norm_eps)
    return shifted * inverse, inverse


def norm_back(upstream, scaled, inverse, gain):
    grad_scaled = upstream * gain
    mean_one = jnp.mean(grad_scaled, axis=-1, keepdims=True)
    mean_two = jnp.mean(grad_scaled * scaled, axis=-1, keepdims=True)
    grad_gain = jnp.sum(upstream * scaled, axis=0, keepdims=True)
    return inverse * (grad_scaled - mean_one - scaled * mean_two), grad_gain


def block_of(turn, s):
    return jnp.bitwise_xor(turn, s)


FFN_W = 2 * UP_W


def piece_copies(info_ref, refs, column, w, sems):
    copies = []
    for s in range(BLOCKS):
        row = []
        for index, ref in enumerate(refs):
            for part in range(8 if ref.shape[1] == 8 else 4):
                if ref.shape[1] == 8:
                    block = part
                    lanes = slice(0, w.shape[2])
                    source = ref.at[
                        block_of(info_ref[0], s), jnp.bitwise_xor(info_ref[1], part), :,
                        column : column + w.shape[2],
                    ]
                else:
                    block = 2 * part + index % 2
                    lanes = slice(index // 2 * D, (index // 2 + 1) * D)
                    source = ref.at[part, s]
                target = w.at[s, block * PIECE : (block + 1) * PIECE, lanes]
                row.append(pltpu.make_async_copy(source, target, sems.at[s, len(row)]))
        copies.append(row)
    return copies


def start_all(copies):
    for row in copies:
        for copy in row:
            copy.start()


def wait_row(row):
    for copy in row:
        copy.wait()


def flip_features(x, mask):
    place = lax.broadcasted_iota(jnp.int32, x.shape, 1)
    block = jnp.zeros(x.shape, jnp.int32)
    for edge in range(1, D // PIECE):
        block = block + (place >= edge * PIECE).astype(jnp.int32)
    for bit in range(3):
        size = PIECE << bit
        even = ((block >> bit) & 1) == 0
        swapped = jnp.where(even, pltpu.roll(x, D - size, axis=1), pltpu.roll(x, size, axis=1))
        x = jnp.where(jnp.full(x.shape, (mask >> bit) & 1, jnp.int32) == 1, swapped, x)
    return x


def prepare_kernel(
    seq, info_ref, counts_ref, images_ref, cot_ref, gains_ref, biases_ref, bup_ref,
    x_ref, g_ref, gains_out, biases_out, bup_out,
):
    mask = info_ref[1]
    live = (info_ref[2] < counts_ref[info_ref[3]]).astype(F32)
    x_ref[ROWS - 16 : ROWS, :] = jnp.zeros((16, D), F32)
    g_ref[ROWS - 16 : ROWS, :] = jnp.zeros((16, D), F32)
    x_ref[0:seq, :] = flip_features(images_ref[0], mask)
    g_ref[0:seq, :] = flip_features(cot_ref[0], mask) * live
    gains_out[...] = flip_features(gains_ref[...], mask)
    biases_out[...] = flip_features(biases_ref[...], mask)
    for level in range(LAYERS):
        for s in range(BLOCKS):
            bup_out[level, s] = bup_ref[level * BLOCKS + block_of(info_ref[0], s)]


def finish_kernel(seq, extra, info_ref, counts_ref, y_ref, *rest):
    out_ref = rest[extra]
    live = (info_ref[2] < counts_ref[info_ref[3]]).astype(F32)
    out_ref[0] = flip_features(y_ref[...], info_ref[1])[0:seq] * live


def attend_kernel(seq, level, n_pieces, info_ref, x_ref, gain_ref, bias_ref, *rest):
    pieces = rest[:n_pieces]
    qkv_ref, lse_ref, oext_ref, h1_ref, a2_ref, blk, w, sems = rest[n_pieces:]
    copies = piece_copies(info_ref, pieces, 0, w, sems)
    start_all(copies)
    turn = info_ref[0]
    x = x_ref[...]
    scaled, _ = scaled_rows(x)
    a1 = (scaled * gain_ref[2 * level : 2 * level + 1, :]).astype(BF)
    for s in range(BLOCKS):
        wait_row(copies[s])
        t = dot_nn(a1, w[s, :, 0:640])
        blk[block_of(turn, s)] = t.astype(BF)
    for b in range(BLOCKS):
        qkv_ref[:, b * QKV_W : (b + 1) * QKV_W] = blk[b, :, 0:QKV_W]
    low_half = lax.broadcasted_iota(jnp.int32, (ROWS, 128), 1) < HD
    key_live = lax.broadcasted_iota(jnp.int32, (ROWS, ROWS), 0) < seq
    scale = HD ** (-0.5)
    oext_ref[:, :, 0:HD] = jnp.zeros((BLOCKS, ROWS, HD), BF)
    for pair in range(HEADS // 2):
        q2 = qkv_ref[:, pair * 128 : (pair + 1) * 128]
        k2 = qkv_ref[:, D + pair * 128 : D + (pair + 1) * 128]
        v2 = qkv_ref[:, 2 * D + pair * 128 : 2 * D + (pair + 1) * 128]
        mixed = []
        for half in range(2):
            live = low_half if half == 0 else jnp.logical_not(low_half)
            qm = jnp.where(live, q2, jnp.zeros_like(q2))
            st = jnp.where(key_live, dot_nt(k2, qm) * scale, -1e30)
            peak = jnp.max(st, axis=0, keepdims=True)
            grown = jnp.exp(st - peak)
            total = jnp.sum(grown, axis=0, keepdims=True)
            head = 2 * pair + half
            lse_ref[head : head + 1, :] = peak + jnp.log(total)
            probs = (grown * (1.0 / total)).astype(BF)
            mixed.append(dot_tn(probs, v2))
        both = jnp.where(low_half, mixed[0], mixed[1]).astype(BF)
        for half in range(2):
            head = 2 * pair + half
            lane = HD + (head % 3) * HD
            oext_ref[head // 3, :, lane : lane + HD] = both[:, half * HD : (half + 1) * HD]
    total = x + bias_ref[2 * level : 2 * level + 1, :]
    for s in range(BLOCKS):
        total = total + dot_nt(oext_ref[block_of(turn, s)], w[s, :, 512:768])
    h1_ref[...] = total
    scaled2, _ = scaled_rows(total)
    a2_ref[...] = (scaled2 * gain_ref[2 * level + 1 : 2 * level + 2, :]).astype(BF)


def feed_kernel(level, n_pieces, info_ref, h1_ref, a2_ref, bias_ref, bup_ref, *rest):
    pieces = rest[:n_pieces]
    z_ref, slope_ref, y_ref, w, sems = rest[n_pieces:]
    s = pl.program_id(0)
    copies = piece_copies(info_ref, pieces, D, w, sems)

    @pl.when(s == 0)
    def _():
        start_all(copies)
        y_ref[...] = h1_ref[...] + bias_ref[2 * level + 1 : 2 * level + 2, :]

    for step in range(BLOCKS):

        @pl.when(s == step)
        def _():
            wait_row(copies[step])

    u = dot_nn(a2_ref[...], w[s, :, 0:UP_W]) + bup_ref[0, 0]
    bell = 0.5 * (1.0 + lax.erf(u * root_half))
    z = (u * bell).astype(BF)
    z_ref[0] = z
    slope_ref[0] = bell + u * inv_root_two_pi * jnp.exp(-0.5 * u * u)
    y_ref[...] += dot_nt(z, w[s, :, UP_W:FFN_W])


def put_grad(near_ref, far_ref, value, first, width):
    for j in range(8):
        ref = near_ref if j % 2 == 0 else far_ref
        ref[j // 2, 0, :, first : first + width] = value[j * PIECE : (j + 1) * PIECE]


def feed_back_kernel(level, n_pieces, n_after, info_ref, g_ref, h1_ref, a2_ref, gain_ref, z_ref, slope_ref, *rest):
    pieces = rest[:n_pieces]
    near_ref, far_ref, bup_ref, dh1_ref, sums_ref, da2, gb_t, a2_t, w, sems = rest[n_pieces + n_after :]
    s = pl.program_id(0)
    copies = piece_copies(info_ref, pieces, D, w, sems)

    @pl.when(s == 0)
    def _():
        start_all(copies)
        da2[...] = jnp.zeros_like(da2)
        gb_t[...] = g_ref[...].T.astype(BF)
        a2_t[...] = a2_ref[...].T

    for step in range(BLOCKS):

        @pl.when(s == step)
        def _():
            wait_row(copies[step])

    gb = g_ref[...].astype(BF)
    put_grad(near_ref, far_ref, dot_nn(gb_t[...], z_ref[0]).astype(BF), UP_W, UP_W)
    du = dot_nn(gb, w[s, :, UP_W:FFN_W]) * slope_ref[0]
    bup_ref[0] = jnp.sum(du, axis=0, keepdims=True)
    dub = du.astype(BF)
    put_grad(near_ref, far_ref, dot_nn(a2_t[...], dub).astype(BF), 0, UP_W)
    da2[...] += dot_nt(dub, w[s, :, 0:UP_W])

    @pl.when(s == BLOCKS - 1)
    def _():
        g = g_ref[...]
        scaled, inverse = scaled_rows(h1_ref[...])
        below, grad_gain = norm_back(da2[...], scaled, inverse, gain_ref[2 * level + 1 : 2 * level + 2, :])
        dh1 = below + g
        dh1_ref[...] = dh1
        sums_ref[0:1, :] = grad_gain
        sums_ref[1:2, :] = jnp.sum(dh1, axis=0, keepdims=True)
        sums_ref[2:3, :] = jnp.sum(g, axis=0, keepdims=True)


def attend_back_kernel(
    seq, level, whole_order, n_pieces, n_after,
    info_ref, dh1_ref, x_ref, gain_ref, qkv_ref, lse_ref, oext_ref, sums_in, bup_in, *rest,
):
    pieces = rest[:n_pieces]
    *outs, below_ref, small_ref = rest[n_pieces + n_after : -6]
    dext, dmix, dqkv, dqx, w, sems = rest[-6:]
    copies = piece_copies(info_ref, pieces, 0, w, sems)
    start_all(copies)
    turn = info_ref[0]
    dh1 = dh1_ref[...]
    hb = dh1.astype(BF)
    hb_t = dh1.T.astype(BF)
    for s in range(BLOCKS):
        wait_row(copies[s])
        dext[block_of(turn, s)] = dot_nn(hb, w[s, :, 512:768]).astype(BF)
    for b in range(BLOCKS):
        dmix[:, b * OUT_W : (b + 1) * OUT_W] = dext[b, :, HD : HD + OUT_W]
    low_half = lax.broadcasted_iota(jnp.int32, (ROWS, 128), 1) < HD
    key_live = lax.broadcasted_iota(jnp.int32, (ROWS, ROWS), 0) < seq
    scale = HD ** (-0.5)
    for pair in range(HEADS // 2):
        q2 = qkv_ref[:, pair * 128 : (pair + 1) * 128]
        k2 = qkv_ref[:, D + pair * 128 : D + (pair + 1) * 128]
        v2 = qkv_ref[:, 2 * D + pair * 128 : 2 * D + (pair + 1) * 128]
        d2 = dmix[:, pair * 128 : (pair + 1) * 128]
        dq = jnp.zeros((ROWS, 128), F32)
        dk = jnp.zeros((ROWS, 128), F32)
        dv = jnp.zeros((ROWS, 128), F32)
        for half in range(2):
            head = 2 * pair + half
            live = low_half if half == 0 else jnp.logical_not(low_half)
            none = jnp.zeros_like(q2)
            qm = jnp.where(live, q2, none)
            km = jnp.where(live, k2, none)
            dm = jnp.where(live, d2, none)
            st = jnp.where(key_live, dot_nt(k2, qm) * scale, -1e30)
            probs = jnp.exp(st - lse_ref[head : head + 1, :])
            dprobs = dot_nt(v2, dm)
            inner = jnp.sum(probs * dprobs, axis=0, keepdims=True)
            dst = (probs * (dprobs - inner) * scale).astype(BF)
            dv = dv + dot_nn(probs.astype(BF), dm)
            dk = dk + dot_nn(dst, qm)
            dq = dq + dot_tn(dst, km)
        dqkv[:, pair * 128 : (pair + 1) * 128] = dq.astype(BF)
        dqkv[:, D + pair * 128 : D + (pair + 1) * 128] = dk.astype(BF)
        dqkv[:, 2 * D + pair * 128 : 2 * D + (pair + 1) * 128] = dv.astype(BF)
    for b in range(BLOCKS):
        dqx[b, :, 0:QKV_W] = dqkv[:, b * QKV_W : (b + 1) * QKV_W]
        dqx[b, :, QKV_W:640] = jnp.zeros((ROWS, 640 - QKV_W), BF)
    gain = gain_ref[2 * level : 2 * level + 1, :]
    scaled, inverse = scaled_rows(x_ref[...])
    a1_t = (scaled * gain).T.astype(BF)
    da1 = jnp.zeros((ROWS, D), F32)
    for s in range(BLOCKS):
        own = block_of(turn, s)
        part = dqx[own]
        da1 = da1 + dot_nt(part, w[s, :, 0:640])
        first = dot_nn(a1_t, part)
        second = dot_nn(hb_t, oext_ref[own])
        for j in range(8):
            rows = slice(j * PIECE, (j + 1) * PIECE)
            if whole_order:
                ref = outs[0].at[own, jnp.bitwise_xor(info_ref[1], j)]
            else:
                ref = outs[j % 2].at[j // 2, s]
            ref[:, 0:512] = first[rows, 0:512].astype(BF)
            ref[:, 512:640] = (first[rows, 512:640] + second[rows, 0:128]).astype(BF)
            ref[:, 640:768] = second[rows, 128:256].astype(BF)
    below, grad_gain = norm_back(da1, scaled, inverse, gain)
    below = below + dh1
    if level == 0:
        below_ref[0] = flip_features(below, info_ref[1])[0:seq]
    else:
        below_ref[...] = below
    small_ref[0:1, :] = grad_gain
    small_ref[1:4, :] = sums_in[0:3, :]
    small_ref[4:8, :] = jnp.zeros((4, D), F32)
    small_ref[...] = flip_features(small_ref[...], info_ref[1])
    for s in range(BLOCKS):
        small_ref[pl.ds(4 + block_of(turn, s), 1), :] = bup_in[s]


VM = pl.BlockSpec(memory_space=pltpu.VMEM)
SM = pl.BlockSpec(memory_space=pltpu.SMEM)
HB = pl.BlockSpec(memory_space=pl.ANY)
LIMIT = 60 * 1024 * 1024


def sds(shape, dtype):
    return jax.ShapeDtypeStruct(shape, dtype)


def params():
    return pltpu.CompilerParams(vmem_limit_bytes=LIMIT)


def cost(flops, traffic):
    return pl.CostEstimate(flops=flops, bytes_accessed=traffic, transcendentals=0)


def weight_scratch(width):
    return [pltpu.VMEM((BLOCKS, D, width), BF), pltpu.SemaphoreType.DMA((BLOCKS, 16))]


def prepare(seq, info, counts, images, cotangent, gains, biases, bup):
    return pl.pallas_call(
        functools.partial(prepare_kernel, seq),
        out_shape=(
            sds((ROWS, D), F32), sds((ROWS, D), F32), sds(gains.shape, F32), sds(biases.shape, F32),
            sds((LAYERS, BLOCKS, 1, UP_W), F32),
        ),
        in_specs=[SM, SM] + [VM] * 5,
        out_specs=[VM] * 5,
        compiler_params=params(),
        cost_estimate=cost(10**7, 10**5),
        name="prepare",
    )(info, counts, images, cotangent, gains, biases, bup)


def finish(seq, info, counts, y, after):
    return pl.pallas_call(
        functools.partial(finish_kernel, seq, len(after)),
        out_shape=sds((1, seq, D), F32),
        in_specs=[SM, SM, VM] + [HB] * len(after),
        out_specs=VM,
        compiler_params=params(),
        cost_estimate=cost(10**7, 10**5),
        name="finish",
    )(info, counts, y, *after)


def attend(seq, level, info, x, gains, biases, pieces):
    return pl.pallas_call(
        functools.partial(attend_kernel, seq, level, len(pieces)),
        out_shape=(
            sds((ROWS, 3 * D), BF), sds((16, ROWS), F32), sds((BLOCKS, ROWS, 256), BF),
            sds((ROWS, D), F32), sds((ROWS, D), BF),
        ),
        in_specs=[SM] + [VM] * 3 + [HB] * len(pieces),
        out_specs=[VM] * 5,
        scratch_shapes=[pltpu.VMEM((BLOCKS, ROWS, 640), BF)] + weight_scratch(D),
        compiler_params=params(),
        cost_estimate=cost(10**7, 10**5),
        name="attend",
    )(info, x, gains, biases, *pieces)


def whole(shape):
    return pl.BlockSpec(shape, lambda s: (0,) * len(shape))


def feed(level, info, h1, a2, biases, bup, pieces):
    return pl.pallas_call(
        functools.partial(feed_kernel, level, len(pieces)),
        grid=(BLOCKS,),
        out_shape=(sds((BLOCKS, ROWS, UP_W), BF), sds((BLOCKS, ROWS, UP_W), F32), sds((ROWS, D), F32)),
        in_specs=[
            SM, whole((ROWS, D)), whole((ROWS, D)), whole(biases.shape),
            pl.BlockSpec((1, 1, 1, UP_W), lambda s: (level, s, 0, 0)),
        ]
        + [HB] * len(pieces),
        out_specs=[
            pl.BlockSpec((1, ROWS, UP_W), lambda s: (s, 0, 0)),
            pl.BlockSpec((1, ROWS, UP_W), lambda s: (s, 0, 0)),
            whole((ROWS, D)),
        ],
        scratch_shapes=weight_scratch(FFN_W),
        compiler_params=params(),
        cost_estimate=cost(10**7, 10**5),
        name="feed",
    )(info, h1, a2, biases, bup, *pieces)


def feed_back(level, info, g, h1, a2, gains, z, slope, pieces, after):
    grad = sds((4, BLOCKS, PIECE, FFN_W), BF)
    grad_spec = pl.BlockSpec((4, 1, PIECE, FFN_W), lambda s: (0, s, 0, 0))
    step_spec = pl.BlockSpec((1, ROWS, UP_W), lambda s: (s, 0, 0))
    return pl.pallas_call(
        functools.partial(feed_back_kernel, level, len(pieces), len(after)),
        grid=(BLOCKS,),
        out_shape=(grad, grad, sds((BLOCKS, 1, UP_W), F32), sds((ROWS, D), F32), sds((8, D), F32)),
        in_specs=[SM, whole((ROWS, D)), whole((ROWS, D)), whole((ROWS, D)), whole(gains.shape), step_spec, step_spec]
        + [HB] * (len(pieces) + len(after)),
        out_specs=[
            grad_spec, grad_spec,
            pl.BlockSpec((1, 1, UP_W), lambda s: (s, 0, 0)), whole((ROWS, D)), whole((8, D)),
        ],
        scratch_shapes=[pltpu.VMEM((ROWS, D), F32), pltpu.VMEM((D, ROWS), BF), pltpu.VMEM((D, ROWS), BF)]
        + weight_scratch(FFN_W),
        compiler_params=params(),
        cost_estimate=cost(10**7, 10**5),
        name="feed_back",
    )(info, g, h1, a2, gains, z, slope, *pieces, *after)


def attend_back(seq, level, whole_order, info, dh1, x, gains, qkv, lse, oext, sums, bup, pieces, after):
    grads = [sds((BLOCKS, 8, PIECE, D), BF)] if whole_order else [sds((4, BLOCKS, PIECE, D), BF)] * 2
    below = sds((1, seq, D), F32) if level == 0 else sds((ROWS, D), F32)
    return pl.pallas_call(
        functools.partial(attend_back_kernel, seq, level, whole_order, len(pieces), len(after)),
        out_shape=(*grads, below, sds((8, D), F32)),
        in_specs=[SM] + [VM] * 8 + [HB] * (len(pieces) + len(after)),
        out_specs=[VM] * (len(grads) + 2),
        scratch_shapes=[
            pltpu.VMEM((BLOCKS, ROWS, 256), BF), pltpu.VMEM((ROWS, D), BF),
            pltpu.VMEM((ROWS, 3 * D), BF), pltpu.VMEM((BLOCKS, ROWS, 640), BF),
        ]
        + weight_scratch(D),
        compiler_params=params(),
        cost_estimate=cost(10**7, 10**5),
        name="attend_back",
    )(info, dh1, x, gains, qkv, lse, oext, sums, bup, *pieces, *after)


def adamw_step(param, gradient, first_moment, second_moment):
    fresh_first = beta_one * first_moment + (1.0 - beta_one) * gradient
    fresh_second = beta_two * second_moment + (1.0 - beta_two) * gradient * gradient
    first_hat = fresh_first / (1.0 - beta_one**STEP)
    second_hat = fresh_second / (1.0 - beta_two**STEP)
    updated = param - learn_rate * (
        first_hat / (jnp.sqrt(second_hat) + adam_eps) + decay_rate * param
    )
    return (updated, fresh_first, fresh_second)


def after(value, *earlier):
    return lax.optimization_barrier((value,) + earlier)[0]


class PlainPlan:
    def __init__(self, mesh):
        self.n_row = mesh.shape["row"]
        self.n_col = mesh.shape["col"]
        self.turn = jnp.int32(0)
        self.mask = jnp.int32(0)

    def gather(self, shard, widths):
        full = lax.all_gather(shard, ("col", "row"), axis=0, tiled=True)
        full = full.reshape(self.n_col, D, sum(widths))
        parts = []
        start = 0
        for width in widths:
            part = full[:, :, start : start + width].transpose(1, 0, 2)
            parts.append(part.reshape(D, BLOCKS, -1).transpose(1, 0, 2))
            start += width
        return jnp.concatenate(parts, axis=2).reshape(BLOCKS, 8, PIECE, -1)

    def reduce(self, near, far, widths, *earlier):
        done = self.scatter(jnp.stack([near, far], axis=1).transpose(2, 0, 1, 3, 4), widths)
        for _ in range(2):
            yield done
        yield done, done
        yield done
        yield done

    def scatter(self, full, widths):
        full = full.reshape(BLOCKS, D, -1).transpose(1, 0, 2)
        parts = []
        start = 0
        for width in widths:
            wide = width * self.n_col // BLOCKS
            part = full[:, :, start : start + wide].reshape(D, self.n_col, width)
            parts.append(part.transpose(1, 0, 2))
            start += wide
        packed = jnp.concatenate(parts, axis=2).reshape(self.n_col * D, sum(widths))
        return lax.psum_scatter(packed, ("col", "row"), scatter_dimension=0, tiled=True)

    def total(self, values, stages):
        return lax.psum(values, ("row", "col"))


def flip_row(x, mask):
    return lax.ppermute(x, "row", [(i, i ^ mask) for i in range(8)])


def flip_col(x, mask):
    return lax.ppermute(x, "col", [(i, i ^ mask) for i in range(4)])


CORE, NEXT_X, NEXT_Y = 1, 2, 4


def update_kernel(turn, *refs):
    grads, inputs, outputs = refs[:LAYERS], refs[LAYERS : LAYERS + 6], refs[LAYERS + 6 :]
    cut = inputs[0].shape[2]
    for level in range(LAYERS):
        both = grads[level][...].astype(F32)
        for index in range(2):
            param, first, second = inputs[3 * index : 3 * index + 3]
            grad_out, param_out, first_out, second_out = outputs[4 * index : 4 * index + 4]
            gradient = both[:, cut:] if index else both[:, :cut]
            if index and turn:
                gradient = gradient.T
            grad_out[level] = gradient
            fresh = adamw_step(param[level], gradient, first[level], second[level])
            param_out[level], first_out[level], second_out[level] = fresh


def update_matrices(turn, grads, first, second):
    return pl.pallas_call(
        functools.partial(update_kernel, turn),
        out_shape=[sds(group[0].shape, F32) for group in (first, second) for _ in range(4)],
        in_specs=[VM] * (LAYERS + 6),
        out_specs=[VM] * 8,
        compiler_params=params(),
        cost_estimate=cost(10**7, 10**5),
        name="update",
    )(*grads, *first, *second)


class RelativeFetch:
    def __init__(self, shard):
        self.shard = shard

    def turn_one(self, *hold):
        shard = after(self.shard, *hold)
        self.pair = jnp.stack([shard, flip_col(shard, 1)])
        return self.pair[1]

    def turn_two(self, *hold):
        self.others = flip_col(after(self.pair, *hold), 2)
        return self.others

    def plane(self, *hold):
        self.own = after(jnp.concatenate([self.pair, self.others], axis=0), *hold)
        self.from_x = flip_row(self.own, NEXT_X)
        self.from_y = flip_row(self.own, NEXT_Y)
        return self.from_x

    def rest(self, *hold):
        from_x, from_y = after(self.from_x, self.from_y, *hold), after(self.from_y, self.from_x, *hold)
        diag_low = flip_row(from_y[0:2], NEXT_X)
        diag_high = flip_row(from_x[2:4], NEXT_Y)
        near = jnp.concatenate([self.own, from_x, from_y, diag_low, diag_high], axis=0)
        near = near.reshape((4, BLOCKS) + self.shard.shape)
        return [near, flip_row(near, CORE)]


class RelativePlan:
    def __init__(self, mesh):
        self.turn = lax.axis_index("col").astype(jnp.int32)
        self.mask = lax.axis_index("row").astype(jnp.int32)

    def gather(self, shard, widths):
        full = lax.all_gather(shard, ("col", "row"), axis=0, tiled=True)
        return full.reshape(BLOCKS, 8, PIECE, -1)

    def scatter(self, full, widths):
        full = full.reshape(BLOCKS * D, -1)
        return lax.psum_scatter(full, ("col", "row"), scatter_dimension=0, tiled=True)

    def reduce(self, near, far, widths, *earlier):
        far = after(far, *earlier)
        other = flip_row(far, CORE)
        hold = yield other
        other = after(other, *hold)

        def joined(m, blocks):
            return near[m, blocks].astype(F32) + other[m, blocks].astype(F32)

        low, high, every = slice(0, 2), slice(2, 4), slice(0, 4)
        diag_low = flip_row(after(joined(3, low).astype(BF), *hold), NEXT_X)
        diag_high = flip_row(after(joined(3, high).astype(BF), *hold), NEXT_Y)
        hold = yield diag_low, diag_high
        to_x = jnp.concatenate([joined(1, low), joined(1, high) + diag_high.astype(F32)], axis=0)
        to_y = jnp.concatenate([joined(2, low) + diag_low.astype(F32), joined(2, high)], axis=0)
        from_x = flip_row(after(to_x.astype(BF), *hold), NEXT_X)
        from_y = flip_row(after(to_y.astype(BF), *hold), NEXT_Y)
        hold = yield from_x, from_y
        from_x, from_y = after(from_x, from_y, *hold), after(from_y, from_x, *hold)
        plane = joined(0, every) + from_x.astype(F32) + from_y.astype(F32)
        others = flip_col(plane[2:4].astype(BF), 2)
        hold, last = yield others
        pair = plane[0:2] + after(others, *hold).astype(F32)
        yield pair[0] + flip_col(after(pair[1].astype(BF), *last), 1).astype(F32)

    def total(self, values, stages):
        hops = [(flip_col, 1), (flip_col, 2), (flip_row, CORE), (flip_row, NEXT_X), (flip_row, NEXT_Y)]
        for (flip, mask), stage in zip(hops, stages):
            values = values + after(flip(values, mask), *stage)
        return values


def per_device(
    mesh,
    images, cotangent, counts, w_qkv, w_out, w_up, w_down, norm_gains, res_biases, b_up,
    m_qkv, m_out, m_up, m_down, m_gains, m_biases, m_bup,
    v_qkv, v_out, v_up, v_down, v_gains, v_biases, v_bup,
):
    seq = images.shape[1]
    relative = mesh.shape["row"] == 8 and mesh.shape["col"] == 4
    plan = RelativePlan(mesh) if relative else PlainPlan(mesh)
    info = jnp.stack([plan.turn, plan.mask, lax.axis_index("col"), lax.axis_index("row")]).astype(jnp.int32)
    att_widths = (w_qkv.shape[2], w_out.shape[1])
    ffn_widths = (w_up.shape[2], w_down.shape[1])
    shards = []
    for level in range(LAYERS):
        shards.append([
            jnp.concatenate([w_qkv[level].astype(BF), w_out[level].T.astype(BF)], axis=1),
            w_up[level].astype(BF),
            w_down[level].T.astype(BF),
        ])

    hidden, upstream, gains, biases, bup = prepare(
        seq, info, counts, images, cotangent,
        norm_gains.reshape(2 * LAYERS, D), res_biases.reshape(2 * LAYERS, D),
        b_up.reshape(LAYERS * BLOCKS, 1, UP_W),
    )
    saved, att_full, ffn_full = [], [], []

    def forward_attend(level, hidden, pieces):
        att_full.append(pieces)
        return attend(seq, level, info, hidden, gains, biases, pieces)

    def forward_feed(level, hidden, state, pieces):
        qkv, lse, oext, h1, a2 = state
        ffn_full.append(pieces)
        z, slope, y = feed(level, info, h1, a2, biases, bup, pieces)
        saved.append((hidden, qkv, lse, oext, h1, a2, z, slope))
        return y

    def gathered(level):
        return [plan.gather(jnp.concatenate(shards[level], axis=1), att_widths + ffn_widths)]

    later = gathered(1)
    if relative:
        fetches = [RelativeFetch(shard) for shard in shards[0]]
        one = fetches[0].turn_one()
        two = fetches[0].turn_two()
        plane, ran, arrived = (), (gains,), []
        for index, fetch in enumerate(fetches):
            plane = (fetch.plane(*plane),)
            if index + 1 < len(fetches):
                one = fetches[index + 1].turn_one(one)
                two = fetches[index + 1].turn_two(two)
            arrived.append(fetch.rest(two, *ran))
            ran = ()
        sooner = arrived[0], arrived[1] + arrived[2]
    else:
        sooner = (gathered(0),) * 2
    state = forward_attend(0, hidden, sooner[0])
    middle = forward_feed(0, hidden, state, sooner[1])
    state = forward_attend(1, middle, later)
    hidden = forward_feed(1, middle, state, later)
    smalls = [None] * LAYERS

    def backward_feed(level, upstream, landed):
        below, qkv, lse, oext, h1, a2, z, slope = saved[level]
        return feed_back(level, info, upstream, h1, a2, gains, z, slope, ffn_full[level], landed)

    def backward_attend(level, dh1, sums, bup_sum, landed):
        below, qkv, lse, oext, h1, a2, z, slope = saved[level]
        return attend_back(
            seq, level, level == 1, info, dh1, below, gains, qkv, lse, oext, sums, bup_sum, att_full[level], landed
        )

    done = {}
    near, far, bup_sum, dh1, sums = backward_feed(1, upstream, [])
    ffn_one = plan.reduce(near, far, ffn_widths)
    core_one = next(ffn_one)
    whole_one, upstream, smalls[1] = backward_attend(1, dh1, sums, bup_sum, [])
    done["att", 1] = plan.scatter(whole_one, att_widths)
    diag_one = ffn_one.send(())
    near, far, bup_sum, dh1, sums = backward_feed(0, upstream, [*diag_one])
    plane_one = ffn_one.send(())
    ffn_zero = plan.reduce(near, far, ffn_widths)
    core_zero = next(ffn_zero)
    near, far, upstream, smalls[0] = backward_attend(0, dh1, sums, bup_sum, [])
    att_zero = plan.reduce(near, far, att_widths, core_zero)
    core_last = next(att_zero)
    diag_zero = ffn_zero.send((smalls[0],))
    plane_zero = ffn_zero.send(())
    diag_last = att_zero.send(diag_zero)
    plane_last = att_zero.send(())
    turn_one, turn_zero, turn_last = ffn_one.send((smalls[0],)), ffn_zero.send(diag_last), att_zero.send((done["att", 1],))
    done["ffn", 1], done["ffn", 0], done["att", 0] = (
        ffn_one.send((diag_zero, ())),
        ffn_zero.send((plane_last, ())),
        att_zero.send(((), ())),
    )
    layer_out = finish(seq, info, counts, hidden, [upstream])
    stages = [plane_zero, plane_zero, diag_last, plane_last, plane_last]
    small = plan.total(jnp.concatenate(smalls, axis=0), stages).reshape(LAYERS, 8, D)
    ffn, att = [[done[name, level] for level in range(LAYERS)] for name in ("ffn", "att")]

    def turned(arrays):
        return [array.transpose(0, 2, 1) for array in arrays]

    tops = update_matrices(True, att, (w_qkv, m_qkv, v_qkv), (w_out, m_out, v_out))
    feeds = update_matrices(False, ffn, (w_up, m_up, v_up), turned((w_down, m_down, v_down)))
    matrices = [tops[0:4], tops[4:8], feeds[0:4], turned(feeds[4:8])]
    vector_grads = [small[:, 0:2], small[:, 2:4], small[:, 4:8].reshape(LAYERS, FF)]
    params_in = [norm_gains, res_biases, b_up]
    firsts = [m_gains, m_biases, m_bup]
    seconds = [v_gains, v_biases, v_bup]
    vectors = [
        adamw_step(params_in[index], vector_grads[index], firsts[index], seconds[index])
        for index in range(3)
    ]
    return (
        (layer_out, upstream)
        + tuple(matrix[0] for matrix in matrices)
        + tuple(vector_grads)
        + tuple(matrix[1] for matrix in matrices)
        + tuple(matrix[2] for matrix in matrices)
        + tuple(vector[1] for vector in vectors)
        + tuple(matrix[3] for matrix in matrices)
        + tuple(vector[2] for vector in vectors)
    )


def solution(mesh):
    tokens = P(("row", "col"), None, None)
    matrices = (P(None, "row", "col"), P(None, "col", "row"), P(None, "row", "col"), P(None, "col", "row"))
    vectors = (P(), P(), P())
    in_specs = (tokens, tokens, P()) + (matrices + vectors) * 3
    out_specs = (tokens, tokens) + matrices + vectors + matrices + (matrices + vectors) * 2
    return jax.shard_map(
        functools.partial(per_device, mesh), mesh=mesh, in_specs=in_specs, out_specs=out_specs, check_vma=False
    )
```
